32 devices in a mesh: seq: 8 (over z, x), tp: 4 (over y, core).
Axes of the slice: x: 2, y: 2, z: 4, core: 2. Of those that a mesh axis runs over, the one named last changes fastest.
Arguments:
- tokens: bfloat16 [2, 4096, 1024], P(None, ('seq', 'tp')), may hold values from -6 to 6
- out_grad: bfloat16 [2, 4096, 1024], P(None, ('seq', 'tp')), may hold values from -6 to 6
- norm_gain: float32 [1024], replicated, may hold values from 0.5 to 1.5
- w_query: bfloat16 [1024, 1024], P(None, 'tp'), may hold values from -0.1875 to 0.1875
- w_key: bfloat16 [1024, 1024], P(None, 'tp'), may hold values from -0.1875 to 0.1875
- w_value: bfloat16 [1024, 1024], P(None, 'tp'), may hold values from -0.1875 to 0.1875
- w_out: bfloat16 [1024, 1024], P('tp'), may hold values from -1.5 to 1.5
- mid_gain: float32 [1024], replicated, may hold values from 0.5 to 1.5
- w_up: bfloat16 [1024, 4096], P(None, 'tp'), may hold values from -0.1875 to 0.1875
- w_down: bfloat16 [4096, 1024], P('tp'), may hold values from -0.09375 to 0.09375
- ssm_rate: float32 [1024, 16], P('tp'), may hold values from 0.00048828125 to 0.1
- ssm_in: float32 [1024, 16], P('tp'), may hold values from -5 to 5
- ssm_out: float32 [1024, 16], P('tp'), may hold values from -1.5 to 1.5
- resets: int32 [2, 8], P(None, 'seq'), may hold values from 0 to 1, as said below
- init_state: float32 [2, 1024, 16], P(None, 'tp'), may hold values from -5 to 5
- states_grad: float32 [2, 8, 1024, 16], P(None, 'seq', 'tp'), may hold values from -6 to 6
Outputs:
- mixed: bfloat16 [2, 4096, 1024], P(None, ('seq', 'tp'))
- block_states: float32 [2, 8, 1024, 16], P(None, 'seq', 'tp')
- tokens_grad: float32 [2, 4096, 1024], P(None, ('seq', 'tp'))
- norm_gain_grad: float32 [1024], P('tp')
- query_grad: float32 [1024, 1024], P(None, 'tp')
- key_grad: float32 [1024, 1024], P(None, 'tp')
- value_grad: float32 [1024, 1024], P(None, 'tp')
- out_proj_grad: float32 [1024, 1024], P('tp')
- mid_gain_grad: float32 [1024], P('tp')
- up_grad: float32 [1024, 4096], P(None, 'tp')
- down_grad: float32 [4096, 1024], P('tp')
- rate_grad: float32 [1024, 16], P('tp')
- ssm_in_grad: float32 [1024, 16], P('tp')
- ssm_out_grad: float32 [1024, 16], P('tp')
The draws below stay inside these ranges and needn't reach their ends.
Inputs may be any that keep to these rules, and one draw needn't show every extreme that they name: resets is 1 in the first block of every stream; in one stream no later block is 1.
All inputs are finite; a program needn't handle non-finite values.
Results may differ from the reference program's by a relative error of at most 0.012.
Values may be sent and summed in bfloat16 or wider, within the bound.
A program may use at most 192 MiB of HBM per device.

```python
import math
import jax
import jax.numpy as jnp
from jax import lax

D = 1024
HEADS = 8
HD = 128
FF = 4096
NS = 16
BLK = 512
CTX = 128
MB = 2
NBLK = 8
STREAM = 4096


def draw_resets(key, part):
    key = jax.random.fold_in(key, 7)
    flag_key = jax.random.fold_in(key, 1)
    kept_key = jax.random.fold_in(key, 2)
    shift_key = jax.random.fold_in(key, 3)
    spot_key = jax.random.fold_in(key, 4)
    flags = (jax.random.randint(flag_key, (MB, NBLK), 0, 3) == 0).astype(jnp.int32)
    kept = jax.random.randint(kept_key, (), 0, MB)
    other = (kept + jax.random.randint(shift_key, (), 1, MB)) % MB
    spot = jax.random.randint(spot_key, (), 1, NBLK)
    row_ids = jnp.arange(MB)[:, None]
    col_ids = jnp.arange(NBLK)[None, :]
    flags = jnp.where((row_ids == other) & (col_ids == spot), 1, flags)
    flags = jnp.where(row_ids == kept, 0, flags)
    return jnp.where(col_ids == 0, 1, flags).astype(jnp.int32)


def steps_of(rng, shape, cuts, least, high):
    level, own = 1.0, jax.random.fold_in(rng, 6)
    for dim, shards_of in cuts:
        steps = jnp.exp(jax.random.uniform(jax.random.fold_in(own, dim), (shards_of,), jnp.float32, least / len(cuts), high / len(cuts)))
        level = level * jnp.repeat(steps, shape[dim] // shards_of).reshape([-1 if axis == dim else 1 for axis in range(len(shape))])
    return level


def gaussian(key, shape, scale, reach, cuts=(), kind=jnp.bfloat16):
    entries = jax.random.normal(key, shape, jnp.float32) * scale
    if len(cuts) > 0:
        entries = steps_of(key, shape, cuts, -0.22, 0.18) * entries
    return jnp.clip(entries, min=-reach, max=reach).astype(kind)


def setup_inputs(seed: int = 0) -> dict:
    seeds = jax.random.split(jax.random.key(seed), 17)
    tokens = gaussian(seeds[0], (MB, STREAM, D), 1.0, 6.0, ((1, 32),))
    out_grad = gaussian(seeds[1], (MB, STREAM, D), 1.0, 6.0, ((1, 32),))
    norm_gain = jnp.clip(1.0 + 0.1 * jax.random.normal(seeds[2], (D,), jnp.float32), 0.5, 1.5)
    w_query = gaussian(seeds[3], (D, D), D ** -0.5, 0.1875, ((1, 4),))
    w_key = gaussian(seeds[4], (D, D), D ** -0.5, 0.1875, ((1, 4),))
    w_value = gaussian(seeds[5], (D, D), D ** -0.5, 0.1875, ((1, 4),))
    w_out = gaussian(seeds[6], (D, D), (max(D // 64, 1)) ** -0.5, 1.5, ((0, 4),))
    mid_gain = jnp.clip(1.0 + 0.1 * jax.random.normal(seeds[7], (D,), jnp.float32), 0.5, 1.5)
    w_up = gaussian(seeds[8], (D, FF), D ** -0.5, 0.1875, ((1, 4),))
    w_down = gaussian(seeds[9], (FF, D), FF ** -0.5, 0.09375, ((0, 4),))
    ssm_rate = jnp.clip(jnp.exp(math.log(0.1) - 5.322034 * jax.random.uniform(seeds[10], (D, NS), jnp.float32) ** steps_of(seeds[10], (D, NS), ((0, 4),), -0.2, 0.2)), 0.00048828125, 0.1)
    ssm_in = gaussian(seeds[11], (D, NS), 1.0, 5.0, ((0, 4),), jnp.float32)
    ssm_out = gaussian(seeds[12], (D, NS), NS ** -0.5, 1.5, ((0, 4),), jnp.float32)
    resets = draw_resets(jax.random.fold_in(seeds[16], 71), 0)
    init_state = gaussian(seeds[14], (MB, D, NS), 1.0, 5.0, ((1, 4),), jnp.float32)
    states_grad = gaussian(seeds[15], (MB, NBLK, D, NS), 1.0, 6.0, ((1, 8), (2, 4)), jnp.float32)
    return {"tokens": tokens, "out_grad": out_grad, "norm_gain": norm_gain, "w_query": w_query, "w_key": w_key, "w_value": w_value, "w_out": w_out, "mid_gain": mid_gain, "w_up": w_up, "w_down": w_down, "ssm_rate": ssm_rate, "ssm_in": ssm_in, "ssm_out": ssm_out, "resets": resets, "init_state": init_state, "states_grad": states_grad}


@jax.custom_vjp
def low(v):
    return lax.optimization_barrier(v.astype(jnp.bfloat16)).astype(jnp.float32)

@jax.custom_vjp
def low_back(v):
    return v

def low_keep(v):
    return (low(v), None)

def low_pass(kept, grad):
    return (grad,)

def back_keep(v):
    return (v, None)

def back_low(kept, grad):
    return (low(grad),)
low.defvjp(low_keep, low_pass)
low_back.defvjp(back_keep, back_low)
eps_norm = 1e-06
sub_len = 128
neg_big = -1e+30
highest = lax.Precision.HIGHEST

def rms_norm(values, gain):
    return values * lax.rsqrt(lax.optimization_barrier(jnp.mean(values * values, axis=-1, keepdims=True)) + eps_norm) * gain

def ssm_block(inputs, start, rate, coef_in, coef_out):
    length, channels = inputs.shape
    width = min(sub_len, length)
    decay = jnp.exp(-rate)
    drive = jnp.sqrt(1.0 - decay * decay) * coef_in
    lag_steps = jnp.arange(width).astype(jnp.float32)
    powers = jnp.exp(-rate[:, :, None] * lag_steps)
    kernel = jnp.einsum('cn,cnl->cl', coef_out * drive, powers, precision=highest)
    row_ids = jnp.arange(width)[:, None]
    col_ids = jnp.arange(width)[None, :]
    lag_index = jnp.maximum(row_ids - col_ids, 0).astype(jnp.int32)
    toeplitz = jnp.where((row_ids >= col_ids)[None], jnp.take(kernel, lag_index, axis=1), 0.0)
    ahead = jnp.exp(-rate[:, :, None] * (lag_steps + 1.0))
    behind = jnp.flip(powers, axis=2) * drive[:, :, None]
    whole_decay = jnp.exp(-rate * width)
    pieces = inputs.reshape(length // width, width, channels)

    def advance(state, piece):
        inner = jnp.einsum('ctj,jc->tc', toeplitz, piece, precision=highest)
        carried = jnp.einsum('cn,cnt->tc', coef_out * state, ahead, precision=highest)
        state = whole_decay * state + jnp.einsum('cnj,jc->cn', behind, piece, precision=highest)
        return (state, inner + carried)
    final, outputs = lax.scan(advance, start, pieces)
    return (outputs.reshape(length, channels), final)

def product(left, right):
    return jnp.einsum('...d,dc->...c', left, right, precision=highest)

def reference(tokens, out_grad, norm_gain, w_query, w_key, w_value, w_out, mid_gain, w_up, w_down, ssm_rate, ssm_in, ssm_out, resets, init_state, states_grad):
    flags = resets.astype(jnp.float32)
    firsts = (jnp.arange(NBLK) == 0).astype(jnp.float32)
    scale = HD ** (-0.5)
    row_ids = jnp.arange(BLK)[:, None]
    col_ids = jnp.arange(CTX + 2 * BLK)[None, :]
    outside = col_ids < CTX + BLK
    causal = col_ids - CTX - BLK <= row_ids

    def attend(item):
        query_part, keys_part, vals_part, flag = item
        mask = jnp.where(outside, flag < 0.5, causal)
        scores = low_back(jnp.einsum('thd,khd->htk', query_part, keys_part, precision=highest) * scale)
        scores = jnp.where(mask[None], scores, neg_big)
        top = lax.optimization_barrier(jnp.max(scores, axis=2, keepdims=True))
        expo = jnp.exp(scores - top)
        weights = low(expo / lax.optimization_barrier(jnp.sum(expo, axis=2, keepdims=True)))
        result = jnp.einsum('htk,khd->thd', weights, vals_part, precision=highest)
        return low(low_back(result)).reshape(BLK, D)

    def forward(inputs, gain_one, query_w, key_w, value_w, out_w, gain_two, up_w, down_w, rate, coef_in, coef_out):
        micro = inputs.shape[0]
        normed = low(rms_norm(inputs, gain_one))

        def stream(item):
            series, flag_row, begin = item
            pieces = series.reshape(NBLK, BLK, D)

            def step(carry, piece_item):
                piece, flag, first = piece_item
                start = (1.0 - flag) * carry + first * begin
                result, final = ssm_block(piece, start, rate, coef_in, coef_out)
                return (final, (result, final))
            _, (results, finals) = lax.scan(jax.checkpoint(step), jnp.zeros((D, NS), jnp.float32), (pieces, flag_row, firsts))
            return (results, finals)
        ssm_y, finals = lax.map(stream, (normed, flags, init_state))
        query = low(low_back(product(normed, query_w)))
        keys = low(low_back(product(normed, key_w)))
        values = low(low_back(product(normed, value_w)))
        context = low(ssm_y[:, :, BLK - CTX:, :])
        context_keys = low(low_back(product(context, key_w)))
        context_values = low(low_back(product(context, value_w)))

        def blocks(array, rows):
            return array.reshape(micro, NBLK, rows, HEADS, HD)

        def previous(array):
            return jnp.concatenate([jnp.zeros_like(array[:, :1]), array[:, :-1]], axis=1)
        keys_b = blocks(keys, BLK)
        vals_b = blocks(values, BLK)
        keys_all = jnp.concatenate([previous(blocks(context_keys, CTX)), previous(keys_b), keys_b], axis=2)
        vals_all = jnp.concatenate([previous(blocks(context_values, CTX)), previous(vals_b), vals_b], axis=2)

        def flat(array):
            return array.reshape((micro * NBLK,) + array.shape[2:])
        attended = lax.map(jax.checkpoint(attend), (flat(blocks(query, BLK)), flat(keys_all), flat(vals_all), flags.reshape(-1)))
        attended = attended.reshape(micro, STREAM, D)
        hidden_one = inputs + low_back(product(attended, out_w))
        normed_mid = low(rms_norm(hidden_one, gain_two))
        pre_act = low_back(product(normed_mid, up_w))
        hidden = low(jax.nn.gelu(pre_act, approximate=True))
        result = hidden_one + low_back(product(hidden, down_w))
        return (result, finals)
    primals = tuple((array.astype(jnp.float32) for array in (tokens, norm_gain, w_query, w_key, w_value, w_out, mid_gain, w_up, w_down, ssm_rate, ssm_in, ssm_out)))
    (mixed, finals), pull = jax.vjp(forward, *primals)
    grads = pull((out_grad.astype(jnp.float32), states_grad.astype(jnp.float32)))
    return (mixed.astype(jnp.bfloat16), finals, grads[0], grads[1], grads[2], grads[3], grads[4], grads[5], grads[6], grads[7], grads[8], grads[9], grads[10], grads[11])
```

```python
import functools

import jax
import jax.numpy as jnp
from jax import lax
from jax.experimental import pallas as pl
from jax.experimental.pallas import tpu as pltpu
from jax.sharding import PartitionSpec as P

HD = 128
NS = 16
CTX = 128


eps_norm = 1e-06
neg_big = -1e30
MESH = pl.DeviceIdType.MESH
VM = pltpu.VMEM
BF = jnp.bfloat16
F32 = jnp.float32
NT = (((1,), (1,)), ((), ()))
TN = (((0,), (0,)), ((), ()))
NN = (((1,), (0,)), ((), ()))


def dot(left, right, dims=NN):
    return lax.dot_general(left, right, dims, preferred_element_type=F32)


def vmem_specs(count):
    return [pl.BlockSpec(memory_space=VM)] * count


def tp_peers():
    me = lax.axis_index("tp")
    mate = me + 1 - 2 * lax.rem(me, 2)
    return me, mate, lax.rem(me + 2, 4), lax.rem(mate + 2, 4)


def remote(src, dst, send, recv, **where):
    return pltpu.make_async_remote_copy(
        src_ref=src,
        dst_ref=dst,
        send_sem=send,
        recv_sem=recv,
        device_id=where,
        device_id_type=MESH,
    )


def greet(n, with_seq):
    s = lax.axis_index("seq")
    barrier = pltpu.get_barrier_semaphore()
    for peer in tp_peers()[1:]:
        pl.semaphore_signal(barrier, inc=1, device_id={"tp": peer}, device_id_type=MESH)
    if with_seq:
        for k in range(1, n):
            pl.semaphore_signal(
                barrier, inc=1, device_id={"seq": lax.rem(s + k, n)}, device_id_type=MESH
            )


def greeted(n, with_seq):
    pl.semaphore_wait(pltpu.get_barrier_semaphore(), 3 + (n - 1 if with_seq else 0))


class Fetch:
    def __init__(self, names, refs, held, sems):
        self.copies = {
            name: pltpu.make_async_copy(ref, held[name], sems.at[i])
            for i, (name, ref) in enumerate(zip(names, refs))
        }
        self.ready = set()
        for c in self.copies.values():
            c.start()

    def need(self, *wanted):
        for name in wanted:
            if name not in self.ready:
                self.copies[name].wait()
                self.ready.add(name)


class Gather:
    def __init__(self, ref, send, recv):
        rows = ref.shape[0] // 4
        me, mate, across, _ = tp_peers()

        def give(slot, quarter, peer):
            part = ref.at[pl.ds(pl.multiple_of(quarter * rows, rows), rows), :]
            return remote(part, part, send.at[slot], recv.at[slot], tp=peer)

        self.cross = give(1, me, across)
        self.side = give(0, me, mate)
        self.relay = give(2, across, mate)

    def start(self):
        self.cross.start()
        self.side.start()

    def near(self):
        self.side.wait_recv()

    def pass_on(self):
        self.cross.wait_recv()
        self.relay.start()

    def far(self):
        self.relay.wait_recv()

    def finish(self):
        for c in (self.side, self.cross, self.relay):
            c.wait_send()


class Scatter:
    def __init__(self, ref, over, into, send, recv):
        self.ref, self.over, self.into = ref, over, into
        self.rows = ref.shape[0] // 4
        self.me, self.mate, self.across, self.diag = tp_peers()
        self.hop = [
            remote(self.quarter(self.diag), into.at[0], send.at[0], recv.at[0], tp=self.mate),
            remote(self.quarter(self.mate), into.at[1], send.at[1], recv.at[1], tp=self.mate),
            remote(over, into.at[2], send.at[2], recv.at[2], tp=self.across),
        ]

    def span(self, quarter):
        return pl.ds(pl.multiple_of(quarter * self.rows, self.rows), self.rows)

    def quarter(self, quarter):
        return self.ref.at[self.span(quarter), :]

    def start(self):
        self.hop[0].start()
        self.hop[1].start()

    def turn(self):
        self.hop[0].wait_recv()
        mine = self.ref[self.span(self.across), :].astype(F32)
        self.over[...] = (mine + self.into[0].astype(F32)).astype(BF)
        self.hop[2].start()

    def end(self):
        self.hop[1].wait_recv()
        value = self.ref[self.span(self.me), :].astype(F32) + self.into[1].astype(F32)
        self.hop[2].wait_recv()
        value = value + self.into[2].astype(F32)
        for c in self.hop:
            c.wait_send()
        return value


FRONT_IN = ("tok", "gain", "wq", "wk", "wv", "rate", "cin", "cout", "keep", "init")


def front_kernel(n, refs_in, outs, held, scr):
    fetch = Fetch(FRONT_IN, refs_in, held, scr["fetch"])
    nf, q_o, k_o, v_o, ctx_o, start_o, end_o = outs
    s = lax.axis_index("seq")
    me, mate, across, diag = tp_peers()
    tok, rate, keep, init = (held[x] for x in ("tok", "rate", "keep", "init"))
    wq, wk, wv = held["wq"], held["wk"], held["wv"]
    u_s, gath, pay, y_s, ctx_s = (scr[x] for x in ("u", "gath", "pay", "y", "ctx"))
    block = nf.shape[1]
    rows = block // 4
    chan = rate.shape[1]
    gath[...] = jnp.zeros_like(gath)

    @pl.when(s == 0)
    def _():
        k_o[:, 0 : CTX + block, :] = jnp.zeros((2, CTX + block, chan), BF)
        v_o[:, 0 : CTX + block, :] = jnp.zeros((2, CTX + block, chan), BF)
        ctx_o[...] = jnp.zeros_like(ctx_o)

    greet(n, True)

    def span(quarter):
        return pl.ds(pl.multiple_of(quarter * rows, rows), rows)

    def lanes(part):
        return pl.ds(pl.multiple_of(part * chan, chan), chan)

    fetch.need("tok", "gain")
    x = tok[...].astype(F32).reshape(2 * rows, -1)
    normed = x * lax.rsqrt(jnp.mean(x * x, axis=-1, keepdims=True) + eps_norm) * held["gain"][...]
    nf[:, span(me), :] = normed.astype(BF).reshape(2, rows, -1)
    greeted(n, True)

    def give(slot, quarter, peer, part=None):
        cols = slice(None) if part is None else lanes(part)
        ref = nf.at[:, span(quarter), cols]
        return remote(ref, ref, scr["ts"].at[slot], scr["tr"].at[slot], tp=peer)

    cross = [give(1 + i, me, across, part) for i, part in enumerate((across, diag, me, mate))]
    relay = [give(5 + i, across, mate, part) for i, part in enumerate((me, mate, across, diag))]
    side = give(0, me, mate)
    for c in cross:
        c.start()
    side.start()

    def pass_kv(slot, src, half):
        high = 2 * rows
        part = pl.ds(pl.multiple_of(CTX + half * high, rows), high)
        own = pl.ds(pl.multiple_of(CTX + block + half * high, rows), high)
        return remote(
            src.at[:, own, :],
            src.at[:, part, :],
            scr["kvs"].at[slot],
            scr["kvr"].at[slot],
            seq=lax.rem(s + 1, n),
        )

    def qkv(order, half):
        high = 2 * rows
        here = pl.ds(pl.multiple_of(half * high, high), high)
        part = nf[:, here, :].reshape(2 * high, -1)
        own = pl.ds(pl.multiple_of(CTX + block + half * high, rows), high)
        k_o[:, own, :] = dot(part, wk[...]).astype(BF).reshape(2, high, chan)
        v_o[:, own, :] = dot(part, wv[...]).astype(BF).reshape(2, high, chan)

        @pl.when(s < n - 1)
        def _():
            pass_kv(2 * order, k_o, half).start()
            pass_kv(2 * order + 1, v_o, half).start()

        q_o[:, here, :] = dot(part, wq[...]).astype(BF).reshape(2, high, chan)

    near = me // 2
    side.wait_recv()
    fetch.need("wk", "wv", "wq")
    qkv(0, near)
    cross[0].wait_recv()
    cross[1].wait_recv()
    relay[1].start()
    relay[0].start()
    relay[1].wait_recv()
    fetch.need("rate", "cin", "cout", "keep", "init")
    cols = lanes(me)
    for m in range(2):
        u_s[m] = nf[m, :, cols].astype(F32)
    decay = jnp.exp(-rate[...])
    drive = jnp.sqrt(1.0 - decay * decay) * held["cin"][...]

    def run(i, state):
        base = pl.multiple_of(i * 8, 8)
        state = list(state)
        for k in range(8):
            for m in range(2):
                state[m] = decay * state[m] + drive * u_s[m, pl.ds(base + k, 1), :]
        return tuple(state)

    zero = jnp.zeros((NS, chan), F32)
    late = lax.fori_loop(0, (block - CTX) // 8, run, (zero, zero))
    last_state = lax.fori_loop((block - CTX) // 8, block // 8, run, late)
    pay[0:NS] = last_state[0]
    pay[NS : 2 * NS] = last_state[1]
    pay[2 * NS : 2 * NS + 8] = keep[...]

    def spread(k):
        return remote(
            pay, gath.at[k], scr["gs"].at[k], scr["gr"].at[k], seq=lax.rem(s + k, n)
        )

    for k in range(1, n):

        @pl.when(s + k < n)
        def _():
            spread(k).start()

    for i in (2, 3):
        cross[i].wait_recv()
        relay[i].start()
    for i in (0, 2, 3):
        relay[i].wait_recv()
    qkv(1, 1 - near)

    whole = jnp.exp(-rate[...] * block)
    for k in range(1, n):

        @pl.when(s >= k)
        def _():
            spread(k).wait_recv()

    def entry(begin_keep, end, b):
        return tuple(jnp.where(b == 0, init[m], begin_keep[m] * end[m]) for m in range(2))

    def chain(b, end):
        k = jnp.maximum(s - b, 0)
        got = gath[k]
        begin = entry((got[2 * NS : 2 * NS + 1], got[2 * NS + 1 : 2 * NS + 2]), end, b)
        new = tuple(got[m * NS : (m + 1) * NS] + whole * begin[m] for m in range(2))
        return tuple(jnp.where(b < s, new[m], end[m]) for m in range(2))

    end = lax.fori_loop(0, n - 1, chain, (zero, zero))
    begin = entry((keep[0:1, :], keep[1:2, :]), end, s)
    toward = jnp.exp(-rate[...] * (block - CTX))
    state = tuple(late[m] + toward * begin[m] for m in range(2))
    out_c = held["cout"][...]

    def run_out(i, state):
        base = pl.multiple_of(block - CTX + i * 8, 8)
        row = pl.multiple_of(i * 8, 8)
        state = list(state)
        for k in range(8):
            for m in range(2):
                state[m] = decay * state[m] + drive * u_s[m, pl.ds(base + k, 1), :]
                y_s[m, pl.ds(row + k, 1), :] = jnp.sum(out_c * state[m], axis=0, keepdims=True)
        return tuple(state)

    state = lax.fori_loop(0, CTX // 8, run_out, state)
    ctx_s[...] = y_s[...].astype(BF)
    down = remote(
        ctx_s, ctx_o.at[:, :, cols], scr["cs"].at[0], scr["cr"].at[0], seq=lax.rem(s + 1, n)
    )

    @pl.when(s < n - 1)
    def _():
        down.start()

    for m in range(2):
        start_o[m] = begin[m]
        end_o[m] = last_state[m] + whole * begin[m]

    @pl.when(s > 0)
    def _():
        down.wait_recv()
        mine = ctx_o.at[:, :, cols]
        shares = [
            remote(mine, mine, scr["cs"].at[1 + i], scr["cr"].at[1 + i], tp=peer)
            for i, peer in enumerate((across, diag, mate))
        ]
        for c in shares:
            c.start()
        for c in shares:
            c.wait_recv()
        flat = ctx_o[...].reshape(2 * CTX, -1)
        k_o[:, 0:CTX, :] = dot(flat, wk[...]).astype(BF).reshape(2, CTX, chan)
        v_o[:, 0:CTX, :] = dot(flat, wv[...]).astype(BF).reshape(2, CTX, chan)
        for order, half in enumerate((near, 1 - near)):
            pass_kv(2 * order, k_o, half).wait_recv()
            pass_kv(2 * order + 1, v_o, half).wait_recv()
        for c in shares:
            c.wait_send()

    @pl.when(s < n - 1)
    def _():
        down.wait_send()
        for order, half in enumerate((near, 1 - near)):
            pass_kv(2 * order, k_o, half).wait_send()
            pass_kv(2 * order + 1, v_o, half).wait_send()

    for k in range(1, n):

        @pl.when(s + k < n)
        def _():
            spread(k).wait_send()

    for c in [side] + cross + relay:
        c.wait_send()


def launch(body, names, args, outs, out_vmem, scratch, collective_id, limit, name):
    keys = list(scratch)
    count = len(names)

    def kernel(*refs):
        refs_in, refs = refs[:count], refs[count:]
        outs_r, refs = refs[: len(outs)], refs[len(outs) :]
        held, refs = dict(zip(names, refs[:count])), refs[count:]
        body(refs_in, outs_r, held, dict(zip(keys, refs)))

    scratch = dict(scratch)
    return pl.pallas_call(
        kernel,
        out_shape=tuple(outs),
        in_specs=[pl.BlockSpec(memory_space=pl.ANY)] * count,
        out_specs=tuple(
            pl.BlockSpec(memory_space=VM if in_vmem else pl.ANY) for in_vmem in out_vmem
        ),
        scratch_shapes=[VM(a.shape, a.dtype) for a in args] + list(scratch.values()),
        compiler_params=pltpu.CompilerParams(
            collective_id=collective_id, has_side_effects=True, vmem_limit_bytes=limit << 20
        ),
        name=name,
    )(*args)


def front(*args):
    n = lax.axis_size("seq")
    micro, rows, width = args[0].shape
    block = 4 * rows
    chan = args[5].shape[1]
    sds = jax.ShapeDtypeStruct
    dma = pltpu.SemaphoreType.DMA
    outs = (
        sds((micro, block, width), BF),
        sds((micro, block, chan), BF),
        sds((micro, CTX + 2 * block, chan), BF),
        sds((micro, CTX + 2 * block, chan), BF),
        sds((micro, CTX, width), BF),
        sds((micro, NS, chan), F32),
        sds((micro, NS, chan), F32),
    )
    scratch = dict(
        fetch=dma((len(FRONT_IN),)),
        u=VM((micro, block, chan), F32),
        gath=VM((n, 2 * NS + 8, chan), F32),
        pay=VM((2 * NS + 8, chan), F32),
        y=VM((micro, CTX, chan), F32),
        ctx=VM((micro, CTX, chan), BF),
        ts=dma((9,)),
        tr=dma((9,)),
        kvs=dma((4,)),
        kvr=dma((4,)),
        gs=dma((n,)),
        gr=dma((n,)),
        cs=dma((4,)),
        cr=dma((4,)),
    )
    return launch(
        functools.partial(front_kernel, n),
        FRONT_IN,
        args,
        outs,
        [True] * 7,
        scratch,
        0,
        62,
        "front",
    )


def rms_back(x, gain, grad):
    inv = lax.rsqrt(jnp.mean(x * x, axis=-1, keepdims=True) + eps_norm)
    unit = x * inv
    scaled = grad * gain
    gain_grad = jnp.sum(grad * unit, axis=0, keepdims=True)
    return inv * (scaled - unit * jnp.mean(scaled * unit, axis=-1, keepdims=True)), gain_grad


MIDDLE_IN = ("q", "k", "v", "keep", "w_out", "tok", "gain", "w_up", "w_down", "og")


def middle_kernel(refs_in, outs, held, scr):
    fetch = Fetch(MIDDLE_IN, refs_in, held, scr["fetch"])
    mlp_o, h1_o, dh1_o, ffn_o, att, lse, gain_o = outs
    nm, pm, dm, hid, dpre = (scr[x] for x in ("nm", "pm", "dm", "hid", "dpre"))
    q, k, v, keep, w_out, tok, gain, w_up, w_down, og = (held[x] for x in MIDDLE_IN)
    me = tp_peers()[0]
    near = me // 2
    block = q.shape[1]
    rows = block // 4
    width = w_out.shape[1]
    tile = 256
    panels = w_up.shape[1] // tile
    greet(0, False)
    own = pl.ds(pl.multiple_of(me * rows, rows), rows)
    edge0 = k.shape[1] - block
    half = block // 2
    row_ids = lax.broadcasted_iota(jnp.int32, (half, half), 0)
    col_ids = lax.broadcasted_iota(jnp.int32, (half, half), 1)
    scale = HD ** (-0.5)

    def attend(m):
        def one(head, c):
            lanes = pl.ds(pl.multiple_of(head * HD, HD), HD)
            shut = (keep[m : m + 1, 0:half] - 1.0) * -neg_big
            for part in range(2):
                mine = slice(part * half, (part + 1) * half)
                edge = edge0 + part * half
                sc = dot(k[m, 0 : edge + half, lanes], q[m, mine, lanes], NT) * scale
                pieces = [sc[:edge0] + shut]
                if part:
                    pieces.append(sc[edge0:edge])
                pieces.append(jnp.where(row_ids <= col_ids, sc[edge:], neg_big))
                sc = jnp.concatenate(pieces, axis=0)
                top = jnp.max(sc, axis=0, keepdims=True)
                expo = jnp.exp(sc - top)
                total = jnp.sum(expo, axis=0, keepdims=True)
                weights = (expo * (1.0 / total)).astype(BF)
                res = dot(v[m, 0 : edge + half, lanes], weights, TN)
                att[m, mine, lanes] = res.T.astype(BF)
                lse[m, head, :, mine] = top + jnp.log(total)
            return c

        lax.fori_loop(0, q.shape[2] // HD, one, 0)

    def scatter(kind, m, ref):
        at = 2 * kind + m
        return Scatter(
            ref.at[m], scr["over"].at[at], scr["into"].at[at], scr["ss"].at[at], scr["sr"].at[at]
        )

    sums1 = [scatter(0, m, pm) for m in range(2)]
    sums2 = [scatter(1, m, dm) for m in range(2)]
    gathers = [Gather(nm.at[m], scr["gs"].at[m], scr["gr"].at[m]) for m in range(2)]

    def project(m):
        def one(j, c):
            cols = pl.ds(pl.multiple_of(j * tile, tile), tile)
            pm[m, :, cols] = dot(att[m], w_out[:, cols]).astype(BF)
            return c

        lax.fori_loop(0, width // tile, one, 0)

    def residual(m):
        h1 = tok[m].astype(F32) + sums1[m].end()
        h1_o[m] = h1
        inv = lax.rsqrt(jnp.mean(h1 * h1, axis=-1, keepdims=True) + eps_norm)
        nm[m, own, :] = (h1 * inv * gain[...]).astype(BF)
        gathers[m].start()

    def feed(m, part):
        here = pl.ds(pl.multiple_of(part * half, half), half)
        flat = pl.ds(pl.multiple_of(m * block + part * half, half), half)

        def panel(j, c):
            cols = pl.ds(pl.multiple_of(j * tile, tile), tile)
            pre = dot(nm[m, here, :], w_up[:, cols])
            sq = pre * pre
            t = jnp.tanh((0.7978845608028654 * pre) * (1.0 + 0.044715 * sq))
            hid[flat, cols] = (0.5 * pre * (1.0 + t)).astype(BF)
            slope = 0.5 * (1.0 + t) + (0.3989422804014327 * pre) * (1.0 - t * t) * (
                1.0 + 0.134145 * sq
            )
            dpre[flat, cols] = (slope * dot(og[m, here, :], w_down[cols, :], NT)).astype(BF)
            return c

        lax.fori_loop(0, panels, panel, 0)

        def back(j, c):
            cols = pl.ds(pl.multiple_of(j * tile, tile), tile)
            dm[m, here, cols] = dot(dpre[flat, :], w_up[cols, :], NT).astype(BF)
            return c

        lax.fori_loop(0, width // tile, back, 0)

    def lower(m):
        def one(j, c):
            cols = pl.ds(pl.multiple_of(j * tile, tile), tile)
            flat = slice(m * block, (m + 1) * block)
            mlp_o[m, :, cols] = dot(hid[flat, :], w_down[:, cols]).astype(BF)
            return c

        lax.fori_loop(0, width // tile, one, 0)

    fetch.need("q", "k", "v", "keep")
    attend(0)
    fetch.need("w_out")
    project(0)
    greeted(0, False)
    sums1[0].start()
    sums1[0].turn()
    attend(1)
    project(1)
    sums1[1].start()
    sums1[1].turn()
    fetch.need("tok", "gain")
    residual(0)
    fetch.need("w_up", "w_down", "og")
    gathers[0].near()
    feed(0, near)
    residual(1)
    gathers[0].pass_on()
    gathers[1].near()
    feed(1, near)
    gathers[0].far()
    feed(0, 1 - near)
    sums2[0].start()
    gathers[1].pass_on()
    sums2[0].turn()
    gathers[1].far()
    feed(1, 1 - near)
    sums2[1].start()
    sums2[1].turn()

    def down_sum(i, c):
        left = hid[:, pl.ds(pl.multiple_of(i * tile, tile), tile)]
        for j in range(width // tile):
            right = og[:, :, j * tile : (j + 1) * tile].reshape(2 * block, tile)
            at = pl.multiple_of((width // tile + j) * panels * tile + i * tile, tile)
            ffn_o[pl.ds(at, tile), :] = dot(left, right, TN).astype(BF)
        return c

    def up_sum(i, c):
        left = nm[:, :, pl.ds(pl.multiple_of(i * tile, tile), tile)].reshape(2 * block, tile)
        for j in range(panels):
            at = pl.multiple_of(j * width + i * tile, tile)
            ffn_o[pl.ds(at, tile), :] = dot(
                left, dpre[:, j * tile : (j + 1) * tile], TN
            ).astype(BF)
        return c

    lax.fori_loop(0, panels, down_sum, 0)
    lax.fori_loop(0, width // tile, up_sum, 0)
    lower(0)
    lower(1)
    total = jnp.zeros((1, width), F32)
    for m in range(2):
        back, gain_grad = rms_back(h1_o[m], gain[...], sums2[m].end())
        total = total + gain_grad
        dh1_o[m] = og[m, own, :].astype(F32) + back
    gain_o[...] = total
    for m in range(2):
        gathers[m].finish()


def middle(*args):
    q, w_out, og, w_up = args[0], args[4], args[9], args[7]
    micro, block, width = og.shape
    rows = block // 4
    units = w_up.shape[1]
    chan = q.shape[2]
    sds = jax.ShapeDtypeStruct
    dma = pltpu.SemaphoreType.DMA
    outs = (
        sds((micro, block, width), BF),
        sds((micro, rows, width), F32),
        sds((micro, rows, width), F32),
        sds((2 * units * width // 256, 256), BF),
        sds((micro, block, chan), BF),
        sds((micro, chan // HD, 1, block), F32),
        sds((1, width), F32),
    )
    scratch = dict(
        fetch=dma((len(MIDDLE_IN),)),
        nm=VM((micro, block, width), BF),
        pm=VM((micro, block, width), BF),
        dm=VM((micro, block, width), BF),
        hid=VM((micro * block, units), BF),
        dpre=VM((micro * block, units), BF),
        over=VM((4, rows, width), BF),
        into=VM((4, 3, rows, width), BF),
        ss=dma((4, 3)),
        sr=dma((4, 3)),
        gs=dma((2, 3)),
        gr=dma((2, 3)),
    )
    return launch(
        middle_kernel, MIDDLE_IN, args, outs, [True] * 7, scratch, 1, 62, "middle"
    )


class Ring:
    def __init__(self, n, x, recv, send_sem, recv_sem):
        self.n, self.x, self.recv = n, x, recv
        self.send_sem, self.recv_sem = send_sem, recv_sem
        self.subs, self.rows = recv.shape[2], recv.shape[3]
        s = lax.axis_index("seq")
        half = n // 2
        self.r = jnp.where(lax.rem(s, 2) == 0, s // 2, n - 1 - s // 2)

        def dev(q):
            q = lax.rem(q + n, n)
            return jnp.where(q < half, 2 * q, 2 * (n - 1 - q) + 1)

        self.target = (dev(self.r + 1), dev(self.r - 1))
        self.done = 0
        self.total = 2 * n - 2

    def chunk(self, d, b, off):
        sign = (1, -1)[d]
        c = lax.rem(self.r + sign * off + 2 * self.n, self.n)
        at = ((d * self.n + c) * self.subs + b) * self.rows
        return pl.ds(pl.multiple_of(at, self.rows), self.rows)

    def copy(self, d, b, src, dst, k):
        return pltpu.make_async_remote_copy(
            src_ref=src,
            dst_ref=dst,
            send_sem=self.send_sem.at[d, b, k],
            recv_sem=self.recv_sem.at[d, b, k],
            device_id={"seq": self.target[d]},
            device_id_type=MESH,
        )

    def first(self, d, b):
        return self.copy(d, b, self.x.at[self.chunk(d, b, 0)], self.recv.at[d, 0, b], 0)

    def sums(self, d, b, k):
        prior = jnp.maximum(k - 1, 0)
        return self.copy(d, b, self.recv.at[d, prior, b], self.recv.at[d, k, b], k)

    def alls(self, d, b, k):
        ref = self.x.at[self.chunk(d, b, 1 - k)]
        return self.copy(d, b, ref, ref, self.n - 1 + k)

    def each(self):
        return [(d, b) for b in range(self.subs) for d in range(2)]

    def add(self, d, b, k):
        mine = self.x[self.chunk(d, b, -k - 1)]
        return (self.recv[d, k, b].astype(F32) + mine.astype(F32)).astype(BF)

    def start(self):
        for d, b in self.each():
            self.first(d, b).start()

    def tick(self, t):
        n = self.n

        def leave():
            for d, b in self.each():
                self.first(d, b).wait_send()

        def sum_step():
            for d, b in self.each():
                self.sums(d, b, t).wait_recv()
                self.recv[d, t, b] = self.add(d, b, t)
                self.sums(d, b, t + 1).start()

        def turn():
            for d, b in self.each():
                self.sums(d, b, n - 2).wait_recv()
                self.x[self.chunk(d, b, 1)] = self.add(d, b, n - 2)
                self.alls(d, b, 0).start()

        def all_step():
            k = t - (n - 1)
            for d, b in self.each():
                self.alls(d, b, k).wait_recv()
                self.alls(d, b, k + 1).start()

        def close():
            for d, b in self.each():
                self.alls(d, b, n - 2).wait_recv()

        steps = (
            (t == 0, leave),
            (t < n - 2, sum_step),
            (t == n - 2, turn),
            ((t > n - 2) & (t < 2 * n - 3), all_step),
            (t == 2 * n - 3, close),
        )
        for when, step in steps:
            if isinstance(t, int):
                if when:
                    step()
            else:
                pl.when(when)(step)

    def go(self, fourteenths):
        upto = min(-(-fourteenths * self.total // 14), self.total)
        if upto - self.done == 1:
            self.tick(self.done)
        elif upto > self.done:

            def one(t, c):
                self.tick(t)
                return c

            lax.fori_loop(self.done, upto, one, 0)
        self.done = max(upto, self.done)

    def drain(self):
        def more(k, c):
            for d, b in self.each():
                self.sums(d, b, k + 1).wait_send()
                self.alls(d, b, k).wait_send()
            return c

        lax.fori_loop(0, self.n - 2, more, 0)
        for d, b in self.each():
            self.alls(d, b, self.n - 2).wait_send()


LAST_IN = (
    "q",
    "k",
    "v",
    "lse",
    "att",
    "w_out",
    "nf",
    "ctx",
    "wq",
    "wk",
    "wv",
    "rate",
    "cin",
    "cout",
    "start",
    "keep",
    "endg",
    "mlp",
    "h1",
    "dh1",
    "tok",
    "gain",
    "midg",
    "ffn",
)


def last_kernel(n, refs_in, outs, h, scr):
    x1, x2 = scr["x1"], scr["x2"]
    ffn_rows = refs_in[LAST_IN.index("ffn")].shape[0]
    h = dict(h, ffn=x1.at[0:ffn_rows])
    fetch = Fetch(LAST_IN, refs_in, h, scr["fetch"])
    need = fetch.need
    mixed_o, tg_o, sum1_o, sum2_o, gain_o = outs
    s = lax.axis_index("seq")
    me, mate, across, diag = tp_peers()
    peers = (mate, across, diag)
    nf, rate, tok = h["nf"], h["rate"], h["tok"]
    block = nf.shape[1]
    rows = block // 4
    width = nf.shape[2]
    chan = rate.shape[1]
    rk, rv, gath, dcr = scr["rk"], scr["rv"], scr["gath"], scr["dcr"]
    gath[...] = jnp.zeros_like(gath)
    if x1.shape[0] > ffn_rows:
        x1[ffn_rows:] = jnp.zeros((x1.shape[0] - ffn_rows, chan), BF)
    used2 = 4 * width + 3 * NS
    if x2.shape[0] > used2:
        x2[used2:] = jnp.zeros((x2.shape[0] - used2, chan), BF)

    @pl.when(s == n - 1)
    def _():
        rk[...] = jnp.zeros_like(rk)
        rv[...] = jnp.zeros_like(rv)
        dcr[...] = jnp.zeros_like(dcr)

    greet(n, True)
    before = lax.rem(s + n - 1, n)
    own = pl.ds(pl.multiple_of(me * rows, rows), rows)

    def to_before(sem, slot, src, dst):
        return remote(
            src, dst, scr["send_k"].at[sem, slot], scr["recv_k"].at[sem, slot], seq=before
        )

    ring1 = Ring(n, x1, scr["r1"], scr["s1s"], scr["s1r"])
    ring2 = Ring(n, x2, scr["r2"], scr["s2s"], scr["s2r"])
    rr, da, dh1 = scr["rr"], scr["da"], h["dh1"]
    need("dh1")
    for m in range(2):
        rr[m, own, :] = dh1[m].astype(BF)
    greeted(n, True)
    gathers = [Gather(rr.at[m], scr["rs"].at[m], scr["rrv"].at[m]) for m in range(2)]
    for g in gathers:
        g.start()
    need("ffn")
    ring1.start()
    need("w_out", "q", "k", "v", "lse", "keep")

    q, k, v, lse, keep, w_out = (h[name] for name in ("q", "k", "v", "lse", "keep", "w_out"))
    edge0 = k.shape[1] - block
    half = block // 2
    row_ids = lax.broadcasted_iota(jnp.int32, (half, half), 0)
    col_ids = lax.broadcasted_iota(jnp.int32, (half, half), 1)
    scale = HD ** (-0.5)
    dq_s, dko, dvo, dkc, dvc = (scr[x] for x in ("dq", "dko", "dvo", "dkc", "dvc"))
    dkp, dvp, ak, av = (scr[x] for x in ("dkp", "dvp", "ak", "av"))

    def attend_one(m, head):
        i = 2 * m + head
        lanes = pl.ds(pl.multiple_of(head * HD, HD), HD)
        shut = (keep[pl.ds(m, 1), 0:half] - 1.0) * -neg_big
        for part in (1, 0):
            mine = slice(part * half, (part + 1) * half)
            edge = edge0 + part * half
            qq = q[m, mine, lanes]
            kk = k[m, 0 : edge + half, lanes]
            dd = da[m, mine, lanes]
            sc = dot(kk, qq, NT) * scale
            pieces = [sc[:edge0] + shut]
            if part:
                pieces.append(sc[edge0:edge])
            pieces.append(jnp.where(row_ids <= col_ids, sc[edge:], neg_big))
            sc = jnp.concatenate(pieces, axis=0)
            probs = jnp.exp(sc - lse[m, head, :, mine])
            dp = dot(v[m, 0 : edge + half, lanes], dd, NT)
            spread_sum = jnp.sum(probs * dp, axis=0, keepdims=True)
            ds = (probs * (dp - spread_sum)).astype(BF)
            dq_s[m, mine, lanes] = (dot(kk, ds, TN) * scale).T.astype(BF)
            dk = dot(ds, qq) * scale
            dv = dot(probs.astype(BF), dd)
            if part:
                ak[...] = dk
                av[...] = dv
            else:
                ak[0 : edge + half] += dk
                av[0 : edge + half] += dv
        for acc, far, prev, own in ((ak, dkc, dkp, dko), (av, dvc, dvp, dvo)):
            far[m, :, lanes] = acc[0:CTX].astype(BF)
            prev[i] = acc[CTX:edge0].astype(BF)
            own[m, :, lanes] = acc[edge0:]

        @pl.when(s > 0)
        def _():
            to_before(0, i, dkp.at[i], rk.at[i]).start()
            to_before(1, i, dvp.at[i], rv.at[i]).start()

    def stream_back(m, c):
        g = Gather(rr.at[m], scr["rs"].at[m], scr["rrv"].at[m])
        g.near()
        g.pass_on()
        g.far()
        da[m] = dot(rr[m], w_out[...], NT).astype(BF)

        def heads(head, c):
            attend_one(m, head)
            return c

        lax.fori_loop(0, chan // HD, heads, 0)
        ring1.tick(m)
        return c

    lax.fori_loop(0, 2, stream_back, 0)
    ring1.done = 2

    cp, cr, dcs = scr["cp"], scr["cr"], scr["dcs"]
    wq, wk, wv = h["wq"], h["wk"], h["wv"]
    need("wq", "wk", "wv")
    ctx_part = dot(dkc[...].reshape(2 * CTX, chan), wk[...], NT) + dot(
        dvc[...].reshape(2 * CTX, chan), wv[...], NT
    )
    for j in range(4):
        cp[j] = ctx_part[:, j * chan : (j + 1) * chan].astype(BF).reshape(2, CTX, chan)

    def to_peer(i, src, dst, kind):
        return remote(
            src, dst, scr["send_c"].at[kind, i], scr["recv_c"].at[kind, i], tp=peers[i]
        )

    ctx_out = [to_peer(i, cp.at[peers[i]], cr.at[i], 0) for i in range(3)]
    for c in ctx_out:
        c.start()
    need("mlp", "h1")
    mlp, h1 = h["mlp"], h["h1"]

    def scatter(kind, m):
        at = 2 * kind + m
        return Scatter(
            mlp.at[m], scr["over"].at[at], scr["into"].at[at], scr["ss"].at[at], scr["sr"].at[at]
        )

    mlp_sums = [scatter(0, m) for m in range(2)]
    for c in mlp_sums:
        c.start()

    u_s, du_s, hist = scr["u"], scr["du"], scr["hist"]
    cols = pl.ds(pl.multiple_of(me * chan, chan), chan)
    need("nf", "rate", "cin", "cout", "start", "endg")
    for m in range(2):
        u_s[m] = nf[m, :, cols].astype(F32)
    decay = jnp.exp(-rate[...])
    root = jnp.sqrt(1.0 - decay * decay)
    drive = root * h["cin"][...]
    out_c = h["cout"][...]
    start, endg = h["start"], h["endg"]
    for m in range(2):
        hist[0, m] = start[m].astype(BF)

    def run(i, state):
        base = pl.multiple_of(i * 8, 8)
        state = list(state)
        for k in range(8):
            for m in range(2):
                state[m] = decay * state[m] + drive * u_s[m, pl.ds(base + k, 1), :]
                hist[base + k + 1, m] = state[m].astype(BF)
        return tuple(state)

    lax.fori_loop(0, block // 8, run, (start[0], start[1]))
    ctx_back = to_before(0, 4, dcs, dcr)
    total = cp[me].astype(F32)
    for i in range(3):
        ctx_out[i].wait_recv()
        total = total + cr[i].astype(F32)
    dcs[...] = total.astype(BF)

    @pl.when(s > 0)
    def _():
        ctx_back.start()

    for c in mlp_sums:
        c.turn()
    need("att")
    flat_att = h["att"][...].reshape(2 * block, chan)
    tile = 256

    def proj(j, c):
        cols = pl.ds(pl.multiple_of(j * tile, tile), tile)
        right = rr[:, :, cols].reshape(2 * block, tile)
        at = pl.multiple_of(3 * width + j * tile, tile)
        x2[pl.ds(at, tile), :] = dot(flat_att, right, TN).astype(BF)
        return c

    lax.fori_loop(0, width // tile, proj, 0)
    ring1.go(3)

    @pl.when(s < n - 1)
    def _():
        ctx_back.wait_recv()

    dy_s = scr["dy"]
    dy_s[...] = dcr[...].astype(F32)
    zero = jnp.zeros((NS, chan), F32)

    def early(i, grad):
        base = pl.multiple_of(CTX - 8 - i * 8, 8)
        grad = list(grad)
        for k in range(7, -1, -1):
            for m in range(2):
                grad[m] = decay * grad[m] + out_c * dy_s[m, pl.ds(base + k, 1), :]
        return tuple(grad)

    got = lax.fori_loop(0, CTX // 8, early, (zero, zero))
    reach = jnp.exp(-rate[...] * (block - CTX + 1.0))
    whole = jnp.exp(-rate[...] * block)
    pay = scr["pay"]
    for m in range(2):
        pay[m * NS : (m + 1) * NS] = reach * got[m] + whole * endg[m]
    pay[2 * NS : 2 * NS + 8] = keep[...]

    def spread(k):
        return remote(
            pay,
            gath.at[k],
            scr["send_g"].at[0, k],
            scr["recv_g"].at[0, k],
            seq=lax.rem(s + n - k, n),
        )

    for k in range(1, n):

        @pl.when(s >= k)
        def _():
            spread(k).start()

    ring1.go(4)
    for m in range(2):
        mixed_o[m] = (h1[m] + mlp_sums[m].end()).astype(BF)
    for k in range(1, n):

        @pl.when(s + k < n)
        def _():
            spread(k).wait_recv()

    def chain(i, carry):
        k = n - 1 - i
        got = gath[k]
        valid = s + k < n
        return tuple(
            jnp.where(
                valid,
                got[2 * NS + m : 2 * NS + m + 1]
                * (got[m * NS : (m + 1) * NS] + whole * carry[m]),
                carry[m],
            )
            for m in range(2)
        )

    carry = lax.fori_loop(0, n - 1, chain, (zero, zero))
    grads0 = tuple(endg[m] + carry[m] for m in range(2))

    def back_late(i, val):
        hold, d_drive, d_decay, d_out = list(val[0:2]), val[2], val[3], val[4]
        low_row = pl.multiple_of(CTX - 8 - i * 8, 8)
        base = pl.multiple_of(block - 8 - i * 8, 8)
        for k in range(7, -1, -1):
            for m in range(2):
                dy = dy_s[m, pl.ds(low_row + k, 1), :]
                grad = hold[m] + out_c * dy
                du_s[m, pl.ds(base + k, 1), :] = jnp.sum(drive * grad, axis=0, keepdims=True)
                d_drive = d_drive + grad * u_s[m, pl.ds(base + k, 1), :]
                d_decay = d_decay + grad * hist[base + k, m].astype(F32)
                d_out = d_out + dy * hist[base + k + 1, m].astype(F32)
                hold[m] = decay * grad
        return hold[0], hold[1], d_drive, d_decay, d_out

    val = lax.fori_loop(0, CTX // 8, back_late, (grads0[0], grads0[1], zero, zero, zero))

    def back_early(i, val):
        hold, d_drive, d_decay = list(val[0:2]), val[2], val[3]
        base = pl.multiple_of(block - CTX - 8 - i * 8, 8)
        for k in range(7, -1, -1):
            for m in range(2):
                grad = hold[m]
                du_s[m, pl.ds(base + k, 1), :] = jnp.sum(drive * grad, axis=0, keepdims=True)
                d_drive = d_drive + grad * u_s[m, pl.ds(base + k, 1), :]
                d_decay = d_decay + grad * hist[base + k, m].astype(F32)
                hold[m] = decay * grad
        return hold[0], hold[1], d_drive, d_decay

    _, _, d_drive, d_decay = lax.fori_loop(0, (block - CTX) // 8, back_early, val[0:4])
    at = 4 * width
    x2[at : at + NS] = (-decay * (d_decay - d_drive * h["cin"][...] * decay / root)).astype(BF)
    x2[at + NS : at + 2 * NS] = (d_drive * root).astype(BF)
    x2[at + 2 * NS : at + 3 * NS] = val[4].astype(BF)
    ring1.go(5)

    @pl.when(s < n - 1)
    def _():
        for i in range(4):
            to_before(0, i, dkp.at[i], rk.at[i]).wait_recv()
            to_before(1, i, dvp.at[i], rv.at[i]).wait_recv()

    dk_b, dv_b = scr["dkb"], scr["dvb"]
    for m in range(2):
        for head in range(chan // HD):
            lanes = slice(head * HD, (head + 1) * HD)
            i = m * (chan // HD) + head
            dk_b[m, :, lanes] = (dko[m, :, lanes] + rk[i].astype(F32)).astype(BF)
            dv_b[m, :, lanes] = (dvo[m, :, lanes] + rv[i].astype(F32)).astype(BF)

    part_s = scr["part"]

    def normed_part(i, c):
        m, part = i // 2, lax.rem(i, 2)
        here = pl.ds(pl.multiple_of(part * half, half), half)
        part_s[...] = (
            dot(dq_s[m, here, :], wq[...], NT)
            + dot(dk_b[m, here, :], wk[...], NT)
            + dot(dv_b[m, here, :], wv[...], NT)
        )
        part_s[:, cols] += du_s[m, here, :]
        mlp[m, here, :] = part_s[...].astype(BF)
        return c

    finals = [scatter(1, m) for m in range(2)]
    for m in range(2):
        lax.fori_loop(2 * m, 2 * m + 2, normed_part, 0)
        finals[m].start()
    finals[0].turn()
    need("ctx")
    ctx = h["ctx"]

    def grads(i, c):
        at = pl.multiple_of(i * tile, tile)
        here = pl.ds(at, tile)
        left = nf[:, :, here].reshape(2 * block, tile)
        left_ctx = ctx[:, :, here].reshape(2 * CTX, tile)
        x2[pl.ds(at, tile), :] = dot(left, dq_s[...].reshape(2 * block, chan), TN).astype(BF)
        for j, (own, far) in enumerate(((dk_b, dkc), (dv_b, dvc))):
            value = dot(left, own[...].reshape(2 * block, chan), TN) + dot(
                left_ctx, far[...].reshape(2 * CTX, chan), TN
            )
            x2[pl.ds((j + 1) * width + at, tile), :] = value.astype(BF)
        return c

    finals[1].turn()
    lax.fori_loop(0, width // tile, grads, 0)
    ring2.start()
    ring1.go(6)
    need("tok", "gain", "midg")
    gain_grad = jnp.zeros((1, width), F32)
    for m in range(2):
        back, one = rms_back(tok[m].astype(F32), h["gain"][...], finals[m].end())
        tg_o[m] = dh1[m] + back
        gain_grad = gain_grad + one
    gp, gr, gs, gg = scr["gp"], scr["gr"], scr["gs"], scr["gg"]
    for j in range(4):
        gp[j, 0:1] = gain_grad[:, j * chan : (j + 1) * chan]
        gp[j, 1:2] = h["midg"][:, j * chan : (j + 1) * chan]
        gp[j, 2:8] = jnp.zeros((6, chan), F32)
    gains = [to_peer(i, gp.at[peers[i]], gr.at[i], 1) for i in range(3)]
    for c in gains:
        c.start()
    ring1.go(7)
    ring2.go(1)
    total = gp[me]
    for i in range(3):
        gains[i].wait_recv()
        total = total + gr[i]
    gs[...] = total

    def gain_out(k):
        return remote(
            gs,
            gg.at[k],
            scr["send_g"].at[1, k],
            scr["recv_g"].at[1, k],
            seq=lax.rem(s + k, n),
        )

    for k in range(1, n):
        gain_out(k).start()
    for t in range(8, 15):
        ring1.go(t)
        ring2.go(t - 6)
    store1 = pltpu.make_async_copy(x1, sum1_o, scr["store"].at[0])
    store1.start()
    for k in range(1, n):
        gain_out(k).wait_recv()
        total = total + gg[k]
    gain_o[...] = total
    for t in range(9, 15):
        ring2.go(t)
    store2 = pltpu.make_async_copy(x2, sum2_o, scr["store"].at[1])
    store2.start()
    for k in range(1, n):
        gain_out(k).wait_send()
    for c in gains + ctx_out:
        c.wait_send()
    for g in gathers:
        g.finish()

    @pl.when(s > 0)
    def _():
        ctx_back.wait_send()
        for i in range(4):
            to_before(0, i, dkp.at[i], rk.at[i]).wait_send()
            to_before(1, i, dvp.at[i], rv.at[i]).wait_send()

    for k in range(1, n):

        @pl.when(s >= k)
        def _():
            spread(k).wait_send()

    ring1.drain()
    ring2.drain()
    store1.wait()
    store2.wait()


def ring_rows(n, used, subs):
    return -(-used // (2 * n * subs * 16)) * 16


def last(*args):
    n = lax.axis_size("seq")
    by = dict(zip(LAST_IN, args))
    micro, block, width = by["nf"].shape
    rows = block // 4
    chan = by["rate"].shape[1]
    keys = by["k"].shape[1]
    sds = jax.ShapeDtypeStruct
    dma = pltpu.SemaphoreType.DMA
    step1 = ring_rows(n, by["ffn"].shape[0], 2)
    step2 = ring_rows(n, 4 * width + 3 * NS, 1)
    x1 = VM((4 * n * step1, chan), BF)
    x2 = VM((2 * n * step2, chan), BF)
    scratch = dict(
        x1=x1,
        r1=VM((2, n - 1, 2, step1, chan), BF),
        x2=x2,
        r2=VM((2, n - 1, 1, step2, chan), BF),
        s1s=dma((2, 2, 2 * n - 2)),
        s1r=dma((2, 2, 2 * n - 2)),
        s2s=dma((2, 1, 2 * n - 2)),
        s2r=dma((2, 1, 2 * n - 2)),
        fetch=dma((len(LAST_IN),)),
        rr=VM((micro, block, width), BF),
        da=VM((micro, block, chan), BF),
        rs=dma((2, 3)),
        rrv=dma((2, 3)),
        rk=VM((4, block, HD), BF),
        rv=VM((4, block, HD), BF),
        dkp=VM((4, block, HD), BF),
        dvp=VM((4, block, HD), BF),
        ak=VM((keys, HD), F32),
        av=VM((keys, HD), F32),
        dq=VM((micro, block, chan), BF),
        dko=VM((micro, block, chan), F32),
        dvo=VM((micro, block, chan), F32),
        dkb=VM((micro, block, chan), BF),
        dvb=VM((micro, block, chan), BF),
        dkc=VM((micro, CTX, chan), BF),
        dvc=VM((micro, CTX, chan), BF),
        cp=VM((4, micro, CTX, chan), BF),
        cr=VM((3, micro, CTX, chan), BF),
        dcs=VM((micro, CTX, chan), BF),
        dcr=VM((micro, CTX, chan), BF),
        dy=VM((micro, CTX, chan), F32),
        u=VM((micro, block, chan), F32),
        du=VM((micro, block, chan), F32),
        hist=VM((block + 1, micro, NS, chan), BF),
        pay=VM((2 * NS + 8, chan), F32),
        gath=VM((n, 2 * NS + 8, chan), F32),
        part=VM((block // 2, width), F32),
        over=VM((4, rows, width), BF),
        into=VM((4, 3, rows, width), BF),
        ss=dma((4, 3)),
        sr=dma((4, 3)),
        gp=VM((4, 8, chan), F32),
        gr=VM((3, 8, chan), F32),
        gs=VM((8, chan), F32),
        gg=VM((n, 8, chan), F32),
        send_k=dma((2, 5)),
        recv_k=dma((2, 5)),
        send_c=dma((2, 3)),
        recv_c=dma((2, 3)),
        send_g=dma((2, n)),
        recv_g=dma((2, n)),
        store=dma((2,)),
    )
    outs = (
        sds((micro, rows, width), BF),
        sds((micro, rows, width), F32),
        sds(x1.shape, BF),
        sds(x2.shape, BF),
        sds((8, chan), F32),
    )
    return launch(
        functools.partial(last_kernel, n),
        LAST_IN,
        args,
        outs,
        [True, True, False, False, True],
        scratch,
        2,
        62,
        "last",
    )


def finish_kernel(up_i, down_i, proj_i, q_i, k_i, v_i, up, down, proj, q, k, v):
    pairs = ((up_i, up), (down_i, down), (proj_i, proj), (q_i, q), (k_i, k), (v_i, v))
    for src, dst in pairs:
        dst[...] = src[...].astype(F32)


def finish(sum1, sum2, width, units, chan):
    across = width // chan
    sds = jax.ShapeDtypeStruct
    down_at = units * width // chan
    tall = lambda high, at: pl.BlockSpec((high, chan), lambda j: (at // high + j, 0))
    wide = lambda high: pl.BlockSpec((high, chan), lambda j: (0, j))
    col = pl.BlockSpec((chan, chan), lambda j: (j, 0))
    return pl.pallas_call(
        finish_kernel,
        grid=(across,),
        out_shape=(
            sds((width, units), F32),
            sds((units, width), F32),
            sds((chan, width), F32),
            sds((width, chan), F32),
            sds((width, chan), F32),
            sds((width, chan), F32),
        ),
        in_specs=[
            tall(width, 0),
            tall(units, down_at),
            tall(chan, 3 * width),
            tall(chan, 0),
            tall(chan, width),
            tall(chan, 2 * width),
        ],
        out_specs=(wide(width), wide(units), wide(chan), col, col, col),
        compiler_params=pltpu.CompilerParams(vmem_limit_bytes=62 << 20),
        name="finish",
    )(sum1, sum1, sum2, sum2, sum2, sum2)


def body(
    tokens,
    out_grad,
    norm_gain,
    w_query,
    w_key,
    w_value,
    w_out,
    mid_gain,
    w_up,
    w_down,
    ssm_rate,
    ssm_in,
    ssm_out,
    resets,
    init_state,
    states_grad,
):
    micro, rows, width = tokens.shape
    chan = ssm_rate.shape[0]
    units = w_up.shape[1]
    og = lax.all_gather(out_grad, "tp", axis=1, tiled=True)
    rate, cin, cout = ssm_rate.T, ssm_in.T, ssm_out.T
    flags = resets[:, 0]
    keep = jnp.zeros((8, chan), F32).at[0:micro].set((1.0 - flags.astype(F32))[:, None])
    init = jnp.swapaxes(init_state, 1, 2)
    endg = jnp.swapaxes(states_grad[:, 0], 1, 2)
    gain_row, mid_row = norm_gain[None], mid_gain[None]
    nf, q, k, v, ctx, start, end = front(
        tokens, gain_row, w_query, w_key, w_value, rate, cin, cout, keep, init
    )
    mlp, h1, dh1, ffn, att, lse, mid_part = middle(
        q, k, v, keep, w_out, tokens, mid_row, w_up, w_down, og
    )
    mixed, tokens_grad, sum1, sum2, gains = last(
        *(q, k, v, lse, att, w_out, nf, ctx, w_query, w_key, w_value, rate, cin, cout),
        *(start, keep, endg, mlp, h1, dh1, tokens, gain_row, mid_part, ffn),
    )
    up_g, down_g, proj_g, query_g, key_g, value_g = finish(sum1, sum2, width, units, chan)
    small = sum2[4 * width : 4 * width + 3 * NS].astype(F32)
    rate_g, in_g, out_g = (small[i * NS : (i + 1) * NS].T for i in range(3))
    return (
        mixed,
        jnp.swapaxes(end, 1, 2)[:, None],
        tokens_grad,
        gains[0],
        query_g,
        key_g,
        value_g,
        proj_g,
        gains[1],
        up_g,
        down_g,
        rate_g,
        in_g,
        out_g,
    )


def solution(mesh):
    return jax.shard_map(
        body,
        mesh=mesh,
        in_specs=(
            P(None, ("seq", "tp"), None),
            P(None, ("seq", "tp"), None),
            P(),
            P(None, "tp"),
            P(None, "tp"),
            P(None, "tp"),
            P("tp", None),
            P(),
            P(None, "tp"),
            P("tp", None),
            P("tp", None),
            P("tp", None),
            P("tp", None),
            P(None, "seq"),
            P(None, "tp", None),
            P(None, "seq", "tp", None),
        ),
        out_specs=(
            P(None, ("seq", "tp"), None),
            P(None, "seq", "tp", None),
            P(None, ("seq", "tp"), None),
            P("tp"),
            P(None, "tp"),
            P(None, "tp"),
            P(None, "tp"),
            P("tp", None),
            P("tp"),
            P(None, "tp"),
            P("tp", None),
            P("tp", None),
            P("tp", None),
            P("tp", None),
        ),
        check_vma=False,
    )
```

```python
import functools

import jax
import jax.numpy as jnp
from jax import lax
from jax.experimental import pallas as pl
from jax.experimental.pallas import tpu as pltpu
from jax.sharding import PartitionSpec as P

HD = 128
NS = 16
CTX = 128


eps_norm = 1e-06
neg_big = -1e30
MESH = pl.DeviceIdType.MESH
VM = pltpu.VMEM
BF = jnp.bfloat16
F32 = jnp.float32
NT = (((1,), (1,)), ((), ()))
TN = (((0,), (0,)), ((), ()))
NN = (((1,), (0,)), ((), ()))


def dot(left, right, dims=NN):
    return lax.dot_general(left, right, dims, preferred_element_type=F32)


def vmem_specs(count):
    return [pl.BlockSpec(memory_space=VM)] * count


def tp_peers():
    me = lax.axis_index("tp")
    mate = me + 1 - 2 * lax.rem(me, 2)
    return me, mate, lax.rem(me + 2, 4), lax.rem(mate + 2, 4)


def remote(src, dst, send, recv, **where):
    return pltpu.make_async_remote_copy(
        src_ref=src,
        dst_ref=dst,
        send_sem=send,
        recv_sem=recv,
        device_id=where,
        device_id_type=MESH,
    )


def greet(n, with_seq):
    s = lax.axis_index("seq")
    barrier = pltpu.get_barrier_semaphore()
    for peer in tp_peers()[1:]:
        pl.semaphore_signal(barrier, inc=1, device_id={"tp": peer}, device_id_type=MESH)
    if with_seq:
        for k in range(1, n):
            pl.semaphore_signal(
                barrier, inc=1, device_id={"seq": lax.rem(s + k, n)}, device_id_type=MESH
            )


def greeted(n, with_seq):
    pl.semaphore_wait(pltpu.get_barrier_semaphore(), 3 + (n - 1 if with_seq else 0))


class Fetch:
    def __init__(self, names, refs, held, sems):
        self.copies = {
            name: pltpu.make_async_copy(ref, held[name], sems.at[i])
            for i, (name, ref) in enumerate(zip(names, refs))
        }
        self.ready = set()
        for c in self.copies.values():
            c.start()

    def need(self, *wanted):
        for name in wanted:
            if name not in self.ready:
                self.copies[name].wait()
                self.ready.add(name)


class Gather:
    def __init__(self, ref, send, recv):
        rows = ref.shape[0] // 4
        me, mate, across, _ = tp_peers()

        def give(slot, quarter, peer):
            part = ref.at[pl.ds(pl.multiple_of(quarter * rows, rows), rows), :]
            return remote(part, part, send.at[slot], recv.at[slot], tp=peer)

        self.cross = give(1, me, across)
        self.side = give(0, me, mate)
        self.relay = give(2, across, mate)

    def start(self):
        self.cross.start()
        self.side.start()

    def near(self):
        self.side.wait_recv()

    def pass_on(self):
        self.cross.wait_recv()
        self.relay.start()

    def far(self):
        self.relay.wait_recv()

    def finish(self):
        for c in (self.side, self.cross, self.relay):
            c.wait_send()


class Scatter:
    def __init__(self, ref, over, into, send, recv):
        self.ref, self.over, self.into = ref, over, into
        self.rows = ref.shape[0] // 4
        self.me, self.mate, self.across, self.diag = tp_peers()
        self.hop = [
            remote(self.quarter(self.diag), into.at[0], send.at[0], recv.at[0], tp=self.mate),
            remote(self.quarter(self.mate), into.at[1], send.at[1], recv.at[1], tp=self.mate),
            remote(over, into.at[2], send.at[2], recv.at[2], tp=self.across),
        ]

    def span(self, quarter):
        return pl.ds(pl.multiple_of(quarter * self.rows, self.rows), self.rows)

    def quarter(self, quarter):
        return self.ref.at[self.span(quarter), :]

    def start(self):
        self.hop[0].start()
        self.hop[1].start()

    def turn(self):
        self.hop[0].wait_recv()
        mine = self.ref[self.span(self.across), :].astype(F32)
        self.over[...] = (mine + self.into[0].astype(F32)).astype(BF)
        self.hop[2].start()

    def end(self):
        self.hop[1].wait_recv()
        value = self.ref[self.span(self.me), :].astype(F32) + self.into[1].astype(F32)
        self.hop[2].wait_recv()
        value = value + self.into[2].astype(F32)
        for c in self.hop:
            c.wait_send()
        return value


FRONT_IN = ("tok", "gain", "wq", "wk", "wv", "rate", "cin", "cout", "keep", "init", "ogm")


class Save:
    def __init__(self, sems):
        self.sems, self.copies = sems, []

    def __call__(self, src, dst):
        self.copies.append(pltpu.make_async_copy(src, dst, self.sems.at[len(self.copies)]))
        self.copies[-1].start()

    def finish(self):
        for c in self.copies:
            c.wait()


def front_kernel(n, refs_in, outs, held, scr):
    s = lax.axis_index("seq")
    me, mate, across, diag = tp_peers()
    og = scr["og"]
    own_rows = og.shape[1] // 4
    own = pl.ds(pl.multiple_of(me * own_rows, own_rows), own_rows)
    held = dict(held, ogm=og.at[:, own, :])
    fetch = Fetch(FRONT_IN, refs_in, held, scr["fetch"])
    nf_d, og_d, q_d, k_d, v_d, ctx_d, start_o, end_o = outs
    nf, q_o, k_o, v_o, ctx_o = (scr[x] for x in ("nf", "q", "k", "v", "ctxa"))
    save = Save(scr["save"])
    grad_gathers = [Gather(og.at[m], scr["os"].at[m], scr["or"].at[m]) for m in range(2)]
    tok, rate, keep, init = (held[x] for x in ("tok", "rate", "keep", "init"))
    wq, wk, wv = held["wq"], held["wk"], held["wv"]
    u_s, gath, pay, y_s, ctx_s = (scr[x] for x in ("u", "gath", "pay", "y", "ctx"))
    block = nf.shape[1]
    rows = block // 4
    chan = rate.shape[1]
    gath[...] = jnp.zeros_like(gath)

    @pl.when(s == 0)
    def _():
        k_o[:, 0 : CTX + block, :] = jnp.zeros((2, CTX + block, chan), BF)
        v_o[:, 0 : CTX + block, :] = jnp.zeros((2, CTX + block, chan), BF)
        ctx_o[...] = jnp.zeros_like(ctx_o)

    greet(n, True)

    def span(quarter):
        return pl.ds(pl.multiple_of(quarter * rows, rows), rows)

    def lanes(part):
        return pl.ds(pl.multiple_of(part * chan, chan), chan)

    fetch.need("tok", "gain")
    x = tok[...].astype(F32).reshape(2 * rows, -1)
    normed = x * lax.rsqrt(jnp.mean(x * x, axis=-1, keepdims=True) + eps_norm) * held["gain"][...]
    nf[:, span(me), :] = normed.astype(BF).reshape(2, rows, -1)
    greeted(n, True)

    def give(slot, quarter, peer, part=None):
        cols = slice(None) if part is None else lanes(part)
        ref = nf.at[:, span(quarter), cols]
        return remote(ref, ref, scr["ts"].at[slot], scr["tr"].at[slot], tp=peer)

    cross = [give(1 + i, me, across, part) for i, part in enumerate((across, diag, me, mate))]
    relay = [give(5 + i, across, mate, part) for i, part in enumerate((me, mate, across, diag))]
    side = give(0, me, mate)
    for c in cross:
        c.start()
    side.start()

    def pass_kv(slot, src, half):
        high = 2 * rows
        part = pl.ds(pl.multiple_of(CTX + half * high, rows), high)
        own = pl.ds(pl.multiple_of(CTX + block + half * high, rows), high)
        return remote(
            src.at[:, own, :],
            src.at[:, part, :],
            scr["kvs"].at[slot],
            scr["kvr"].at[slot],
            seq=lax.rem(s + 1, n),
        )

    def qkv(order, half):
        high = 2 * rows
        here = pl.ds(pl.multiple_of(half * high, high), high)
        part = nf[:, here, :].reshape(2 * high, -1)
        own = pl.ds(pl.multiple_of(CTX + block + half * high, rows), high)
        k_o[:, own, :] = dot(part, wk[...]).astype(BF).reshape(2, high, chan)
        v_o[:, own, :] = dot(part, wv[...]).astype(BF).reshape(2, high, chan)

        @pl.when(s < n - 1)
        def _():
            pass_kv(2 * order, k_o, half).start()
            pass_kv(2 * order + 1, v_o, half).start()

        q_o[:, here, :] = dot(part, wq[...]).astype(BF).reshape(2, high, chan)

    near = me // 2
    side.wait_recv()
    fetch.need("wk", "wv", "wq")
    qkv(0, near)
    cross[0].wait_recv()
    cross[1].wait_recv()
    relay[1].start()
    relay[0].start()
    relay[1].wait_recv()
    fetch.need("rate", "cin", "cout", "keep", "init")
    cols = lanes(me)
    for m in range(2):
        u_s[m] = nf[m, :, cols].astype(F32)
    decay = jnp.exp(-rate[...])
    drive = jnp.sqrt(1.0 - decay * decay) * held["cin"][...]

    def run(i, state):
        base = pl.multiple_of(i * 8, 8)
        state = list(state)
        for k in range(8):
            for m in range(2):
                state[m] = decay * state[m] + drive * u_s[m, pl.ds(base + k, 1), :]
        return tuple(state)

    zero = jnp.zeros((NS, chan), F32)
    late = lax.fori_loop(0, (block - CTX) // 8, run, (zero, zero))
    last_state = lax.fori_loop((block - CTX) // 8, block // 8, run, late)
    pay[0:NS] = last_state[0]
    pay[NS : 2 * NS] = last_state[1]
    pay[2 * NS : 2 * NS + 8] = keep[...]

    def spread(k):
        return remote(
            pay, gath.at[k], scr["gs"].at[k], scr["gr"].at[k], seq=lax.rem(s + k, n)
        )

    for k in range(1, n):

        @pl.when(s + k < n)
        def _():
            spread(k).start()

    for i in (2, 3):
        cross[i].wait_recv()
        relay[i].start()
    for i in (0, 2, 3):
        relay[i].wait_recv()
    fetch.need("ogm")
    for g in grad_gathers:
        g.start()
    qkv(1, 1 - near)
    save(nf, nf_d)
    save(q_o, q_d)

    whole = jnp.exp(-rate[...] * block)
    for k in range(1, n):

        @pl.when(s >= k)
        def _():
            spread(k).wait_recv()

    def entry(begin_keep, end, b):
        return tuple(jnp.where(b == 0, init[m], begin_keep[m] * end[m]) for m in range(2))

    def chain(b, end):
        k = jnp.maximum(s - b, 0)
        got = gath[k]
        begin = entry((got[2 * NS : 2 * NS + 1], got[2 * NS + 1 : 2 * NS + 2]), end, b)
        new = tuple(got[m * NS : (m + 1) * NS] + whole * begin[m] for m in range(2))
        return tuple(jnp.where(b < s, new[m], end[m]) for m in range(2))

    end = lax.fori_loop(0, n - 1, chain, (zero, zero))
    begin = entry((keep[0:1, :], keep[1:2, :]), end, s)
    toward = jnp.exp(-rate[...] * (block - CTX))
    state = tuple(late[m] + toward * begin[m] for m in range(2))
    out_c = held["cout"][...]

    def run_out(i, state):
        base = pl.multiple_of(block - CTX + i * 8, 8)
        row = pl.multiple_of(i * 8, 8)
        state = list(state)
        for k in range(8):
            for m in range(2):
                state[m] = decay * state[m] + drive * u_s[m, pl.ds(base + k, 1), :]
                y_s[m, pl.ds(row + k, 1), :] = jnp.sum(out_c * state[m], axis=0, keepdims=True)
        return tuple(state)

    state = lax.fori_loop(0, CTX // 8, run_out, state)
    ctx_s[...] = y_s[...].astype(BF)
    down = remote(
        ctx_s, ctx_o.at[:, :, cols], scr["cs"].at[0], scr["cr"].at[0], seq=lax.rem(s + 1, n)
    )

    @pl.when(s < n - 1)
    def _():
        down.start()

    for m in range(2):
        start_o[m] = begin[m]
        end_o[m] = last_state[m] + whole * begin[m]
    for g in grad_gathers:
        g.near()
        g.pass_on()

    @pl.when(s > 0)
    def _():
        down.wait_recv()
        mine = ctx_o.at[:, :, cols]
        shares = [
            remote(mine, mine, scr["cs"].at[1 + i], scr["cr"].at[1 + i], tp=peer)
            for i, peer in enumerate((across, diag, mate))
        ]
        for c in shares:
            c.start()
        for c in shares:
            c.wait_recv()
        flat = ctx_o[...].reshape(2 * CTX, -1)
        k_o[:, 0:CTX, :] = dot(flat, wk[...]).astype(BF).reshape(2, CTX, chan)
        v_o[:, 0:CTX, :] = dot(flat, wv[...]).astype(BF).reshape(2, CTX, chan)
        for order, half in enumerate((near, 1 - near)):
            pass_kv(2 * order, k_o, half).wait_recv()
            pass_kv(2 * order + 1, v_o, half).wait_recv()
        for c in shares:
            c.wait_send()

    save(k_o, k_d)
    save(v_o, v_d)
    save(ctx_o, ctx_d)
    for g in grad_gathers:
        g.far()
    save(og, og_d)

    @pl.when(s < n - 1)
    def _():
        down.wait_send()
        for order, half in enumerate((near, 1 - near)):
            pass_kv(2 * order, k_o, half).wait_send()
            pass_kv(2 * order + 1, v_o, half).wait_send()

    for k in range(1, n):

        @pl.when(s + k < n)
        def _():
            spread(k).wait_send()

    for c in [side] + cross + relay:
        c.wait_send()
    for g in grad_gathers:
        g.finish()
    save.finish()


def launch(
    body, names, args, outs, out_vmem, scratch, collective_id, limit, name, placed=()
):
    keys = list(scratch)
    count = len(names)
    plain = [name for name in names if name not in placed]

    def kernel(*refs):
        refs_in, refs = refs[:count], refs[count:]
        outs_r, refs = refs[: len(outs)], refs[len(outs) :]
        held, refs = dict(zip(plain, refs)), refs[len(plain) :]
        body(refs_in, outs_r, held, dict(zip(keys, refs)))

    scratch = dict(scratch)
    return pl.pallas_call(
        kernel,
        out_shape=tuple(outs),
        in_specs=[pl.BlockSpec(memory_space=pl.ANY)] * count,
        out_specs=tuple(
            pl.BlockSpec(memory_space=VM if in_vmem else pl.ANY) for in_vmem in out_vmem
        ),
        scratch_shapes=[VM(a.shape, a.dtype) for x, a in zip(names, args) if x in plain]
        + list(scratch.values()),
        compiler_params=pltpu.CompilerParams(
            collective_id=collective_id, has_side_effects=True, vmem_limit_bytes=limit << 20
        ),
        name=name,
    )(*args)


def front(*args):
    n = lax.axis_size("seq")
    micro, rows, width = args[0].shape
    block = 4 * rows
    chan = args[5].shape[1]
    sds = jax.ShapeDtypeStruct
    dma = pltpu.SemaphoreType.DMA
    outs = (
        sds((micro, block, width), BF),
        sds((micro, block, width), BF),
        sds((micro, block, chan), BF),
        sds((micro, CTX + 2 * block, chan), BF),
        sds((micro, CTX + 2 * block, chan), BF),
        sds((micro, CTX, width), BF),
        sds((micro, NS, chan), F32),
        sds((micro, NS, chan), F32),
    )
    scratch = dict(
        fetch=dma((len(FRONT_IN),)),
        nf=VM((micro, block, width), BF),
        og=VM((micro, block, width), BF),
        q=VM((micro, block, chan), BF),
        k=VM((micro, CTX + 2 * block, chan), BF),
        v=VM((micro, CTX + 2 * block, chan), BF),
        ctxa=VM((micro, CTX, width), BF),
        save=dma((6,)),
        os=dma((2, 3)),
        u=VM((micro, block, chan), F32),
        gath=VM((n, 2 * NS + 8, chan), F32),
        pay=VM((2 * NS + 8, chan), F32),
        y=VM((micro, CTX, chan), F32),
        ctx=VM((micro, CTX, chan), BF),
        ts=dma((9,)),
        tr=dma((9,)),
        kvs=dma((4,)),
        kvr=dma((4,)),
        gs=dma((n,)),
        gr=dma((n,)),
        cs=dma((4,)),
        cr=dma((4,)),
    )
    scratch["or"] = dma((2, 3))
    return launch(
        functools.partial(front_kernel, n),
        FRONT_IN,
        args,
        outs,
        [False] * 6 + [True] * 2,
        scratch,
        0,
        62,
        "front",
        ("ogm",),
    )


def rms_back(x, gain, grad):
    inv = lax.rsqrt(jnp.mean(x * x, axis=-1, keepdims=True) + eps_norm)
    unit = x * inv
    scaled = grad * gain
    gain_grad = jnp.sum(grad * unit, axis=0, keepdims=True)
    return inv * (scaled - unit * jnp.mean(scaled * unit, axis=-1, keepdims=True)), gain_grad


MIDDLE_IN = ("q", "k", "v", "keep", "w_out", "tok", "gain", "w_up", "w_down", "og")


def middle_kernel(refs_in, outs, held, scr):
    fetch = Fetch(MIDDLE_IN, refs_in, held, scr["fetch"])
    nm, pm, dm, hid, dpre = (scr[x] for x in ("nm", "pm", "dm", "hid", "dpre"))
    mlp_o, h1_o, ffn_o, att, lse = (scr[x] for x in ("mlp", "h1", "ffn", "att", "lse"))
    save = Save(scr["save"])
    q, k, v, keep, w_out, tok, gain, w_up, w_down, og = (held[x] for x in MIDDLE_IN)
    me = tp_peers()[0]
    near = me // 2
    block = q.shape[1]
    rows = block // 4
    width = w_out.shape[1]
    tile = 256
    panels = w_up.shape[1] // tile
    greet(0, False)
    own = pl.ds(pl.multiple_of(me * rows, rows), rows)
    edge0 = k.shape[1] - block
    half = block // 2
    row_ids = lax.broadcasted_iota(jnp.int32, (half, half), 0)
    col_ids = lax.broadcasted_iota(jnp.int32, (half, half), 1)
    scale = HD ** (-0.5)

    def attend(m):
        def one(head, c):
            lanes = pl.ds(pl.multiple_of(head * HD, HD), HD)
            shut = (keep[m : m + 1, 0:half] - 1.0) * -neg_big
            for part in range(2):
                mine = slice(part * half, (part + 1) * half)
                edge = edge0 + part * half
                sc = dot(k[m, 0 : edge + half, lanes], q[m, mine, lanes], NT) * scale
                pieces = [sc[:edge0] + shut]
                if part:
                    pieces.append(sc[edge0:edge])
                pieces.append(jnp.where(row_ids <= col_ids, sc[edge:], neg_big))
                sc = jnp.concatenate(pieces, axis=0)
                top = jnp.max(sc, axis=0, keepdims=True)
                expo = jnp.exp(sc - top)
                total = jnp.sum(expo, axis=0, keepdims=True)
                weights = (expo * (1.0 / total)).astype(BF)
                res = dot(v[m, 0 : edge + half, lanes], weights, TN)
                att[m, mine, lanes] = res.T.astype(BF)
                lse[m, head, :, mine] = top + jnp.log(total)
            return c

        lax.fori_loop(0, q.shape[2] // HD, one, 0)

    def scatter(kind, m, ref):
        at = 2 * kind + m
        return Scatter(
            ref.at[m], scr["over"].at[at], scr["into"].at[at], scr["ss"].at[at], scr["sr"].at[at]
        )

    mlp_d, h1_d, dm_d, ffn_d, att_d, lse_d = outs
    sums1 = [scatter(0, m, pm) for m in range(2)]
    gathers = [Gather(nm.at[m], scr["gs"].at[m], scr["gr"].at[m]) for m in range(2)]

    def project(m):
        def one(j, c):
            cols = pl.ds(pl.multiple_of(j * tile, tile), tile)
            pm[m, :, cols] = dot(att[m], w_out[:, cols]).astype(BF)
            return c

        lax.fori_loop(0, width // tile, one, 0)

    def residual(m):
        h1 = tok[m].astype(F32) + sums1[m].end()
        h1_o[m] = h1
        inv = lax.rsqrt(jnp.mean(h1 * h1, axis=-1, keepdims=True) + eps_norm)
        nm[m, own, :] = (h1 * inv * gain[...]).astype(BF)
        gathers[m].start()

    def feed(m, part):
        here = pl.ds(pl.multiple_of(part * half, half), half)
        flat = pl.ds(pl.multiple_of(m * block + part * half, half), half)

        def panel(j, c):
            cols = pl.ds(pl.multiple_of(j * tile, tile), tile)
            pre = dot(nm[m, here, :], w_up[:, cols])
            sq = pre * pre
            t = jnp.tanh((0.7978845608028654 * pre) * (1.0 + 0.044715 * sq))
            hid[flat, cols] = (0.5 * pre * (1.0 + t)).astype(BF)
            slope = 0.5 * (1.0 + t) + (0.3989422804014327 * pre) * (1.0 - t * t) * (
                1.0 + 0.134145 * sq
            )
            dpre[flat, cols] = (slope * dot(og[m, here, :], w_down[cols, :], NT)).astype(BF)
            return c

        lax.fori_loop(0, panels, panel, 0)

        def back(j, c):
            cols = pl.ds(pl.multiple_of(j * tile, tile), tile)
            dm[m, here, cols] = dot(dpre[flat, :], w_up[cols, :], NT).astype(BF)
            return c

        lax.fori_loop(0, width // tile, back, 0)

    def lower(m):
        def one(j, c):
            cols = pl.ds(pl.multiple_of(j * tile, tile), tile)
            flat = slice(m * block, (m + 1) * block)
            mlp_o[m, :, cols] = dot(hid[flat, :], w_down[:, cols]).astype(BF)
            return c

        lax.fori_loop(0, width // tile, one, 0)

    fetch.need("q", "k", "v", "keep")
    attend(0)
    fetch.need("w_out")
    project(0)
    greeted(0, False)
    sums1[0].start()
    sums1[0].turn()
    attend(1)
    project(1)
    save(att, att_d)
    save(lse, lse_d)
    sums1[1].start()
    sums1[1].turn()
    fetch.need("tok", "gain")
    residual(0)
    fetch.need("w_up", "w_down", "og")
    gathers[0].near()
    feed(0, near)
    residual(1)
    save(h1_o, h1_d)
    gathers[0].pass_on()
    gathers[1].near()
    feed(1, near)
    gathers[0].far()
    feed(0, 1 - near)
    save(dm.at[0], dm_d.at[0])
    gathers[1].pass_on()
    gathers[1].far()
    feed(1, 1 - near)
    save(dm.at[1], dm_d.at[1])

    def down_sum(i, c):
        left = hid[:, pl.ds(pl.multiple_of(i * tile, tile), tile)]
        for j in range(width // tile):
            right = og[:, :, j * tile : (j + 1) * tile].reshape(2 * block, tile)
            at = pl.multiple_of((width // tile + j) * panels * tile + i * tile, tile)
            ffn_o[pl.ds(at, tile), :] = dot(left, right, TN).astype(BF)
        return c

    def up_sum(i, c):
        left = nm[:, :, pl.ds(pl.multiple_of(i * tile, tile), tile)].reshape(2 * block, tile)
        for j in range(panels):
            at = pl.multiple_of(j * width + i * tile, tile)
            ffn_o[pl.ds(at, tile), :] = dot(
                left, dpre[:, j * tile : (j + 1) * tile], TN
            ).astype(BF)
        return c

    high = panels * tile * (width // tile)
    lax.fori_loop(0, panels, down_sum, 0)
    save(ffn_o.at[high : 2 * high], ffn_d.at[high : 2 * high])
    lower(0)
    lower(1)
    save(mlp_o, mlp_d)
    lax.fori_loop(0, width // tile, up_sum, 0)
    save(ffn_o.at[0:high], ffn_d.at[0:high])
    for m in range(2):
        gathers[m].finish()
    save.finish()


def middle(*args):
    q, w_out, og, w_up = args[0], args[4], args[9], args[7]
    micro, block, width = og.shape
    rows = block // 4
    units = w_up.shape[1]
    chan = q.shape[2]
    sds = jax.ShapeDtypeStruct
    dma = pltpu.SemaphoreType.DMA
    outs = (
        sds((micro, block, width), BF),
        sds((micro, rows, width), F32),
        sds((micro, block, width), BF),
        sds((2 * units * width // 256, 256), BF),
        sds((micro, block, chan), BF),
        sds((micro, chan // HD, 1, block), F32),
    )
    scratch = dict(
        fetch=dma((len(MIDDLE_IN),)),
        nm=VM((micro, block, width), BF),
        pm=VM((micro, block, width), BF),
        dm=VM((micro, block, width), BF),
        hid=VM((micro * block, units), BF),
        dpre=VM((micro * block, units), BF),
        mlp=VM((micro, block, width), BF),
        h1=VM((micro, rows, width), F32),
        ffn=VM((2 * units * width // 256, 256), BF),
        att=VM((micro, block, chan), BF),
        lse=VM((micro, chan // HD, 1, block), F32),
        save=dma((8,)),
        over=VM((2, rows, width), BF),
        into=VM((2, 3, rows, width), BF),
        ss=dma((2, 3)),
        sr=dma((2, 3)),
        gs=dma((2, 3)),
        gr=dma((2, 3)),
    )
    return launch(
        middle_kernel, MIDDLE_IN, args, outs, [False] * 6, scratch, 1, 62, "middle"
    )


class Ring:
    def __init__(self, n, x, recv, send_sem, recv_sem):
        self.n, self.x, self.recv = n, x, recv
        self.send_sem, self.recv_sem = send_sem, recv_sem
        self.subs, self.rows = recv.shape[2], recv.shape[3]
        s = lax.axis_index("seq")
        half = n // 2
        self.r = jnp.where(lax.rem(s, 2) == 0, s // 2, n - 1 - s // 2)

        def dev(q):
            q = lax.rem(q + n, n)
            return jnp.where(q < half, 2 * q, 2 * (n - 1 - q) + 1)

        self.target = (dev(self.r + 1), dev(self.r - 1))
        self.done = 0
        self.total = 2 * n - 2

    def chunk(self, d, b, off):
        sign = (1, -1)[d]
        c = lax.rem(self.r + sign * off + 2 * self.n, self.n)
        at = ((d * self.n + c) * self.subs + b) * self.rows
        return pl.ds(pl.multiple_of(at, self.rows), self.rows)

    def copy(self, d, b, src, dst, k):
        return pltpu.make_async_remote_copy(
            src_ref=src,
            dst_ref=dst,
            send_sem=self.send_sem.at[d, b, k],
            recv_sem=self.recv_sem.at[d, b, k],
            device_id={"seq": self.target[d]},
            device_id_type=MESH,
        )

    def first(self, d, b):
        return self.copy(d, b, self.x.at[self.chunk(d, b, 0)], self.recv.at[d, 0, b], 0)

    def sums(self, d, b, k):
        prior = jnp.maximum(k - 1, 0)
        return self.copy(d, b, self.recv.at[d, prior, b], self.recv.at[d, k, b], k)

    def alls(self, d, b, k):
        ref = self.x.at[self.chunk(d, b, 1 - k)]
        return self.copy(d, b, ref, ref, self.n - 1 + k)

    def each(self):
        return [(d, b) for b in range(self.subs) for d in range(2)]

    def add(self, d, b, k):
        mine = self.x[self.chunk(d, b, -k - 1)]
        return (self.recv[d, k, b].astype(F32) + mine.astype(F32)).astype(BF)

    def start(self):
        for d, b in self.each():
            self.first(d, b).start()

    def tick(self, t):
        n = self.n

        def leave():
            for d, b in self.each():
                self.first(d, b).wait_send()

        def sum_step():
            for d, b in self.each():
                self.sums(d, b, t).wait_recv()
                self.recv[d, t, b] = self.add(d, b, t)
                self.sums(d, b, t + 1).start()

        def turn():
            for d, b in self.each():
                self.sums(d, b, n - 2).wait_recv()
                self.x[self.chunk(d, b, 1)] = self.add(d, b, n - 2)
                self.alls(d, b, 0).start()

        def all_step():
            k = t - (n - 1)
            for d, b in self.each():
                self.alls(d, b, k).wait_recv()
                self.alls(d, b, k + 1).start()

        def close():
            for d, b in self.each():
                self.alls(d, b, n - 2).wait_recv()

        steps = (
            (t == 0, leave),
            (t < n - 2, sum_step),
            (t == n - 2, turn),
            ((t > n - 2) & (t < 2 * n - 3), all_step),
            (t == 2 * n - 3, close),
        )
        for when, step in steps:
            if isinstance(t, int):
                if when:
                    step()
            else:
                pl.when(when)(step)

    def go(self, fourteenths):
        upto = min(-(-fourteenths * self.total // 14), self.total)
        if upto - self.done == 1:
            self.tick(self.done)
        elif upto > self.done:

            def one(t, c):
                self.tick(t)
                return c

            lax.fori_loop(self.done, upto, one, 0)
        self.done = max(upto, self.done)

    def drain(self):
        def more(k, c):
            for d, b in self.each():
                self.sums(d, b, k + 1).wait_send()
                self.alls(d, b, k).wait_send()
            return c

        lax.fori_loop(0, self.n - 2, more, 0)
        for d, b in self.each():
            self.alls(d, b, self.n - 2).wait_send()


LAST_IN = (
    "q",
    "k",
    "v",
    "lse",
    "att",
    "w_out",
    "nf",
    "ctx",
    "wq",
    "wk",
    "wv",
    "rate",
    "cin",
    "cout",
    "start",
    "keep",
    "endg",
    "mlp",
    "h1",
    "dm",
    "ogm",
    "mid",
    "tok",
    "gain",
    "ffn",
)


def last_kernel(n, refs_in, outs, h, scr):
    x1, x2, x3 = scr["x1"], scr["x2"], scr["x3"]
    ffn_rows = refs_in[LAST_IN.index("ffn")].shape[0]
    h = dict(h, ffn=x1.at[0:ffn_rows])
    fetch = Fetch(LAST_IN, refs_in, h, scr["fetch"])
    need = fetch.need
    mixed_o, tg_o, sum1_o, sum2_o, small_o = outs
    s = lax.axis_index("seq")
    me, mate, across, diag = tp_peers()
    peers = (mate, across, diag)
    nf, rate, tok = h["nf"], h["rate"], h["tok"]
    block = nf.shape[1]
    rows = block // 4
    width = nf.shape[2]
    chan = rate.shape[1]
    rk, rv, gath, dcr = scr["rk"], scr["rv"], scr["gath"], scr["dcr"]
    gath[...] = jnp.zeros_like(gath)
    if x1.shape[0] > ffn_rows:
        x1[ffn_rows:] = jnp.zeros((x1.shape[0] - ffn_rows, chan), BF)
    used2 = 4 * width
    if x2.shape[0] > used2:
        x2[used2:] = jnp.zeros((x2.shape[0] - used2, chan), BF)
    x3[...] = jnp.zeros_like(x3)

    @pl.when(s == n - 1)
    def _():
        rk[...] = jnp.zeros_like(rk)
        rv[...] = jnp.zeros_like(rv)
        dcr[...] = jnp.zeros_like(dcr)

    greet(n, True)
    before = lax.rem(s + n - 1, n)
    own = pl.ds(pl.multiple_of(me * rows, rows), rows)

    def to_before(sem, slot, src, dst):
        return remote(
            src, dst, scr["send_k"].at[sem, slot], scr["recv_k"].at[sem, slot], seq=before
        )

    ring1 = Ring(n, x1, scr["r1"], scr["s1s"], scr["s1r"])
    ring2 = Ring(n, x2, scr["r2"], scr["s2s"], scr["s2r"])
    ring3 = Ring(n, x3, scr["r3"], scr["s3s"], scr["s3r"])
    rr, da, dh1, mlp, h1 = scr["rr"], scr["da"], scr["dh1"], h["mlp"], h["h1"]

    def scatter(ref, at, m):
        at = 2 * at + m
        return Scatter(
            ref.at[m], scr["over"].at[at], scr["into"].at[at], scr["ss"].at[at], scr["sr"].at[at]
        )

    mid_sums = [scatter(h["dm"], 0, m) for m in range(2)]
    gathers = [Gather(rr.at[m], scr["rs"].at[m], scr["rrv"].at[m]) for m in range(2)]
    need("dm")
    greeted(n, True)
    for c in mid_sums:
        c.start()
    need("ffn")
    ring1.start()
    for c in mid_sums:
        c.turn()
    need("h1", "ogm", "mid")
    mid_grad = jnp.zeros((1, width), F32)
    for m in range(2):
        back, one = rms_back(h1[m], h["mid"][...], mid_sums[m].end())
        mid_grad = mid_grad + one
        dh1[m] = h["ogm"][m].astype(F32) + back
        rr[m, own, :] = dh1[m].astype(BF)
        gathers[m].start()
        ring1.go(m + 1)
    need("w_out", "q", "k", "v", "lse", "keep")

    q, k, v, lse, keep, w_out = (h[name] for name in ("q", "k", "v", "lse", "keep", "w_out"))
    edge0 = k.shape[1] - block
    half = block // 2
    row_ids = lax.broadcasted_iota(jnp.int32, (half, half), 0)
    col_ids = lax.broadcasted_iota(jnp.int32, (half, half), 1)
    scale = HD ** (-0.5)
    dq_s, dko, dvo, dkc, dvc = (scr[x] for x in ("dq", "dko", "dvo", "dkc", "dvc"))
    dkp, dvp, ak, av = (scr[x] for x in ("dkp", "dvp", "ak", "av"))

    def attend_one(m, head):
        i = 2 * m + head
        lanes = pl.ds(pl.multiple_of(head * HD, HD), HD)
        shut = (keep[pl.ds(m, 1), 0:half] - 1.0) * -neg_big
        for part in (1, 0):
            mine = slice(part * half, (part + 1) * half)
            edge = edge0 + part * half
            qq = q[m, mine, lanes]
            kk = k[m, 0 : edge + half, lanes]
            dd = da[m, mine, lanes]
            sc = dot(kk, qq, NT) * scale
            pieces = [sc[:edge0] + shut]
            if part:
                pieces.append(sc[edge0:edge])
            pieces.append(jnp.where(row_ids <= col_ids, sc[edge:], neg_big))
            sc = jnp.concatenate(pieces, axis=0)
            probs = jnp.exp(sc - lse[m, head, :, mine])
            dp = dot(v[m, 0 : edge + half, lanes], dd, NT)
            spread_sum = jnp.sum(probs * dp, axis=0, keepdims=True)
            ds = (probs * (dp - spread_sum)).astype(BF)
            dq_s[m, mine, lanes] = (dot(kk, ds, TN) * scale).T.astype(BF)
            dk = dot(ds, qq) * scale
            dv = dot(probs.astype(BF), dd)
            if part:
                ak[...] = dk
                av[...] = dv
            else:
                ak[0 : edge + half] += dk
                av[0 : edge + half] += dv
        for acc, far, prev, own in ((ak, dkc, dkp, dko), (av, dvc, dvp, dvo)):
            far[m, :, lanes] = acc[0:CTX].astype(BF)
            prev[i] = acc[CTX:edge0].astype(BF)
            own[m, :, lanes] = acc[edge0:]

        @pl.when(s > 0)
        def _():
            to_before(0, i, dkp.at[i], rk.at[i]).start()
            to_before(1, i, dvp.at[i], rv.at[i]).start()

    def stream_back(m, c):
        g = Gather(rr.at[m], scr["rs"].at[m], scr["rrv"].at[m])
        g.near()
        g.pass_on()
        g.far()
        ring1.tick(m + ring1.done)
        da[m] = dot(rr[m], w_out[...], NT).astype(BF)

        def heads(head, c):
            attend_one(m, head)
            return c

        lax.fori_loop(0, chan // HD, heads, 0)
        return c

    lax.fori_loop(0, 2, stream_back, 0)
    ring1.done += 2

    cp, cr, dcs = scr["cp"], scr["cr"], scr["dcs"]
    wq, wk, wv = h["wq"], h["wk"], h["wv"]
    need("wq", "wk", "wv")
    ctx_part = dot(dkc[...].reshape(2 * CTX, chan), wk[...], NT) + dot(
        dvc[...].reshape(2 * CTX, chan), wv[...], NT
    )
    for j in range(4):
        cp[j] = ctx_part[:, j * chan : (j + 1) * chan].astype(BF).reshape(2, CTX, chan)

    def to_peer(i, src, dst, kind):
        return remote(
            src, dst, scr["send_c"].at[kind, i], scr["recv_c"].at[kind, i], tp=peers[i]
        )

    ctx_out = [to_peer(i, cp.at[peers[i]], cr.at[i], 0) for i in range(3)]
    for c in ctx_out:
        c.start()
    need("mlp")
    mlp_sums = [scatter(mlp, 1, m) for m in range(2)]
    for c in mlp_sums:
        c.start()
    ring1.go(5)

    u_s, du_s, hist = scr["u"], scr["du"], scr["hist"]
    cols = pl.ds(pl.multiple_of(me * chan, chan), chan)
    need("nf", "rate", "cin", "cout", "start", "endg")
    for m in range(2):
        u_s[m] = nf[m, :, cols].astype(F32)
    decay = jnp.exp(-rate[...])
    root = jnp.sqrt(1.0 - decay * decay)
    drive = root * h["cin"][...]
    out_c = h["cout"][...]
    start, endg = h["start"], h["endg"]
    for m in range(2):
        hist[0, m] = start[m].astype(BF)

    def run(i, state):
        base = pl.multiple_of(i * 8, 8)
        state = list(state)
        for k in range(8):
            for m in range(2):
                state[m] = decay * state[m] + drive * u_s[m, pl.ds(base + k, 1), :]
                hist[base + k + 1, m] = state[m].astype(BF)
        return tuple(state)

    lax.fori_loop(0, block // 8, run, (start[0], start[1]))
    ctx_back = to_before(0, 4, dcs, dcr)
    total = cp[me].astype(F32)
    for i in range(3):
        ctx_out[i].wait_recv()
        total = total + cr[i].astype(F32)
    dcs[...] = total.astype(BF)

    @pl.when(s > 0)
    def _():
        ctx_back.start()

    for c in mlp_sums:
        c.turn()
    need("att")
    flat_att = h["att"][...].reshape(2 * block, chan)
    tile = 256

    def proj(j, c):
        cols = pl.ds(pl.multiple_of(j * tile, tile), tile)
        right = rr[:, :, cols].reshape(2 * block, tile)
        at = pl.multiple_of(3 * width + j * tile, tile)
        x2[pl.ds(at, tile), :] = dot(flat_att, right, TN).astype(BF)
        here = pl.ds(pl.multiple_of(j * tile, tile), tile)
        left = nf[:, :, here].reshape(2 * block, tile)
        x2[here, :] = dot(left, dq_s[...].reshape(2 * block, chan), TN).astype(BF)
        return c

    ring1.go(6)
    lax.fori_loop(0, width // tile, proj, 0)

    @pl.when(s < n - 1)
    def _():
        ctx_back.wait_recv()

    dy_s = scr["dy"]
    dy_s[...] = dcr[...].astype(F32)
    zero = jnp.zeros((NS, chan), F32)

    def early(i, grad):
        base = pl.multiple_of(CTX - 8 - i * 8, 8)
        grad = list(grad)
        for k in range(7, -1, -1):
            for m in range(2):
                grad[m] = decay * grad[m] + out_c * dy_s[m, pl.ds(base + k, 1), :]
        return tuple(grad)

    got = lax.fori_loop(0, CTX // 8, early, (zero, zero))
    reach = jnp.exp(-rate[...] * (block - CTX + 1.0))
    whole = jnp.exp(-rate[...] * block)
    pay = scr["pay"]
    for m in range(2):
        pay[m * NS : (m + 1) * NS] = reach * got[m] + whole * endg[m]
    pay[2 * NS : 2 * NS + 8] = keep[...]

    def spread(k):
        return remote(
            pay,
            gath.at[k],
            scr["send_g"].at[k],
            scr["recv_g"].at[k],
            seq=lax.rem(s + n - k, n),
        )

    for k in range(1, n):

        @pl.when(s >= k)
        def _():
            spread(k).start()

    ring1.go(7)
    for m in range(2):
        mixed_o[m] = (h1[m] + mlp_sums[m].end()).astype(BF)
    @pl.when(s < n - 1)
    def _():
        for i in range(4):
            to_before(0, i, dkp.at[i], rk.at[i]).wait_recv()
            to_before(1, i, dvp.at[i], rv.at[i]).wait_recv()

    dk_b, dv_b = scr["dkb"], scr["dvb"]
    for m in range(2):
        for head in range(chan // HD):
            lanes = slice(head * HD, (head + 1) * HD)
            i = m * (chan // HD) + head
            dk_b[m, :, lanes] = (dko[m, :, lanes] + rk[i].astype(F32)).astype(BF)
            dv_b[m, :, lanes] = (dvo[m, :, lanes] + rv[i].astype(F32)).astype(BF)

    need("ctx")
    ctx = h["ctx"]

    def kv_grads(i, c):
        at = pl.multiple_of(i * tile, tile)
        here = pl.ds(at, tile)
        left = nf[:, :, here].reshape(2 * block, tile)
        left_ctx = ctx[:, :, here].reshape(2 * CTX, tile)
        for j, (own, far) in enumerate(((dk_b, dkc), (dv_b, dvc))):
            value = dot(left, own[...].reshape(2 * block, chan), TN) + dot(
                left_ctx, far[...].reshape(2 * CTX, chan), TN
            )
            x2[pl.ds((j + 1) * width + at, tile), :] = value.astype(BF)
        return c

    lax.fori_loop(0, width // tile, kv_grads, 0)
    ring2.start()
    ring1.go(8)
    for k in range(1, n):

        @pl.when(s + k < n)
        def _():
            spread(k).wait_recv()

    def chain(i, carry):
        k = n - 1 - i
        got = gath[k]
        valid = s + k < n
        return tuple(
            jnp.where(
                valid,
                got[2 * NS + m : 2 * NS + m + 1]
                * (got[m * NS : (m + 1) * NS] + whole * carry[m]),
                carry[m],
            )
            for m in range(2)
        )

    carry = lax.fori_loop(0, n - 1, chain, (zero, zero))
    grads0 = tuple(endg[m] + carry[m] for m in range(2))

    def back_late(i, val):
        hold, d_drive, d_decay, d_out = list(val[0:2]), val[2], val[3], val[4]
        low_row = pl.multiple_of(CTX - 8 - i * 8, 8)
        base = pl.multiple_of(block - 8 - i * 8, 8)
        for k in range(7, -1, -1):
            for m in range(2):
                dy = dy_s[m, pl.ds(low_row + k, 1), :]
                grad = hold[m] + out_c * dy
                du_s[m, pl.ds(base + k, 1), :] = jnp.sum(drive * grad, axis=0, keepdims=True)
                d_drive = d_drive + grad * u_s[m, pl.ds(base + k, 1), :]
                d_decay = d_decay + grad * hist[base + k, m].astype(F32)
                d_out = d_out + dy * hist[base + k + 1, m].astype(F32)
                hold[m] = decay * grad
        return hold[0], hold[1], d_drive, d_decay, d_out

    val = lax.fori_loop(0, CTX // 8, back_late, (grads0[0], grads0[1], zero, zero, zero))

    def back_early(i, val):
        hold, d_drive, d_decay = list(val[0:2]), val[2], val[3]
        base = pl.multiple_of(block - CTX - 8 - i * 8, 8)
        for k in range(7, -1, -1):
            for m in range(2):
                grad = hold[m]
                du_s[m, pl.ds(base + k, 1), :] = jnp.sum(drive * grad, axis=0, keepdims=True)
                d_drive = d_drive + grad * u_s[m, pl.ds(base + k, 1), :]
                d_decay = d_decay + grad * hist[base + k, m].astype(F32)
                hold[m] = decay * grad
        return hold[0], hold[1], d_drive, d_decay

    _, _, d_drive, d_decay = lax.fori_loop(0, (block - CTX) // 8, back_early, val[0:4])
    x3[0:NS] = (-decay * (d_decay - d_drive * h["cin"][...] * decay / root)).astype(BF)
    x3[NS : 2 * NS] = (d_drive * root).astype(BF)
    x3[2 * NS : 3 * NS] = val[4].astype(BF)
    ring3.start()
    ring1.go(9)
    ring2.go(1)
    part_s = scr["part"]

    def normed_part(i, c):
        m, part = i // 2, lax.rem(i, 2)
        here = pl.ds(pl.multiple_of(part * half, half), half)
        part_s[...] = (
            dot(dq_s[m, here, :], wq[...], NT)
            + dot(dk_b[m, here, :], wk[...], NT)
            + dot(dv_b[m, here, :], wv[...], NT)
        )
        part_s[:, cols] += du_s[m, here, :]
        mlp[m, here, :] = part_s[...].astype(BF)
        return c

    finals = [scatter(mlp, 0, m) for m in range(2)]
    for m in range(2):
        lax.fori_loop(2 * m, 2 * m + 2, normed_part, 0)
        finals[m].start()
    for c in finals:
        c.turn()
    ring1.go(10)
    ring2.go(2)
    ring3.go(1)
    need("tok", "gain")
    gain_grad = jnp.zeros((1, width), F32)
    for m in range(2):
        back, one = rms_back(tok[m].astype(F32), h["gain"][...], finals[m].end())
        tg_o[m] = dh1[m] + back
        gain_grad = gain_grad + one
    gp, gr, gs, gg = scr["gp"], scr["gr"], scr["gs"], scr["gg"]
    for j in range(4):
        gp[j, 0:1] = gain_grad[:, j * chan : (j + 1) * chan]
        gp[j, 1:2] = mid_grad[:, j * chan : (j + 1) * chan]
        gp[j, 2:8] = jnp.zeros((6, chan), F32)
    gains = [to_peer(i, gp.at[peers[i]], gr.at[i], 1) for i in range(3)]
    for c in gains:
        c.start()
    ring1.go(11)
    ring2.go(3)
    ring3.go(2)
    total = gp[me]
    for i in range(3):
        gains[i].wait_recv()
        total = total + gr[i]
    gs[...] = total

    def gain_out(k):
        return remote(
            gs,
            gg.at[k],
            scr["gain_s"].at[k],
            scr["gain_r"].at[k],
            seq=lax.rem(s + k, n),
        )

    for k in range(1, n):
        gain_out(k).start()
    for t in range(12, 15):
        ring1.go(t)
        ring2.go(t - 8)
        ring3.go(t - 9)
    store1 = pltpu.make_async_copy(x1, sum1_o, scr["store"].at[0])
    store1.start()
    for t in range(7, 15):
        ring2.go(t)
        ring3.go(min(t - 1 + (t - 7) // 3, 14))
    store2 = pltpu.make_async_copy(x2, sum2_o, scr["store"].at[1])
    store2.start()
    ring3.go(14)
    small_o[0 : 3 * NS] = x3[0 : 3 * NS].astype(F32)
    for k in range(1, n):
        gain_out(k).wait_recv()
        total = total + gg[k]
    small_o[3 * NS : 3 * NS + 8] = total
    for k in range(1, n):
        gain_out(k).wait_send()
    for c in gains + ctx_out:
        c.wait_send()
    for g in gathers:
        g.finish()

    @pl.when(s > 0)
    def _():
        ctx_back.wait_send()
        for i in range(4):
            to_before(0, i, dkp.at[i], rk.at[i]).wait_send()
            to_before(1, i, dvp.at[i], rv.at[i]).wait_send()

    for k in range(1, n):

        @pl.when(s >= k)
        def _():
            spread(k).wait_send()

    ring1.drain()
    ring2.drain()
    ring3.drain()
    store1.wait()
    store2.wait()


def ring_rows(n, used, subs):
    return -(-used // (2 * n * subs * 16)) * 16


def last(*args):
    n = lax.axis_size("seq")
    by = dict(zip(LAST_IN, args))
    micro, block, width = by["nf"].shape
    rows = block // 4
    chan = by["rate"].shape[1]
    keys = by["k"].shape[1]
    sds = jax.ShapeDtypeStruct
    dma = pltpu.SemaphoreType.DMA
    step1 = ring_rows(n, by["ffn"].shape[0], 2)
    step2 = ring_rows(n, 4 * width, 2)
    step3 = ring_rows(n, 3 * NS, 1)
    x1 = VM((4 * n * step1, chan), BF)
    x2 = VM((4 * n * step2, chan), BF)
    scratch = dict(
        x1=x1,
        r1=VM((2, n - 1, 2, step1, chan), BF),
        x2=x2,
        r2=VM((2, n - 1, 2, step2, chan), BF),
        x3=VM((2 * n * step3, chan), BF),
        r3=VM((2, n - 1, 1, step3, chan), BF),
        s1s=dma((2, 2, 2 * n - 2)),
        s1r=dma((2, 2, 2 * n - 2)),
        s2s=dma((2, 2, 2 * n - 2)),
        s2r=dma((2, 2, 2 * n - 2)),
        s3s=dma((2, 1, 2 * n - 2)),
        s3r=dma((2, 1, 2 * n - 2)),
        fetch=dma((len(LAST_IN),)),
        rr=VM((micro, block, width), BF),
        da=VM((micro, block, chan), BF),
        rs=dma((2, 3)),
        rrv=dma((2, 3)),
        rk=VM((4, block, HD), BF),
        rv=VM((4, block, HD), BF),
        dkp=VM((4, block, HD), BF),
        dvp=VM((4, block, HD), BF),
        ak=VM((keys, HD), F32),
        av=VM((keys, HD), F32),
        dq=VM((micro, block, chan), BF),
        dko=VM((micro, block, chan), F32),
        dvo=VM((micro, block, chan), F32),
        dkb=VM((micro, block, chan), BF),
        dvb=VM((micro, block, chan), BF),
        dkc=VM((micro, CTX, chan), BF),
        dvc=VM((micro, CTX, chan), BF),
        cp=VM((4, micro, CTX, chan), BF),
        cr=VM((3, micro, CTX, chan), BF),
        dcs=VM((micro, CTX, chan), BF),
        dcr=VM((micro, CTX, chan), BF),
        dy=VM((micro, CTX, chan), F32),
        u=VM((micro, block, chan), F32),
        du=VM((micro, block, chan), F32),
        hist=VM((block + 1, micro, NS, chan), BF),
        pay=VM((2 * NS + 8, chan), F32),
        gath=VM((n, 2 * NS + 8, chan), F32),
        part=VM((block // 2, width), F32),
        dh1=VM((micro, rows, width), F32),
        over=VM((4, rows, width), BF),
        into=VM((4, 3, rows, width), BF),
        ss=dma((4, 3)),
        sr=dma((4, 3)),
        gp=VM((4, 8, chan), F32),
        gr=VM((3, 8, chan), F32),
        gs=VM((8, chan), F32),
        gg=VM((n, 8, chan), F32),
        gain_s=dma((n,)),
        gain_r=dma((n,)),
        send_k=dma((2, 5)),
        recv_k=dma((2, 5)),
        send_c=dma((2, 3)),
        recv_c=dma((2, 3)),
        send_g=dma((n,)),
        recv_g=dma((n,)),
        store=dma((2,)),
    )
    outs = (
        sds((micro, rows, width), BF),
        sds((micro, rows, width), F32),
        sds(x1.shape, BF),
        sds(x2.shape, BF),
        sds((3 * NS + 8, chan), F32),
    )
    return launch(
        functools.partial(last_kernel, n),
        LAST_IN,
        args,
        outs,
        [True, True, False, False, True],
        scratch,
        2,
        62,
        "last",
        ("ffn",),
    )


def finish_kernel(*refs):
    half = len(refs) // 2
    for src, dst in zip(refs[:half], refs[half:]):
        dst[...] = src[...].astype(dst.dtype)


def finish(sum1, sum2, mixed, tokens_grad, end, width, units, chan):
    across = width // chan
    sds = jax.ShapeDtypeStruct
    down_at = units * width // chan
    tall = lambda high, at: pl.BlockSpec((high, chan), lambda j: (at // high + j, 0))
    wide = lambda high: pl.BlockSpec((high, chan), lambda j: (0, j))
    col = pl.BlockSpec((chan, chan), lambda j: (j, 0))
    micro, rows, _ = mixed.shape
    same = [
        pl.BlockSpec((micro, rows // across, width), lambda j: (0, j, 0)),
        pl.BlockSpec((micro, rows // across, width), lambda j: (0, j, 0)),
        pl.BlockSpec(end.shape, lambda j: (0, 0, 0)),
    ]
    return pl.pallas_call(
        finish_kernel,
        grid=(across,),
        out_shape=(
            sds((width, units), F32),
            sds((units, width), F32),
            sds((chan, width), F32),
            sds((width, chan), F32),
            sds((width, chan), F32),
            sds((width, chan), F32),
            sds(mixed.shape, BF),
            sds(tokens_grad.shape, F32),
            sds(end.shape, F32),
        ),
        in_specs=[
            tall(width, 0),
            tall(units, down_at),
            tall(chan, 3 * width),
            tall(chan, 0),
            tall(chan, width),
            tall(chan, 2 * width),
        ]
        + same,
        out_specs=tuple([wide(width), wide(units), wide(chan), col, col, col] + same),
        compiler_params=pltpu.CompilerParams(vmem_limit_bytes=62 << 20),
        name="finish",
    )(sum1, sum1, sum2, sum2, sum2, sum2, mixed, tokens_grad, end)


def body(
    tokens,
    out_grad,
    norm_gain,
    w_query,
    w_key,
    w_value,
    w_out,
    mid_gain,
    w_up,
    w_down,
    ssm_rate,
    ssm_in,
    ssm_out,
    resets,
    init_state,
    states_grad,
):
    micro, rows, width = tokens.shape
    chan = ssm_rate.shape[0]
    units = w_up.shape[1]
    rate, cin, cout = ssm_rate.T, ssm_in.T, ssm_out.T
    flags = resets[:, 0]
    keep = jnp.zeros((8, chan), F32).at[0:micro].set((1.0 - flags.astype(F32))[:, None])
    init = jnp.swapaxes(init_state, 1, 2)
    endg = jnp.swapaxes(states_grad[:, 0], 1, 2)
    gain_row, mid_row = norm_gain[None], mid_gain[None]
    nf, og, q, k, v, ctx, start, end = front(
        tokens, gain_row, w_query, w_key, w_value, rate, cin, cout, keep, init, out_grad
    )
    mlp, h1, dm, ffn, att, lse = middle(
        q, k, v, keep, w_out, tokens, mid_row, w_up, w_down, og
    )
    mixed, tokens_grad, sum1, sum2, small = last(
        *(q, k, v, lse, att, w_out, nf, ctx, w_query, w_key, w_value, rate, cin, cout),
        *(start, keep, endg, mlp, h1, dm, out_grad, mid_row, tokens, gain_row, ffn),
    )
    up_g, down_g, proj_g, query_g, key_g, value_g, mixed, tokens_grad, end = finish(
        sum1, sum2, mixed, tokens_grad, end, width, units, chan
    )
    rate_g, in_g, out_g = (small[i * NS : (i + 1) * NS].T for i in range(3))
    return (
        mixed,
        jnp.swapaxes(end, 1, 2)[:, None],
        tokens_grad,
        small[3 * NS],
        query_g,
        key_g,
        value_g,
        proj_g,
        small[3 * NS + 1],
        up_g,
        down_g,
        rate_g,
        in_g,
        out_g,
    )


def solution(mesh):
    return jax.shard_map(
        body,
        mesh=mesh,
        in_specs=(
            P(None, ("seq", "tp"), None),
            P(None, ("seq", "tp"), None),
            P(),
            P(None, "tp"),
            P(None, "tp"),
            P(None, "tp"),
            P("tp", None),
            P(),
            P(None, "tp"),
            P("tp", None),
            P("tp", None),
            P("tp", None),
            P("tp", None),
            P(None, "seq"),
            P(None, "tp", None),
            P(None, "seq", "tp", None),
        ),
        out_specs=(
            P(None, ("seq", "tp"), None),
            P(None, "seq", "tp", None),
            P(None, ("seq", "tp"), None),
            P("tp"),
            P(None, "tp"),
            P(None, "tp"),
            P(None, "tp"),
            P("tp", None),
            P("tp"),
            P(None, "tp"),
            P("tp", None),
            P("tp", None),
            P("tp", None),
            P("tp", None),
        ),
        check_vma=False,
    )
```

```python
import functools

import jax
import jax.numpy as jnp
from jax import lax
from jax.experimental import pallas as pl
from jax.experimental.pallas import tpu as pltpu
from jax.sharding import PartitionSpec as P

HD = 128
NS = 16
CTX = 128


eps_norm = 1e-06
neg_big = -1e30
MESH = pl.DeviceIdType.MESH
VM = pltpu.VMEM
BF = jnp.bfloat16
F32 = jnp.float32
NT = (((1,), (1,)), ((), ()))
TN = (((0,), (0,)), ((), ()))
NN = (((1,), (0,)), ((), ()))


def dot(left, right, dims=NN):
    return lax.dot_general(left, right, dims, preferred_element_type=F32)


def vmem_specs(count):
    return [pl.BlockSpec(memory_space=VM)] * count


def tp_peers():
    me = lax.axis_index("tp")
    mate = me + 1 - 2 * lax.rem(me, 2)
    return me, mate, lax.rem(me + 2, 4), lax.rem(mate + 2, 4)


def remote(src, dst, send, recv, **where):
    return pltpu.make_async_remote_copy(
        src_ref=src,
        dst_ref=dst,
        send_sem=send,
        recv_sem=recv,
        device_id=where,
        device_id_type=MESH,
    )


def greet(n, with_seq):
    s = lax.axis_index("seq")
    barrier = pltpu.get_barrier_semaphore()
    for peer in tp_peers()[1:]:
        pl.semaphore_signal(barrier, inc=1, device_id={"tp": peer}, device_id_type=MESH)
    if with_seq:
        for k in range(1, n):
            pl.semaphore_signal(
                barrier, inc=1, device_id={"seq": lax.rem(s + k, n)}, device_id_type=MESH
            )


def greeted(n, with_seq):
    pl.semaphore_wait(pltpu.get_barrier_semaphore(), 3 + (n - 1 if with_seq else 0))


class Fetch:
    def __init__(self, names, refs, held, sems):
        self.copies = {
            name: pltpu.make_async_copy(ref, held[name], sems.at[i])
            for i, (name, ref) in enumerate(zip(names, refs))
        }
        self.ready = set()
        for c in self.copies.values():
            c.start()

    def need(self, *wanted):
        for name in wanted:
            if name not in self.ready:
                self.copies[name].wait()
                self.ready.add(name)


class Gather:
    def __init__(self, ref, send, recv):
        rows = ref.shape[0] // 4
        me, mate, across, _ = tp_peers()

        def give(slot, quarter, peer):
            part = ref.at[pl.ds(pl.multiple_of(quarter * rows, rows), rows), :]
            return remote(part, part, send.at[slot], recv.at[slot], tp=peer)

        self.cross = give(1, me, across)
        self.side = give(0, me, mate)
        self.relay = give(2, across, mate)

    def start(self):
        self.cross.start()
        self.side.start()

    def near(self):
        self.side.wait_recv()

    def pass_on(self):
        self.cross.wait_recv()
        self.relay.start()

    def far(self):
        self.relay.wait_recv()

    def finish(self):
        for c in (self.side, self.cross, self.relay):
            c.wait_send()


class Scatter:
    def __init__(self, ref, over, into, send, recv):
        self.ref, self.over, self.into = ref, over, into
        self.rows = ref.shape[0] // 4
        self.me, self.mate, self.across, self.diag = tp_peers()
        self.hop = [
            remote(self.quarter(self.diag), into.at[0], send.at[0], recv.at[0], tp=self.mate),
            remote(self.quarter(self.mate), into.at[1], send.at[1], recv.at[1], tp=self.mate),
            remote(over, into.at[2], send.at[2], recv.at[2], tp=self.across),
        ]

    def span(self, quarter):
        return pl.ds(pl.multiple_of(quarter * self.rows, self.rows), self.rows)

    def quarter(self, quarter):
        return self.ref.at[self.span(quarter), :]

    def start(self):
        self.hop[0].start()
        self.hop[1].start()

    def turn(self):
        self.hop[0].wait_recv()
        mine = self.ref[self.span(self.across), :].astype(F32)
        self.over[...] = (mine + self.into[0].astype(F32)).astype(BF)
        self.hop[2].start()

    def end(self):
        self.hop[1].wait_recv()
        value = self.ref[self.span(self.me), :].astype(F32) + self.into[1].astype(F32)
        self.hop[2].wait_recv()
        value = value + self.into[2].astype(F32)
        for c in self.hop:
            c.wait_send()
        return value


FORWARD_IN = (
    "tok",
    "gain",
    "wk",
    "wv",
    "wq",
    "rate",
    "cin",
    "cout",
    "keep",
    "init",
    "ogm",
    "w_out",
    "mid",
    "w_up",
    "w_down",
)


class Save:
    def __init__(self, sems):
        self.sems, self.copies = sems, []

    def __call__(self, src, dst):
        self.copies.append(pltpu.make_async_copy(src, dst, self.sems.at[len(self.copies)]))
        self.copies[-1].start()

    def finish(self):
        for c in self.copies:
            c.wait()


def forward_kernel(n, refs_in, outs, held, scr):
    s = lax.axis_index("seq")
    me, mate, across, diag = tp_peers()
    og = scr["og"]
    own_rows = og.shape[1] // 4
    own = pl.ds(pl.multiple_of(me * own_rows, own_rows), own_rows)
    held = dict(held, ogm=og.at[:, own, :])
    fetch = Fetch(FORWARD_IN, refs_in, held, scr["fetch"])
    nf_d, q_d, k_d, v_d, ctx_d, start_o, end_o = outs[:7]
    nf, q_o, k_o, v_o, ctx_o = (scr[x] for x in ("nf", "q", "k", "v", "ctxa"))
    save = Save(scr["save"])
    grad_gathers = [Gather(og.at[m], scr["os"].at[m], scr["or"].at[m]) for m in range(2)]
    tok, rate, keep, init = (held[x] for x in ("tok", "rate", "keep", "init"))
    wq, wk, wv = held["wq"], held["wk"], held["wv"]
    u_s, gath, pay, y_s, ctx_s = (scr[x] for x in ("u", "gath", "pay", "y", "ctx"))
    block = nf.shape[1]
    rows = block // 4
    chan = rate.shape[1]
    gath[...] = jnp.zeros_like(gath)

    @pl.when(s == 0)
    def _():
        k_o[:, 0 : CTX + block, :] = jnp.zeros((2, CTX + block, chan), BF)
        v_o[:, 0 : CTX + block, :] = jnp.zeros((2, CTX + block, chan), BF)
        ctx_o[...] = jnp.zeros_like(ctx_o)

    greet(n, True)

    def span(quarter):
        return pl.ds(pl.multiple_of(quarter * rows, rows), rows)

    def lanes(part):
        return pl.ds(pl.multiple_of(part * chan, chan), chan)

    fetch.need("tok", "gain")
    x = tok[...].astype(F32).reshape(2 * rows, -1)
    normed = x * lax.rsqrt(jnp.mean(x * x, axis=-1, keepdims=True) + eps_norm) * held["gain"][...]
    nf[:, span(me), :] = normed.astype(BF).reshape(2, rows, -1)
    greeted(n, True)

    def give(slot, quarter, peer, part=None):
        cols = slice(None) if part is None else lanes(part)
        ref = nf.at[:, span(quarter), cols]
        return remote(ref, ref, scr["ts"].at[slot], scr["tr"].at[slot], tp=peer)

    cross = [give(1 + i, me, across, part) for i, part in enumerate((across, diag, me, mate))]
    relay = [give(5 + i, across, mate, part) for i, part in enumerate((me, mate, across, diag))]
    side = give(0, me, mate)
    for c in cross:
        c.start()
    side.start()

    def pass_kv(slot, src, half):
        high = 2 * rows
        part = pl.ds(pl.multiple_of(CTX + half * high, rows), high)
        own = pl.ds(pl.multiple_of(CTX + block + half * high, rows), high)
        return remote(
            src.at[:, own, :],
            src.at[:, part, :],
            scr["kvs"].at[slot],
            scr["kvr"].at[slot],
            seq=lax.rem(s + 1, n),
        )

    def qkv(order, half):
        high = 2 * rows
        here = pl.ds(pl.multiple_of(half * high, high), high)
        part = nf[:, here, :].reshape(2 * high, -1)
        own = pl.ds(pl.multiple_of(CTX + block + half * high, rows), high)
        k_o[:, own, :] = dot(part, wk[...]).astype(BF).reshape(2, high, chan)
        v_o[:, own, :] = dot(part, wv[...]).astype(BF).reshape(2, high, chan)

        @pl.when(s < n - 1)
        def _():
            pass_kv(2 * order, k_o, half).start()
            if order == 0:
                pass_kv(1, v_o, half).start()

        q_o[:, here, :] = dot(part, wq[...]).astype(BF).reshape(2, high, chan)

    near = me // 2
    side.wait_recv()
    fetch.need("wk", "wv", "wq")
    qkv(0, near)
    cross[0].wait_recv()
    cross[1].wait_recv()
    relay[1].start()
    relay[0].start()
    relay[1].wait_recv()
    fetch.need("rate", "cin", "cout", "keep", "init")
    cols = lanes(me)
    for m in range(2):
        u_s[m] = nf[m, :, cols].astype(F32)
    decay = jnp.exp(-rate[...])
    drive = jnp.sqrt(1.0 - decay * decay) * held["cin"][...]

    def run(i, state):
        base = pl.multiple_of(i * 8, 8)
        state = list(state)
        for k in range(8):
            for m in range(2):
                state[m] = decay * state[m] + drive * u_s[m, pl.ds(base + k, 1), :]
        return tuple(state)

    zero = jnp.zeros((NS, chan), F32)
    late = lax.fori_loop(0, (block - CTX) // 8, run, (zero, zero))
    last_state = lax.fori_loop((block - CTX) // 8, block // 8, run, late)
    pay[0:NS] = last_state[0]
    pay[NS : 2 * NS] = last_state[1]
    pay[2 * NS : 2 * NS + 8] = keep[...]

    def spread(k):
        return remote(
            pay, gath.at[k], scr["gs"].at[k], scr["gr"].at[k], seq=lax.rem(s + k, n)
        )

    for k in range(1, n):

        @pl.when(s + k < n)
        def _():
            spread(k).start()

    for i in (2, 3):
        cross[i].wait_recv()
        relay[i].start()
    for i in (0, 2, 3):
        relay[i].wait_recv()
    fetch.need("ogm")
    for g in grad_gathers:
        g.start()
    qkv(1, 1 - near)
    save(nf, nf_d)
    save(q_o, q_d)

    whole = jnp.exp(-rate[...] * block)
    for k in range(1, n):

        @pl.when(s >= k)
        def _():
            spread(k).wait_recv()

    def entry(begin_keep, end, b):
        return tuple(jnp.where(b == 0, init[m], begin_keep[m] * end[m]) for m in range(2))

    def chain(b, end):
        k = jnp.maximum(s - b, 0)
        got = gath[k]
        begin = entry((got[2 * NS : 2 * NS + 1], got[2 * NS + 1 : 2 * NS + 2]), end, b)
        new = tuple(got[m * NS : (m + 1) * NS] + whole * begin[m] for m in range(2))
        return tuple(jnp.where(b < s, new[m], end[m]) for m in range(2))

    end = lax.fori_loop(0, n - 1, chain, (zero, zero))
    begin = entry((keep[0:1, :], keep[1:2, :]), end, s)
    toward = jnp.exp(-rate[...] * (block - CTX))
    state = tuple(late[m] + toward * begin[m] for m in range(2))
    out_c = held["cout"][...]

    def run_out(i, state):
        base = pl.multiple_of(block - CTX + i * 8, 8)
        row = pl.multiple_of(i * 8, 8)
        state = list(state)
        for k in range(8):
            for m in range(2):
                state[m] = decay * state[m] + drive * u_s[m, pl.ds(base + k, 1), :]
                y_s[m, pl.ds(row + k, 1), :] = jnp.sum(out_c * state[m], axis=0, keepdims=True)
        return tuple(state)

    state = lax.fori_loop(0, CTX // 8, run_out, state)
    ctx_s[...] = y_s[...].astype(BF)
    down = remote(
        ctx_s, ctx_o.at[:, :, cols], scr["cs"].at[0], scr["cr"].at[0], seq=lax.rem(s + 1, n)
    )

    @pl.when(s < n - 1)
    def _():
        down.start()
        pass_kv(3, v_o, 1 - near).start()

    for m in range(2):
        start_o[m] = begin[m]
        end_o[m] = last_state[m] + whole * begin[m]
    for g in grad_gathers:
        g.near()
        g.pass_on()

    @pl.when(s > 0)
    def _():
        down.wait_recv()
        mine = ctx_o.at[:, :, cols]
        shares = [
            remote(mine, mine, scr["cs"].at[1 + i], scr["cr"].at[1 + i], tp=peer)
            for i, peer in enumerate((across, diag, mate))
        ]
        for c in shares:
            c.start()
        for c in shares:
            c.wait_recv()
        flat = ctx_o[...].reshape(2 * CTX, -1)
        k_o[:, 0:CTX, :] = dot(flat, wk[...]).astype(BF).reshape(2, CTX, chan)
        v_o[:, 0:CTX, :] = dot(flat, wv[...]).astype(BF).reshape(2, CTX, chan)
        for order, half in enumerate((near, 1 - near)):
            pass_kv(2 * order, k_o, half).wait_recv()
            pass_kv(2 * order + 1, v_o, half).wait_recv()
        for c in shares:
            c.wait_send()

    save(k_o, k_d)
    save(v_o, v_d)
    save(ctx_o, ctx_d)
    forward_middle(fetch, held, scr, outs[7:], save, q_o, k_o, v_o, og, grad_gathers)

    @pl.when(s < n - 1)
    def _():
        down.wait_send()
        for order, half in enumerate((near, 1 - near)):
            pass_kv(2 * order, k_o, half).wait_send()
            pass_kv(2 * order + 1, v_o, half).wait_send()

    for k in range(1, n):

        @pl.when(s + k < n)
        def _():
            spread(k).wait_send()

    for c in [side] + cross + relay:
        c.wait_send()
    for g in grad_gathers:
        g.finish()
    save.finish()


def launch(
    body, names, args, outs, out_vmem, scratch, collective_id, limit, name, placed=()
):
    keys = list(scratch)
    count = len(names)
    plain = [name for name in names if name not in placed]

    def kernel(*refs):
        refs_in, refs = refs[:count], refs[count:]
        outs_r, refs = refs[: len(outs)], refs[len(outs) :]
        held, refs = dict(zip(plain, refs)), refs[len(plain) :]
        body(refs_in, outs_r, held, dict(zip(keys, refs)))

    scratch = dict(scratch)
    return pl.pallas_call(
        kernel,
        out_shape=tuple(outs),
        in_specs=[pl.BlockSpec(memory_space=pl.ANY)] * count,
        out_specs=tuple(
            pl.BlockSpec(memory_space=VM if in_vmem else pl.ANY) for in_vmem in out_vmem
        ),
        scratch_shapes=[VM(a.shape, a.dtype) for x, a in zip(names, args) if x in plain]
        + list(scratch.values()),
        compiler_params=pltpu.CompilerParams(
            collective_id=collective_id, has_side_effects=True, vmem_limit_bytes=limit << 20
        ),
        name=name,
    )(*args)


def rms_back(x, gain, grad):
    inv = lax.rsqrt(jnp.mean(x * x, axis=-1, keepdims=True) + eps_norm)
    unit = x * inv
    scaled = grad * gain
    gain_grad = jnp.sum(grad * unit, axis=0, keepdims=True)
    return inv * (scaled - unit * jnp.mean(scaled * unit, axis=-1, keepdims=True)), gain_grad


def forward_middle(fetch, held, scr, outs, save, q, k, v, og, grad_gathers):
    nm, pm, dm, hid, dpre = (scr[x] for x in ("nm", "pm", "dm", "hid", "dpre"))
    mlp_o, h1_o, ffn_o, att, lse = (scr[x] for x in ("mlp", "h1", "ffn", "att", "lse"))
    keep, w_out, tok, gain, w_up, w_down = (
        held[x] for x in ("keep", "w_out", "tok", "mid", "w_up", "w_down")
    )
    me = tp_peers()[0]
    near = me // 2
    block = q.shape[1]
    rows = block // 4
    width = w_out.shape[1]
    tile = 256
    panels = w_up.shape[1] // tile
    own = pl.ds(pl.multiple_of(me * rows, rows), rows)
    edge0 = k.shape[1] - block
    half = block // 2
    row_ids = lax.broadcasted_iota(jnp.int32, (half, half), 0)
    col_ids = lax.broadcasted_iota(jnp.int32, (half, half), 1)
    scale = HD ** (-0.5)

    def attend(m):
        def one(head, c):
            lanes = pl.ds(pl.multiple_of(head * HD, HD), HD)
            shut = (keep[m : m + 1, 0:half] - 1.0) * -neg_big
            for part in range(2):
                mine = slice(part * half, (part + 1) * half)
                edge = edge0 + part * half
                sc = dot(k[m, 0 : edge + half, lanes], q[m, mine, lanes], NT) * scale
                pieces = [sc[:edge0] + shut]
                if part:
                    pieces.append(sc[edge0:edge])
                pieces.append(jnp.where(row_ids <= col_ids, sc[edge:], neg_big))
                sc = jnp.concatenate(pieces, axis=0)
                top = jnp.max(sc, axis=0, keepdims=True)
                expo = jnp.exp(sc - top)
                total = jnp.sum(expo, axis=0, keepdims=True)
                weights = (expo * (1.0 / total)).astype(BF)
                res = dot(v[m, 0 : edge + half, lanes], weights, TN)
                att[m, mine, lanes] = res.T.astype(BF)
                lse[m, head, :, mine] = top + jnp.log(total)
            return c

        lax.fori_loop(0, q.shape[2] // HD, one, 0)

    def scatter(kind, m, ref):
        at = 2 * kind + m
        return Scatter(
            ref.at[m], scr["over"].at[at], scr["into"].at[at], scr["ss"].at[at], scr["sr"].at[at]
        )

    mlp_d, h1_d, dm_d, ffn_d, att_d, lse_d = outs
    sums1 = [scatter(0, m, pm) for m in range(2)]
    gathers = [Gather(nm.at[m], scr["mgs"].at[m], scr["mgr"].at[m]) for m in range(2)]

    def project(m):
        def one(j, c):
            cols = pl.ds(pl.multiple_of(j * tile, tile), tile)
            pm[m, :, cols] = dot(att[m], w_out[:, cols]).astype(BF)
            return c

        lax.fori_loop(0, width // tile, one, 0)

    def residual(m):
        h1 = tok[m].astype(F32) + sums1[m].end()
        h1_o[m] = h1
        inv = lax.rsqrt(jnp.mean(h1 * h1, axis=-1, keepdims=True) + eps_norm)
        nm[m, own, :] = (h1 * inv * gain[...]).astype(BF)
        gathers[m].start()

    def feed(m, part):
        here = pl.ds(pl.multiple_of(part * half, half), half)
        flat = pl.ds(pl.multiple_of(m * block + part * half, half), half)

        def panel(j, c):
            cols = pl.ds(pl.multiple_of(j * tile, tile), tile)
            pre = dot(nm[m, here, :], w_up[:, cols])
            sq = pre * pre
            t = jnp.tanh((0.7978845608028654 * pre) * (1.0 + 0.044715 * sq))
            hid[flat, cols] = (0.5 * pre * (1.0 + t)).astype(BF)
            slope = 0.5 * (1.0 + t) + (0.3989422804014327 * pre) * (1.0 - t * t) * (
                1.0 + 0.134145 * sq
            )
            dpre[flat, cols] = (slope * dot(og[m, here, :], w_down[cols, :], NT)).astype(BF)
            return c

        lax.fori_loop(0, panels, panel, 0)

        def back(j, c):
            cols = pl.ds(pl.multiple_of(j * tile, tile), tile)
            dm[m, here, cols] = dot(dpre[flat, :], w_up[cols, :], NT).astype(BF)
            return c

        lax.fori_loop(0, width // tile, back, 0)

    def lower(m, part):
        here = pl.ds(pl.multiple_of(part * half, half), half)
        flat = pl.ds(pl.multiple_of(m * block + part * half, half), half)

        def one(j, c):
            cols = pl.ds(pl.multiple_of(j * tile, tile), tile)
            mlp_o[m, here, cols] = dot(hid[flat, :], w_down[:, cols]).astype(BF)
            return c

        lax.fori_loop(0, width // tile, one, 0)

    attend(0)
    fetch.need("w_out")
    project(0)
    sums1[0].start()
    sums1[0].turn()
    attend(1)
    project(1)
    save(att, att_d)
    save(lse, lse_d)
    sums1[1].start()
    sums1[1].turn()
    fetch.need("mid")
    residual(0)
    fetch.need("w_up", "w_down")
    for g in grad_gathers:
        g.far()
    gathers[0].near()
    feed(0, near)
    residual(1)
    save(h1_o, h1_d)
    gathers[0].pass_on()
    gathers[1].near()
    feed(1, near)
    lower(0, near)
    lower(1, near)
    gathers[0].far()
    feed(0, 1 - near)
    save(dm.at[0], dm_d.at[0])
    gathers[1].pass_on()
    gathers[1].far()
    feed(1, 1 - near)
    save(dm.at[1], dm_d.at[1])

    def down_sum(i, c):
        left = hid[:, pl.ds(pl.multiple_of(i * tile, tile), tile)]
        for j in range(width // tile):
            right = og[:, :, j * tile : (j + 1) * tile].reshape(2 * block, tile)
            at = pl.multiple_of((width // tile + j) * panels * tile + i * tile, tile)
            ffn_o[pl.ds(at, tile), :] = dot(left, right, TN).astype(BF)
        return c

    def up_sum(i, c):
        left = nm[:, :, pl.ds(pl.multiple_of(i * tile, tile), tile)].reshape(2 * block, tile)
        for j in range(panels):
            at = pl.multiple_of(j * width + i * tile, tile)
            ffn_o[pl.ds(at, tile), :] = dot(
                left, dpre[:, j * tile : (j + 1) * tile], TN
            ).astype(BF)
        return c

    high = panels * tile * (width // tile)
    lax.fori_loop(0, panels, down_sum, 0)
    save(ffn_o.at[high : 2 * high], ffn_d.at[high : 2 * high])
    lower(0, 1 - near)
    lower(1, 1 - near)
    save(mlp_o, mlp_d)
    lax.fori_loop(0, width // tile, up_sum, 0)
    save(ffn_o.at[0:high], ffn_d.at[0:high])
    for m in range(2):
        gathers[m].finish()


def forward(*args):
    n = lax.axis_size("seq")
    by = dict(zip(FORWARD_IN, args))
    micro, rows, width = by["tok"].shape
    block = 4 * rows
    chan = by["rate"].shape[1]
    units = by["w_up"].shape[1]
    keys = CTX + 2 * block
    sds = jax.ShapeDtypeStruct
    dma = pltpu.SemaphoreType.DMA
    results = dict(
        nf=sds((micro, block, width), BF),
        q=sds((micro, block, chan), BF),
        k=sds((micro, keys, chan), BF),
        v=sds((micro, keys, chan), BF),
        ctxa=sds((micro, CTX, width), BF),
        start=sds((micro, NS, chan), F32),
        end=sds((micro, NS, chan), F32),
        mlp=sds((micro, block, width), BF),
        h1=sds((micro, rows, width), F32),
        dm=sds((micro, block, width), BF),
        ffn=sds((2 * units * width // 256, 256), BF),
        att=sds((micro, block, chan), BF),
        lse=sds((micro, chan // HD, 1, block), F32),
    )
    in_vmem = ("start", "end")
    scratch = {x: VM(a.shape, a.dtype) for x, a in results.items() if x not in in_vmem}
    scratch.update(
        og=VM((micro, block, width), BF),
        fetch=dma((len(FORWARD_IN),)),
        save=dma((16,)),
        os=dma((2, 3)),
        u=VM((micro, block, chan), F32),
        gath=VM((n, 2 * NS + 8, chan), F32),
        pay=VM((2 * NS + 8, chan), F32),
        y=VM((micro, CTX, chan), F32),
        ctx=VM((micro, CTX, chan), BF),
        ts=dma((9,)),
        tr=dma((9,)),
        kvs=dma((4,)),
        kvr=dma((4,)),
        gs=dma((n,)),
        gr=dma((n,)),
        cs=dma((4,)),
        cr=dma((4,)),
        nm=VM((micro, block, width), BF),
        pm=VM((micro, block, width), BF),
        hid=VM((micro * block, units), BF),
        dpre=VM((micro * block, units), BF),
        over=VM((2, rows, width), BF),
        into=VM((2, 3, rows, width), BF),
        ss=dma((2, 3)),
        sr=dma((2, 3)),
        mgs=dma((2, 3)),
        mgr=dma((2, 3)),
    )
    scratch["or"] = dma((2, 3))
    return launch(
        functools.partial(forward_kernel, n),
        FORWARD_IN,
        args,
        tuple(results.values()),
        [x in in_vmem for x in results],
        scratch,
        0,
        62,
        "forward",
        ("ogm",),
    )


class Ring:
    def __init__(self, n, x, recv, send_sem, recv_sem):
        self.n, self.x, self.recv = n, x, recv
        self.send_sem, self.recv_sem = send_sem, recv_sem
        self.subs, self.rows = recv.shape[2], recv.shape[3]
        s = lax.axis_index("seq")
        half = n // 2
        self.r = jnp.where(lax.rem(s, 2) == 0, s // 2, n - 1 - s // 2)

        def dev(q):
            q = lax.rem(q + n, n)
            return jnp.where(q < half, 2 * q, 2 * (n - 1 - q) + 1)

        self.target = (dev(self.r + 1), dev(self.r - 1))
        self.done = 0
        self.total = 2 * n - 2

    def chunk(self, d, b, off):
        sign = (1, -1)[d]
        c = lax.rem(self.r + sign * off + 2 * self.n, self.n)
        at = ((d * self.n + c) * self.subs + b) * self.rows
        return pl.ds(pl.multiple_of(at, self.rows), self.rows)

    def copy(self, d, b, src, dst, k):
        return pltpu.make_async_remote_copy(
            src_ref=src,
            dst_ref=dst,
            send_sem=self.send_sem.at[d, b, k],
            recv_sem=self.recv_sem.at[d, b, k],
            device_id={"seq": self.target[d]},
            device_id_type=MESH,
        )

    def first(self, d, b):
        return self.copy(d, b, self.x.at[self.chunk(d, b, 0)], self.recv.at[d, 0, b], 0)

    def sums(self, d, b, k):
        prior = jnp.maximum(k - 1, 0)
        return self.copy(d, b, self.recv.at[d, prior, b], self.recv.at[d, k, b], k)

    def alls(self, d, b, k):
        ref = self.x.at[self.chunk(d, b, 1 - k)]
        return self.copy(d, b, ref, ref, self.n - 1 + k)

    def each(self):
        return [(d, b) for b in range(self.subs) for d in range(2)]

    def add(self, d, b, k):
        mine = self.x[self.chunk(d, b, -k - 1)]
        return (self.recv[d, k, b].astype(F32) + mine.astype(F32)).astype(BF)

    def start(self):
        for d, b in self.each():
            self.first(d, b).start()

    def tick(self, t):
        n = self.n

        def leave():
            for d, b in self.each():
                self.first(d, b).wait_send()

        def sum_step():
            for d, b in self.each():
                self.sums(d, b, t).wait_recv()
                self.recv[d, t, b] = self.add(d, b, t)
                self.sums(d, b, t + 1).start()

        def turn():
            for d, b in self.each():
                self.sums(d, b, n - 2).wait_recv()
                self.x[self.chunk(d, b, 1)] = self.add(d, b, n - 2)
                self.alls(d, b, 0).start()

        def all_step():
            k = t - (n - 1)
            for d, b in self.each():
                self.alls(d, b, k).wait_recv()
                self.alls(d, b, k + 1).start()

        def close():
            for d, b in self.each():
                self.alls(d, b, n - 2).wait_recv()

        steps = (
            (t == 0, leave),
            (t < n - 2, sum_step),
            (t == n - 2, turn),
            ((t > n - 2) & (t < 2 * n - 3), all_step),
            (t == 2 * n - 3, close),
        )
        for when, step in steps:
            if isinstance(t, int):
                if when:
                    step()
            else:
                pl.when(when)(step)

    def go(self, fourteenths):
        upto = min(-(-fourteenths * self.total // 14), self.total)
        if upto - self.done == 1:
            self.tick(self.done)
        elif upto > self.done:

            def one(t, c):
                self.tick(t)
                return c

            lax.fori_loop(self.done, upto, one, 0)
        self.done = max(upto, self.done)

    def drain(self):
        def more(k, c):
            for d, b in self.each():
                self.sums(d, b, k + 1).wait_send()
                self.alls(d, b, k).wait_send()
            return c

        lax.fori_loop(0, self.n - 2, more, 0)
        for d, b in self.each():
            self.alls(d, b, self.n - 2).wait_send()


LAST_IN = (
    "q",
    "k",
    "v",
    "lse",
    "att",
    "w_out",
    "nf",
    "ctx",
    "wq",
    "wk",
    "wv",
    "rate",
    "cin",
    "cout",
    "start",
    "keep",
    "endg",
    "mlp",
    "h1",
    "dm",
    "ogm",
    "mid",
    "tok",
    "gain",
    "ffn",
)


def last_kernel(n, refs_in, outs, h, scr):
    x1, x2, x3 = scr["x1"], scr["x2"], scr["x3"]
    ffn_rows = refs_in[LAST_IN.index("ffn")].shape[0]
    h = dict(h, ffn=x1.at[0:ffn_rows])
    fetch = Fetch(LAST_IN, refs_in, h, scr["fetch"])
    need = fetch.need
    mixed_o, tg_o, sum1_o, sum2_o, small_o = outs
    s = lax.axis_index("seq")
    me, mate, across, diag = tp_peers()
    peers = (mate, across, diag)
    nf, rate, tok = h["nf"], h["rate"], h["tok"]
    block = nf.shape[1]
    rows = block // 4
    width = nf.shape[2]
    chan = rate.shape[1]
    rk, rv, gath, dcr = scr["rk"], scr["rv"], scr["gath"], scr["dcr"]
    gath[...] = jnp.zeros_like(gath)
    if x1.shape[0] > ffn_rows:
        x1[ffn_rows:] = jnp.zeros((x1.shape[0] - ffn_rows, chan), BF)
    used2 = 4 * width
    if x2.shape[0] > used2:
        x2[used2:] = jnp.zeros((x2.shape[0] - used2, chan), BF)
    x3[...] = jnp.zeros_like(x3)

    @pl.when(s == n - 1)
    def _():
        rk[...] = jnp.zeros_like(rk)
        rv[...] = jnp.zeros_like(rv)
        dcr[...] = jnp.zeros_like(dcr)

    greet(n, True)
    before = lax.rem(s + n - 1, n)
    own = pl.ds(pl.multiple_of(me * rows, rows), rows)

    def to_before(sem, slot, src, dst):
        return remote(
            src, dst, scr["send_k"].at[sem, slot], scr["recv_k"].at[sem, slot], seq=before
        )

    ring1 = Ring(n, x1, scr["r1"], scr["s1s"], scr["s1r"])
    ring2 = Ring(n, x2, scr["r2"], scr["s2s"], scr["s2r"])
    ring3 = Ring(n, x3, scr["r3"], scr["s3s"], scr["s3r"])
    rr, da, dh1, mlp, h1 = scr["rr"], scr["da"], scr["dh1"], h["mlp"], h["h1"]

    def scatter(ref, at, m):
        at = 2 * at + m
        return Scatter(
            ref.at[m], scr["over"].at[at], scr["into"].at[at], scr["ss"].at[at], scr["sr"].at[at]
        )

    mid_sums = [scatter(h["dm"], 0, m) for m in range(2)]
    gathers = [Gather(rr.at[m], scr["rs"].at[m], scr["rrv"].at[m]) for m in range(2)]
    need("dm")
    greeted(n, True)
    for c in mid_sums:
        c.start()
    need("ffn")
    ring1.start()
    for c in mid_sums:
        c.turn()
    need("h1", "ogm", "mid")
    mid_grad = jnp.zeros((1, width), F32)
    for m in range(2):
        back, one = rms_back(h1[m], h["mid"][...], mid_sums[m].end())
        mid_grad = mid_grad + one
        dh1[m] = h["ogm"][m].astype(F32) + back
        rr[m, own, :] = dh1[m].astype(BF)
        gathers[m].start()
        ring1.go(m + 1)
    need("w_out", "q", "k", "v", "lse", "keep")

    q, k, v, lse, keep, w_out = (h[name] for name in ("q", "k", "v", "lse", "keep", "w_out"))
    edge0 = k.shape[1] - block
    half = block // 2
    row_ids = lax.broadcasted_iota(jnp.int32, (half, half), 0)
    col_ids = lax.broadcasted_iota(jnp.int32, (half, half), 1)
    scale = HD ** (-0.5)
    dq_s, dko, dvo, dkc, dvc = (scr[x] for x in ("dq", "dko", "dvo", "dkc", "dvc"))
    dkp, dvp, ak, av = (scr[x] for x in ("dkp", "dvp", "ak", "av"))

    def attend_one(m, head):
        i = 2 * m + head
        lanes = pl.ds(pl.multiple_of(head * HD, HD), HD)
        shut = (keep[pl.ds(m, 1), 0:half] - 1.0) * -neg_big
        for part in (1, 0):
            mine = slice(part * half, (part + 1) * half)
            edge = edge0 + part * half
            qq = q[m, mine, lanes]
            kk = k[m, 0 : edge + half, lanes]
            dd = da[m, mine, lanes]
            sc = dot(kk, qq, NT) * scale
            pieces = [sc[:edge0] + shut]
            if part:
                pieces.append(sc[edge0:edge])
            pieces.append(jnp.where(row_ids <= col_ids, sc[edge:], neg_big))
            sc = jnp.concatenate(pieces, axis=0)
            probs = jnp.exp(sc - lse[m, head, :, mine])
            dp = dot(v[m, 0 : edge + half, lanes], dd, NT)
            spread_sum = jnp.sum(probs * dp, axis=0, keepdims=True)
            ds = (probs * (dp - spread_sum)).astype(BF)
            dq_s[m, mine, lanes] = (dot(kk, ds, TN) * scale).T.astype(BF)
            dk = dot(ds, qq) * scale
            dv = dot(probs.astype(BF), dd)
            if part:
                ak[...] = dk
                av[...] = dv
            else:
                ak[0 : edge + half] += dk
                av[0 : edge + half] += dv
        for acc, far, prev, own in ((ak, dkc, dkp, dko), (av, dvc, dvp, dvo)):
            far[m, :, lanes] = acc[0:CTX].astype(BF)
            prev[i] = acc[CTX:edge0].astype(BF)
            own[m, :, lanes] = acc[edge0:]

        @pl.when(s > 0)
        def _():
            to_before(0, i, dkp.at[i], rk.at[i]).start()
            to_before(1, i, dvp.at[i], rv.at[i]).start()

    def stream_back(m, c):
        g = Gather(rr.at[m], scr["rs"].at[m], scr["rrv"].at[m])
        g.near()
        g.pass_on()
        g.far()
        ring1.tick(m + ring1.done)
        da[m] = dot(rr[m], w_out[...], NT).astype(BF)

        def heads(head, c):
            attend_one(m, head)
            return c

        lax.fori_loop(0, chan // HD, heads, 0)
        return c

    lax.fori_loop(0, 2, stream_back, 0)
    ring1.done += 2

    cp, cr, dcs = scr["cp"], scr["cr"], scr["dcs"]
    wq, wk, wv = h["wq"], h["wk"], h["wv"]
    need("wq", "wk", "wv")
    ctx_part = dot(dkc[...].reshape(2 * CTX, chan), wk[...], NT) + dot(
        dvc[...].reshape(2 * CTX, chan), wv[...], NT
    )
    for j in range(4):
        cp[j] = ctx_part[:, j * chan : (j + 1) * chan].astype(BF).reshape(2, CTX, chan)

    def to_peer(i, src, dst, kind):
        return remote(
            src, dst, scr["send_c"].at[kind, i], scr["recv_c"].at[kind, i], tp=peers[i]
        )

    ctx_out = [to_peer(i, cp.at[peers[i]], cr.at[i], 0) for i in range(3)]
    for c in ctx_out:
        c.start()
    need("mlp")
    mlp_sums = [scatter(mlp, 1, m) for m in range(2)]
    for c in mlp_sums:
        c.start()
    ring1.go(5)

    u_s, du_s, hist = scr["u"], scr["du"], scr["hist"]
    cols = pl.ds(pl.multiple_of(me * chan, chan), chan)
    need("nf", "rate", "cin", "cout", "start", "endg")
    for m in range(2):
        u_s[m] = nf[m, :, cols].astype(F32)
    decay = jnp.exp(-rate[...])
    root = jnp.sqrt(1.0 - decay * decay)
    drive = root * h["cin"][...]
    out_c = h["cout"][...]
    start, endg = h["start"], h["endg"]
    for m in range(2):
        hist[0, m] = start[m].astype(BF)

    def run(i, state):
        base = pl.multiple_of(i * 8, 8)
        state = list(state)
        for k in range(8):
            for m in range(2):
                state[m] = decay * state[m] + drive * u_s[m, pl.ds(base + k, 1), :]
                hist[base + k + 1, m] = state[m].astype(BF)
        return tuple(state)

    lax.fori_loop(0, block // 8, run, (start[0], start[1]))
    ctx_back = to_before(0, 4, dcs, dcr)
    total = cp[me].astype(F32)
    for i in range(3):
        ctx_out[i].wait_recv()
        total = total + cr[i].astype(F32)
    dcs[...] = total.astype(BF)

    @pl.when(s > 0)
    def _():
        ctx_back.start()

    for c in mlp_sums:
        c.turn()
    need("att")
    flat_att = h["att"][...].reshape(2 * block, chan)
    tile = 256

    def proj(j, c):
        cols = pl.ds(pl.multiple_of(j * tile, tile), tile)
        right = rr[:, :, cols].reshape(2 * block, tile)
        at = pl.multiple_of(3 * width + j * tile, tile)
        x2[pl.ds(at, tile), :] = dot(flat_att, right, TN).astype(BF)
        here = pl.ds(pl.multiple_of(j * tile, tile), tile)
        left = nf[:, :, here].reshape(2 * block, tile)
        x2[here, :] = dot(left, dq_s[...].reshape(2 * block, chan), TN).astype(BF)
        return c

    ring1.go(6)
    lax.fori_loop(0, width // tile, proj, 0)

    @pl.when(s < n - 1)
    def _():
        ctx_back.wait_recv()

    dy_s = scr["dy"]
    dy_s[...] = dcr[...].astype(F32)
    zero = jnp.zeros((NS, chan), F32)

    def early(i, grad):
        base = pl.multiple_of(CTX - 8 - i * 8, 8)
        grad = list(grad)
        for k in range(7, -1, -1):
            for m in range(2):
                grad[m] = decay * grad[m] + out_c * dy_s[m, pl.ds(base + k, 1), :]
        return tuple(grad)

    got = lax.fori_loop(0, CTX // 8, early, (zero, zero))
    reach = jnp.exp(-rate[...] * (block - CTX + 1.0))
    whole = jnp.exp(-rate[...] * block)
    pay = scr["pay"]
    for m in range(2):
        pay[m * NS : (m + 1) * NS] = reach * got[m] + whole * endg[m]
    pay[2 * NS : 2 * NS + 8] = keep[...]

    def spread(k):
        return remote(
            pay,
            gath.at[k],
            scr["send_g"].at[k],
            scr["recv_g"].at[k],
            seq=lax.rem(s + n - k, n),
        )

    for k in range(1, n):

        @pl.when(s >= k)
        def _():
            spread(k).start()

    ring1.go(7)
    for m in range(2):
        mixed_o[m] = (h1[m] + mlp_sums[m].end()).astype(BF)
    @pl.when(s < n - 1)
    def _():
        for i in range(4):
            to_before(0, i, dkp.at[i], rk.at[i]).wait_recv()
            to_before(1, i, dvp.at[i], rv.at[i]).wait_recv()

    dk_b, dv_b = scr["dkb"], scr["dvb"]
    for m in range(2):
        for head in range(chan // HD):
            lanes = slice(head * HD, (head + 1) * HD)
            i = m * (chan // HD) + head
            dk_b[m, :, lanes] = (dko[m, :, lanes] + rk[i].astype(F32)).astype(BF)
            dv_b[m, :, lanes] = (dvo[m, :, lanes] + rv[i].astype(F32)).astype(BF)

    need("ctx")
    ctx = h["ctx"]

    def kv_grads(i, c):
        at = pl.multiple_of(i * tile, tile)
        here = pl.ds(at, tile)
        left = nf[:, :, here].reshape(2 * block, tile)
        left_ctx = ctx[:, :, here].reshape(2 * CTX, tile)
        for j, (own, far) in enumerate(((dk_b, dkc), (dv_b, dvc))):
            value = dot(left, own[...].reshape(2 * block, chan), TN) + dot(
                left_ctx, far[...].reshape(2 * CTX, chan), TN
            )
            x2[pl.ds((j + 1) * width + at, tile), :] = value.astype(BF)
        return c

    lax.fori_loop(0, width // tile, kv_grads, 0)
    ring2.start()
    ring1.go(8)
    for k in range(1, n):

        @pl.when(s + k < n)
        def _():
            spread(k).wait_recv()

    def chain(i, carry):
        k = n - 1 - i
        got = gath[k]
        valid = s + k < n
        return tuple(
            jnp.where(
                valid,
                got[2 * NS + m : 2 * NS + m + 1]
                * (got[m * NS : (m + 1) * NS] + whole * carry[m]),
                carry[m],
            )
            for m in range(2)
        )

    carry = lax.fori_loop(0, n - 1, chain, (zero, zero))
    grads0 = tuple(endg[m] + carry[m] for m in range(2))

    def back_late(i, val):
        hold, d_drive, d_decay, d_out = list(val[0:2]), val[2], val[3], val[4]
        low_row = pl.multiple_of(CTX - 8 - i * 8, 8)
        base = pl.multiple_of(block - 8 - i * 8, 8)
        for k in range(7, -1, -1):
            for m in range(2):
                dy = dy_s[m, pl.ds(low_row + k, 1), :]
                grad = hold[m] + out_c * dy
                du_s[m, pl.ds(base + k, 1), :] = jnp.sum(drive * grad, axis=0, keepdims=True)
                d_drive = d_drive + grad * u_s[m, pl.ds(base + k, 1), :]
                d_decay = d_decay + grad * hist[base + k, m].astype(F32)
                d_out = d_out + dy * hist[base + k + 1, m].astype(F32)
                hold[m] = decay * grad
        return hold[0], hold[1], d_drive, d_decay, d_out

    val = lax.fori_loop(0, CTX // 8, back_late, (grads0[0], grads0[1], zero, zero, zero))

    def back_early(i, val):
        hold, d_drive, d_decay = list(val[0:2]), val[2], val[3]
        base = pl.multiple_of(block - CTX - 8 - i * 8, 8)
        for k in range(7, -1, -1):
            for m in range(2):
                grad = hold[m]
                du_s[m, pl.ds(base + k, 1), :] = jnp.sum(drive * grad, axis=0, keepdims=True)
                d_drive = d_drive + grad * u_s[m, pl.ds(base + k, 1), :]
                d_decay = d_decay + grad * hist[base + k, m].astype(F32)
                hold[m] = decay * grad
        return hold[0], hold[1], d_drive, d_decay

    _, _, d_drive, d_decay = lax.fori_loop(0, (block - CTX) // 8, back_early, val[0:4])
    x3[0:NS] = (-decay * (d_decay - d_drive * h["cin"][...] * decay / root)).astype(BF)
    x3[NS : 2 * NS] = (d_drive * root).astype(BF)
    x3[2 * NS : 3 * NS] = val[4].astype(BF)
    ring3.start()
    ring1.go(9)
    ring2.go(1)
    part_s = scr["part"]

    def normed_part(i, c):
        m, part = i // 2, lax.rem(i, 2)
        here = pl.ds(pl.multiple_of(part * half, half), half)
        part_s[...] = (
            dot(dq_s[m, here, :], wq[...], NT)
            + dot(dk_b[m, here, :], wk[...], NT)
            + dot(dv_b[m, here, :], wv[...], NT)
        )
        part_s[:, cols] += du_s[m, here, :]
        mlp[m, here, :] = part_s[...].astype(BF)
        return c

    finals = [scatter(mlp, 0, m) for m in range(2)]
    for m in range(2):
        lax.fori_loop(2 * m, 2 * m + 2, normed_part, 0)
        finals[m].start()
    for c in finals:
        c.turn()
    ring1.go(10)
    ring2.go(2)
    ring3.go(1)
    need("tok", "gain")
    gain_grad = jnp.zeros((1, width), F32)
    for m in range(2):
        back, one = rms_back(tok[m].astype(F32), h["gain"][...], finals[m].end())
        tg_o[m] = dh1[m] + back
        gain_grad = gain_grad + one
    gp, gr, gs, gg = scr["gp"], scr["gr"], scr["gs"], scr["gg"]
    for j in range(4):
        gp[j, 0:1] = gain_grad[:, j * chan : (j + 1) * chan]
        gp[j, 1:2] = mid_grad[:, j * chan : (j + 1) * chan]
        gp[j, 2:8] = jnp.zeros((6, chan), F32)
    gains = [to_peer(i, gp.at[peers[i]], gr.at[i], 1) for i in range(3)]
    for c in gains:
        c.start()
    ring1.go(11)
    ring2.go(3)
    ring3.go(2)
    total = gp[me]
    for i in range(3):
        gains[i].wait_recv()
        total = total + gr[i]
    gs[...] = total

    def gain_out(k):
        return remote(
            gs,
            gg.at[k],
            scr["gain_s"].at[k],
            scr["gain_r"].at[k],
            seq=lax.rem(s + k, n),
        )

    for k in range(1, n):
        gain_out(k).start()
    for t in range(12, 15):
        ring1.go(t)
        ring2.go(t - 8)
        ring3.go(t - 9)
    store1 = pltpu.make_async_copy(x1, sum1_o, scr["store"].at[0])
    store1.start()
    for t in range(7, 15):
        ring2.go(t)
        ring3.go(min(t - 1 + (t - 7) // 3, 14))
    store2 = pltpu.make_async_copy(x2, sum2_o, scr["store"].at[1])
    store2.start()
    ring3.go(14)
    small_o[0 : 3 * NS] = x3[0 : 3 * NS].astype(F32)
    for k in range(1, n):
        gain_out(k).wait_recv()
        total = total + gg[k]
    small_o[3 * NS : 3 * NS + 8] = total
    for k in range(1, n):
        gain_out(k).wait_send()
    for c in gains + ctx_out:
        c.wait_send()
    for g in gathers:
        g.finish()

    @pl.when(s > 0)
    def _():
        ctx_back.wait_send()
        for i in range(4):
            to_before(0, i, dkp.at[i], rk.at[i]).wait_send()
            to_before(1, i, dvp.at[i], rv.at[i]).wait_send()

    for k in range(1, n):

        @pl.when(s >= k)
        def _():
            spread(k).wait_send()

    ring1.drain()
    ring2.drain()
    ring3.drain()
    store1.wait()
    store2.wait()


def ring_rows(n, used, subs):
    return -(-used // (2 * n * subs * 16)) * 16


def last(*args):
    n = lax.axis_size("seq")
    by = dict(zip(LAST_IN, args))
    micro, block, width = by["nf"].shape
    rows = block // 4
    chan = by["rate"].shape[1]
    keys = by["k"].shape[1]
    sds = jax.ShapeDtypeStruct
    dma = pltpu.SemaphoreType.DMA
    step1 = ring_rows(n, by["ffn"].shape[0], 2)
    step2 = ring_rows(n, 4 * width, 2)
    step3 = ring_rows(n, 3 * NS, 1)
    x1 = VM((4 * n * step1, chan), BF)
    x2 = VM((4 * n * step2, chan), BF)
    scratch = dict(
        x1=x1,
        r1=VM((2, n - 1, 2, step1, chan), BF),
        x2=x2,
        r2=VM((2, n - 1, 2, step2, chan), BF),
        x3=VM((2 * n * step3, chan), BF),
        r3=VM((2, n - 1, 1, step3, chan), BF),
        s1s=dma((2, 2, 2 * n - 2)),
        s1r=dma((2, 2, 2 * n - 2)),
        s2s=dma((2, 2, 2 * n - 2)),
        s2r=dma((2, 2, 2 * n - 2)),
        s3s=dma((2, 1, 2 * n - 2)),
        s3r=dma((2, 1, 2 * n - 2)),
        fetch=dma((len(LAST_IN),)),
        rr=VM((micro, block, width), BF),
        da=VM((micro, block, chan), BF),
        rs=dma((2, 3)),
        rrv=dma((2, 3)),
        rk=VM((4, block, HD), BF),
        rv=VM((4, block, HD), BF),
        dkp=VM((4, block, HD), BF),
        dvp=VM((4, block, HD), BF),
        ak=VM((keys, HD), F32),
        av=VM((keys, HD), F32),
        dq=VM((micro, block, chan), BF),
        dko=VM((micro, block, chan), F32),
        dvo=VM((micro, block, chan), F32),
        dkb=VM((micro, block, chan), BF),
        dvb=VM((micro, block, chan), BF),
        dkc=VM((micro, CTX, chan), BF),
        dvc=VM((micro, CTX, chan), BF),
        cp=VM((4, micro, CTX, chan), BF),
        cr=VM((3, micro, CTX, chan), BF),
        dcs=VM((micro, CTX, chan), BF),
        dcr=VM((micro, CTX, chan), BF),
        dy=VM((micro, CTX, chan), F32),
        u=VM((micro, block, chan), F32),
        du=VM((micro, block, chan), F32),
        hist=VM((block + 1, micro, NS, chan), BF),
        pay=VM((2 * NS + 8, chan), F32),
        gath=VM((n, 2 * NS + 8, chan), F32),
        part=VM((block // 2, width), F32),
        dh1=VM((micro, rows, width), F32),
        over=VM((4, rows, width), BF),
        into=VM((4, 3, rows, width), BF),
        ss=dma((4, 3)),
        sr=dma((4, 3)),
        gp=VM((4, 8, chan), F32),
        gr=VM((3, 8, chan), F32),
        gs=VM((8, chan), F32),
        gg=VM((n, 8, chan), F32),
        gain_s=dma((n,)),
        gain_r=dma((n,)),
        send_k=dma((2, 5)),
        recv_k=dma((2, 5)),
        send_c=dma((2, 3)),
        recv_c=dma((2, 3)),
        send_g=dma((n,)),
        recv_g=dma((n,)),
        store=dma((2,)),
    )
    outs = (
        sds((micro, rows, width), BF),
        sds((micro, rows, width), F32),
        sds(x1.shape, BF),
        sds(x2.shape, BF),
        sds((3 * NS + 8, chan), F32),
    )
    return launch(
        functools.partial(last_kernel, n),
        LAST_IN,
        args,
        outs,
        [True, True, False, False, True],
        scratch,
        2,
        62,
        "last",
        ("ffn",),
    )


def finish_kernel(*refs):
    half = len(refs) // 2
    for src, dst in zip(refs[:half], refs[half:]):
        dst[...] = src[...].astype(dst.dtype)


def finish(sum1, sum2, mixed, tokens_grad, end, small, width, units, chan):
    across = width // chan
    sds = jax.ShapeDtypeStruct
    down_at = units * width // chan
    tall = lambda high, at: pl.BlockSpec((high, chan), lambda j: (at // high + j, 0))
    wide = lambda high: pl.BlockSpec((high, chan), lambda j: (0, j))
    col = pl.BlockSpec((chan, chan), lambda j: (j, 0))
    micro, rows, _ = mixed.shape
    same = [
        pl.BlockSpec((micro, rows // across, width), lambda j: (0, j, 0)),
        pl.BlockSpec((micro, rows // across, width), lambda j: (0, j, 0)),
        pl.BlockSpec(end.shape, lambda j: (0, 0, 0)),
    ]
    states = [pl.BlockSpec((NS, chan), lambda j, i=i: (i, 0)) for i in range(3)]
    alone = [pl.BlockSpec((NS, chan), lambda j: (0, 0))] * 3
    return pl.pallas_call(
        finish_kernel,
        grid=(across,),
        out_shape=(
            sds((width, units), F32),
            sds((units, width), F32),
            sds((chan, width), F32),
            sds((width, chan), F32),
            sds((width, chan), F32),
            sds((width, chan), F32),
            sds(mixed.shape, BF),
            sds(tokens_grad.shape, F32),
            sds(end.shape, F32),
            sds((NS, chan), F32),
            sds((NS, chan), F32),
            sds((NS, chan), F32),
        ),
        in_specs=[
            tall(width, 0),
            tall(units, down_at),
            tall(chan, 3 * width),
            tall(chan, 0),
            tall(chan, width),
            tall(chan, 2 * width),
        ]
        + same
        + states,
        out_specs=tuple([wide(width), wide(units), wide(chan), col, col, col] + same + alone),
        compiler_params=pltpu.CompilerParams(vmem_limit_bytes=62 << 20),
        name="finish",
    )(sum1, sum1, sum2, sum2, sum2, sum2, mixed, tokens_grad, end, small, small, small)


def body(
    tokens,
    out_grad,
    norm_gain,
    w_query,
    w_key,
    w_value,
    w_out,
    mid_gain,
    w_up,
    w_down,
    ssm_rate,
    ssm_in,
    ssm_out,
    resets,
    init_state,
    states_grad,
):
    micro, rows, width = tokens.shape
    chan = ssm_rate.shape[0]
    units = w_up.shape[1]
    rate, cin, cout = ssm_rate.T, ssm_in.T, ssm_out.T
    flags = resets[:, 0]
    keep = jnp.pad(1.0 - flags.astype(F32), (0, 8 - micro))
    keep = jnp.broadcast_to(keep[:, None], (8, chan))
    init = jnp.swapaxes(init_state, 1, 2)
    endg = jnp.swapaxes(states_grad[:, 0], 1, 2)
    gain_row, mid_row = norm_gain[None], mid_gain[None]
    nf, q, k, v, ctx, start, end, mlp, h1, dm, ffn, att, lse = forward(
        *(tokens, gain_row, w_key, w_value, w_query, rate, cin, cout, keep, init, out_grad),
        *(w_out, mid_row, w_up, w_down),
    )
    mixed, tokens_grad, sum1, sum2, small = last(
        *(q, k, v, lse, att, w_out, nf, ctx, w_query, w_key, w_value, rate, cin, cout),
        *(start, keep, endg, mlp, h1, dm, out_grad, mid_row, tokens, gain_row, ffn),
    )
    done = finish(sum1, sum2, mixed, tokens_grad, end, small, width, units, chan)
    up_g, down_g, proj_g, query_g, key_g, value_g, mixed, tokens_grad, end = done[:9]
    rate_g, in_g, out_g = (part.T for part in done[9:])
    return (
        mixed,
        jnp.swapaxes(end, 1, 2)[:, None],
        tokens_grad,
        small[3 * NS],
        query_g,
        key_g,
        value_g,
        proj_g,
        small[3 * NS + 1],
        up_g,
        down_g,
        rate_g,
        in_g,
        out_g,
    )


def solution(mesh):
    return jax.shard_map(
        body,
        mesh=mesh,
        in_specs=(
            P(None, ("seq", "tp"), None),
            P(None, ("seq", "tp"), None),
            P(),
            P(None, "tp"),
            P(None, "tp"),
            P(None, "tp"),
            P("tp", None),
            P(),
            P(None, "tp"),
            P("tp", None),
            P("tp", None),
            P("tp", None),
            P("tp", None),
            P(None, "seq"),
            P(None, "tp", None),
            P(None, "seq", "tp", None),
        ),
        out_specs=(
            P(None, ("seq", "tp"), None),
            P(None, "seq", "tp", None),
            P(None, ("seq", "tp"), None),
            P("tp"),
            P(None, "tp"),
            P(None, "tp"),
            P(None, "tp"),
            P("tp", None),
            P("tp"),
            P(None, "tp"),
            P("tp", None),
            P("tp", None),
            P("tp", None),
            P("tp", None),
        ),
        check_vma=False,
    )
```

```python
import functools

import jax
import jax.numpy as jnp
from jax import lax
from jax.experimental import pallas as pl
from jax.experimental.pallas import tpu as pltpu
from jax.sharding import PartitionSpec as P

HD = 128
NS = 16
CTX = 128


eps_norm = 1e-06
neg_big = -1e30
MESH = pl.DeviceIdType.MESH
VM = pltpu.VMEM
BF = jnp.bfloat16
F32 = jnp.float32
NT = (((1,), (1,)), ((), ()))
TN = (((0,), (0,)), ((), ()))
NN = (((1,), (0,)), ((), ()))


def dot(left, right, dims=NN):
    return lax.dot_general(left, right, dims, preferred_element_type=F32)


def vmem_specs(count):
    return [pl.BlockSpec(memory_space=VM)] * count


def tp_peers():
    me = lax.axis_index("tp")
    mate = me + 1 - 2 * lax.rem(me, 2)
    return me, mate, lax.rem(me + 2, 4), lax.rem(mate + 2, 4)


def flag_rows(keep):
    rest = jnp.zeros((NS - keep.shape[0], keep.shape[1]), F32)
    return jnp.concatenate([keep[...], rest], axis=0).astype(BF)


def remote(src, dst, send, recv, **where):
    return pltpu.make_async_remote_copy(
        src_ref=src,
        dst_ref=dst,
        send_sem=send,
        recv_sem=recv,
        device_id=where,
        device_id_type=MESH,
    )


def greet(n, with_seq):
    s = lax.axis_index("seq")
    barrier = pltpu.get_barrier_semaphore()
    for peer in tp_peers()[1:]:
        pl.semaphore_signal(barrier, inc=1, device_id={"tp": peer}, device_id_type=MESH)
    if with_seq:
        for k in range(1, n):
            pl.semaphore_signal(
                barrier, inc=1, device_id={"seq": lax.rem(s + k, n)}, device_id_type=MESH
            )


def greeted(n, with_seq):
    pl.semaphore_wait(pltpu.get_barrier_semaphore(), 3 + (n - 1 if with_seq else 0))


class Fetch:
    def __init__(self, names, refs, held, sems):
        self.copies = {
            name: pltpu.make_async_copy(ref, held[name], sems.at[i])
            for i, (name, ref) in enumerate(zip(names, refs))
        }
        self.ready = set()
        for c in self.copies.values():
            c.start()

    def need(self, *wanted):
        for name in wanted:
            if name not in self.ready:
                self.copies[name].wait()
                self.ready.add(name)


class Gather:
    def __init__(self, ref, send, recv):
        rows = ref.shape[0] // 4
        me, mate, across, _ = tp_peers()

        def give(slot, quarter, peer):
            part = ref.at[pl.ds(pl.multiple_of(quarter * rows, rows), rows), :]
            return remote(part, part, send.at[slot], recv.at[slot], tp=peer)

        self.cross = give(1, me, across)
        self.side = give(0, me, mate)
        self.relay = give(2, across, mate)

    def start(self):
        self.cross.start()
        self.side.start()

    def near(self):
        self.side.wait_recv()

    def pass_on(self):
        self.cross.wait_recv()
        self.relay.start()

    def far(self):
        self.relay.wait_recv()

    def finish(self):
        for c in (self.side, self.cross, self.relay):
            c.wait_send()


class Scatter:
    def __init__(self, ref, over, into, send, recv):
        self.ref, self.over, self.into = ref, over, into
        self.rows = ref.shape[0] // 4
        self.me, self.mate, self.across, self.diag = tp_peers()
        self.hop = [
            remote(self.quarter(self.diag), into.at[0], send.at[0], recv.at[0], tp=self.mate),
            remote(self.quarter(self.mate), into.at[1], send.at[1], recv.at[1], tp=self.mate),
            remote(over, into.at[2], send.at[2], recv.at[2], tp=self.across),
        ]

    def span(self, quarter):
        return pl.ds(pl.multiple_of(quarter * self.rows, self.rows), self.rows)

    def quarter(self, quarter):
        return self.ref.at[self.span(quarter), :]

    def start(self):
        self.hop[0].start()
        self.hop[1].start()

    def turn(self):
        self.hop[0].wait_recv()
        mine = self.ref[self.span(self.across), :].astype(F32)
        self.over[...] = (mine + self.into[0].astype(F32)).astype(BF)
        self.hop[2].start()

    def end(self):
        self.hop[1].wait_recv()
        value = self.ref[self.span(self.me), :].astype(F32) + self.into[1].astype(F32)
        self.hop[2].wait_recv()
        value = value + self.into[2].astype(F32)
        for c in self.hop:
            c.wait_send()
        return value


FORWARD_IN = (
    "tok",
    "gain",
    "wk",
    "wv",
    "wq",
    "rate",
    "cin",
    "cout",
    "keep",
    "init",
    "ogm",
    "w_out",
    "mid",
    "w_up",
    "w_down",
)


class Save:
    def __init__(self, sems):
        self.sems, self.copies = sems, []

    def __call__(self, src, dst):
        self.copies.append(pltpu.make_async_copy(src, dst, self.sems.at[len(self.copies)]))
        self.copies[-1].start()

    def finish(self):
        for c in self.copies:
            c.wait()


def forward_kernel(n, refs_in, outs, held, scr):
    s = lax.axis_index("seq")
    me, mate, across, diag = tp_peers()
    og = scr["og"]
    own_rows = og.shape[1] // 4
    own = pl.ds(pl.multiple_of(me * own_rows, own_rows), own_rows)
    held = dict(held, ogm=og.at[:, own, :])
    fetch = Fetch(FORWARD_IN, refs_in, held, scr["fetch"])
    nf_d, q_d, k_d, v_d, ctx_d, start_o, end_o = outs[:7]
    nf, q_o, k_o, v_o, ctx_o = (scr[x] for x in ("nf", "q", "k", "v", "ctxa"))
    save = Save(scr["save"])
    grad_gathers = [Gather(og.at[m], scr["os"].at[m], scr["or"].at[m]) for m in range(2)]
    tok, rate, keep, init = (held[x] for x in ("tok", "rate", "keep", "init"))
    wq, wk, wv = held["wq"], held["wk"], held["wv"]
    u_s, gath, pay, y_s, ctx_s = (scr[x] for x in ("u", "gath", "pay", "y", "ctx"))
    block = nf.shape[1]
    rows = block // 4
    chan = rate.shape[1]
    gath[...] = jnp.zeros_like(gath)

    @pl.when(s == 0)
    def _():
        k_o[:, 0 : CTX + block, :] = jnp.zeros((2, CTX + block, chan), BF)
        v_o[:, 0 : CTX + block, :] = jnp.zeros((2, CTX + block, chan), BF)
        ctx_o[...] = jnp.zeros_like(ctx_o)

    greet(n, True)

    def span(quarter):
        return pl.ds(pl.multiple_of(quarter * rows, rows), rows)

    def lanes(part):
        return pl.ds(pl.multiple_of(part * chan, chan), chan)

    fetch.need("tok", "gain")
    x = tok[...].astype(F32).reshape(2 * rows, -1)
    normed = x * lax.rsqrt(jnp.mean(x * x, axis=-1, keepdims=True) + eps_norm) * held["gain"][...]
    nf[:, span(me), :] = normed.astype(BF).reshape(2, rows, -1)
    greeted(n, True)

    def give(slot, quarter, peer, part=None):
        cols = slice(None) if part is None else lanes(part)
        ref = nf.at[:, span(quarter), cols]
        return remote(ref, ref, scr["ts"].at[slot], scr["tr"].at[slot], tp=peer)

    cross = [give(1 + i, me, across, part) for i, part in enumerate((across, diag, me, mate))]
    relay = [give(5 + i, across, mate, part) for i, part in enumerate((me, mate, across, diag))]
    side = give(0, me, mate)
    for c in cross:
        c.start()
    side.start()

    def pass_kv(slot, src, half):
        high = 2 * rows
        part = pl.ds(pl.multiple_of(CTX + half * high, rows), high)
        own = pl.ds(pl.multiple_of(CTX + block + half * high, rows), high)
        return remote(
            src.at[:, own, :],
            src.at[:, part, :],
            scr["kvs"].at[slot],
            scr["kvr"].at[slot],
            seq=lax.rem(s + 1, n),
        )

    def qkv(order, half):
        high = 2 * rows
        here = pl.ds(pl.multiple_of(half * high, high), high)
        part = nf[:, here, :].reshape(2 * high, -1)
        own = pl.ds(pl.multiple_of(CTX + block + half * high, rows), high)
        k_o[:, own, :] = dot(part, wk[...]).astype(BF).reshape(2, high, chan)
        v_o[:, own, :] = dot(part, wv[...]).astype(BF).reshape(2, high, chan)

        @pl.when(s < n - 1)
        def _():
            pass_kv(2 * order, k_o, half).start()
            if order == 0:
                pass_kv(1, v_o, half).start()

        q_o[:, here, :] = dot(part, wq[...]).astype(BF).reshape(2, high, chan)

    near = me // 2
    side.wait_recv()
    fetch.need("wk", "wv", "wq")
    qkv(0, near)
    cross[0].wait_recv()
    cross[1].wait_recv()
    relay[1].start()
    relay[0].start()
    relay[1].wait_recv()
    fetch.need("rate", "cin", "cout", "keep", "init")
    cols = lanes(me)
    for m in range(2):
        u_s[m] = nf[m, :, cols].astype(F32)
    decay = jnp.exp(-rate[...])
    drive = jnp.sqrt(1.0 - decay * decay) * held["cin"][...]

    def run(i, state):
        base = pl.multiple_of(i * 8, 8)
        state = list(state)
        for k in range(8):
            for m in range(2):
                state[m] = decay * state[m] + drive * u_s[m, pl.ds(base + k, 1), :]
        return tuple(state)

    zero = jnp.zeros((NS, chan), F32)
    late = lax.fori_loop(0, (block - CTX) // 8, run, (zero, zero))
    last_state = lax.fori_loop((block - CTX) // 8, block // 8, run, late)
    for m in range(2):
        pay[m * NS : (m + 1) * NS] = last_state[m].astype(BF)
    pay[2 * NS : 3 * NS] = flag_rows(keep)

    def spread(k):
        return remote(
            pay, gath.at[k], scr["gs"].at[k], scr["gr"].at[k], seq=lax.rem(s + k, n)
        )

    for k in range(1, n):

        @pl.when(s + k < n)
        def _():
            spread(k).start()

    for i in (2, 3):
        cross[i].wait_recv()
        relay[i].start()
    for i in (0, 2, 3):
        relay[i].wait_recv()
    fetch.need("ogm")
    for g in grad_gathers:
        g.start()
    qkv(1, 1 - near)
    save(nf, nf_d)
    save(q_o, q_d)

    whole = jnp.exp(-rate[...] * block)
    for k in range(1, n):

        @pl.when(s >= k)
        def _():
            spread(k).wait_recv()

    def entry(begin_keep, end, b):
        return tuple(jnp.where(b == 0, init[m], begin_keep[m] * end[m]) for m in range(2))

    def chain(b, end):
        k = jnp.maximum(s - b, 0)
        got = gath[k].astype(F32)
        begin = entry((got[2 * NS : 2 * NS + 1], got[2 * NS + 1 : 2 * NS + 2]), end, b)
        new = tuple(got[m * NS : (m + 1) * NS] + whole * begin[m] for m in range(2))
        return tuple(jnp.where(b < s, new[m], end[m]) for m in range(2))

    end = lax.fori_loop(0, n - 1, chain, (zero, zero))
    begin = entry((keep[0:1, :], keep[1:2, :]), end, s)
    toward = jnp.exp(-rate[...] * (block - CTX))
    state = tuple(late[m] + toward * begin[m] for m in range(2))
    out_c = held["cout"][...]

    def run_out(i, state):
        base = pl.multiple_of(block - CTX + i * 8, 8)
        row = pl.multiple_of(i * 8, 8)
        state = list(state)
        for k in range(8):
            for m in range(2):
                state[m] = decay * state[m] + drive * u_s[m, pl.ds(base + k, 1), :]
                y_s[m, pl.ds(row + k, 1), :] = jnp.sum(out_c * state[m], axis=0, keepdims=True)
        return tuple(state)

    state = lax.fori_loop(0, CTX // 8, run_out, state)
    ctx_s[...] = y_s[...].astype(BF)
    down = remote(
        ctx_s, ctx_o.at[:, :, cols], scr["cs"].at[0], scr["cr"].at[0], seq=lax.rem(s + 1, n)
    )

    @pl.when(s < n - 1)
    def _():
        down.start()
        pass_kv(3, v_o, 1 - near).start()

    for m in range(2):
        start_o[m] = begin[m]
        end_o[m] = last_state[m] + whole * begin[m]
    for g in grad_gathers:
        g.near()
        g.pass_on()

    @pl.when(s > 0)
    def _():
        down.wait_recv()
        theirs = lanes(across)
        shares = [
            remote(
                ctx_o.at[:, :, part],
                ctx_o.at[:, :, part],
                scr["cs"].at[1 + i],
                scr["cr"].at[1 + i],
                tp=peer,
            )
            for i, (part, peer) in enumerate(((cols, across), (cols, mate), (theirs, mate)))
        ]
        shares[0].start()
        shares[1].start()
        shares[0].wait_recv()
        shares[2].start()
        shares[1].wait_recv()
        shares[2].wait_recv()
        flat = ctx_o[...].reshape(2 * CTX, -1)
        k_o[:, 0:CTX, :] = dot(flat, wk[...]).astype(BF).reshape(2, CTX, chan)
        v_o[:, 0:CTX, :] = dot(flat, wv[...]).astype(BF).reshape(2, CTX, chan)
        for order, half in enumerate((near, 1 - near)):
            pass_kv(2 * order, k_o, half).wait_recv()
            pass_kv(2 * order + 1, v_o, half).wait_recv()
        for c in shares:
            c.wait_send()

    save(k_o, k_d)
    save(v_o, v_d)
    save(ctx_o, ctx_d)
    forward_middle(fetch, held, scr, outs[7:], save, q_o, k_o, v_o, og, grad_gathers)

    @pl.when(s < n - 1)
    def _():
        down.wait_send()
        for order, half in enumerate((near, 1 - near)):
            pass_kv(2 * order, k_o, half).wait_send()
            pass_kv(2 * order + 1, v_o, half).wait_send()

    for k in range(1, n):

        @pl.when(s + k < n)
        def _():
            spread(k).wait_send()

    for c in [side] + cross + relay:
        c.wait_send()
    for g in grad_gathers:
        g.finish()
    save.finish()


def launch(
    body, names, args, outs, out_vmem, scratch, collective_id, limit, name, placed=()
):
    keys = list(scratch)
    count = len(names)
    plain = [name for name in names if name not in placed]

    def kernel(*refs):
        refs_in, refs = refs[:count], refs[count:]
        outs_r, refs = refs[: len(outs)], refs[len(outs) :]
        held, refs = dict(zip(plain, refs)), refs[len(plain) :]
        body(refs_in, outs_r, held, dict(zip(keys, refs)))

    scratch = dict(scratch)
    return pl.pallas_call(
        kernel,
        out_shape=tuple(outs),
        in_specs=[pl.BlockSpec(memory_space=pl.ANY)] * count,
        out_specs=tuple(
            pl.BlockSpec(memory_space=VM if in_vmem else pl.ANY) for in_vmem in out_vmem
        ),
        scratch_shapes=[VM(a.shape, a.dtype) for x, a in zip(names, args) if x in plain]
        + list(scratch.values()),
        compiler_params=pltpu.CompilerParams(
            collective_id=collective_id, has_side_effects=True, vmem_limit_bytes=limit << 20
        ),
        name=name,
    )(*args)


def rms_back(x, gain, grad):
    inv = lax.rsqrt(jnp.mean(x * x, axis=-1, keepdims=True) + eps_norm)
    unit = x * inv
    scaled = grad * gain
    gain_grad = jnp.sum(grad * unit, axis=0, keepdims=True)
    return inv * (scaled - unit * jnp.mean(scaled * unit, axis=-1, keepdims=True)), gain_grad


def forward_middle(fetch, held, scr, outs, save, q, k, v, og, grad_gathers):
    nm, pm, dm, hid, dpre = (scr[x] for x in ("nm", "pm", "dm", "hid", "dpre"))
    mlp_o, h1_o, ffn_o, att, lse = (scr[x] for x in ("mlp", "h1", "ffn", "att", "lse"))
    keep, w_out, tok, gain, w_up, w_down = (
        held[x] for x in ("keep", "w_out", "tok", "mid", "w_up", "w_down")
    )
    me = tp_peers()[0]
    near = me // 2
    block = q.shape[1]
    rows = block // 4
    width = w_out.shape[1]
    tile = 256
    panels = w_up.shape[1] // tile
    own = pl.ds(pl.multiple_of(me * rows, rows), rows)
    edge0 = k.shape[1] - block
    half = block // 2
    row_ids = lax.broadcasted_iota(jnp.int32, (half, half), 0)
    col_ids = lax.broadcasted_iota(jnp.int32, (half, half), 1)
    scale = HD ** (-0.5)

    def attend(m):
        def one(head, c):
            lanes = pl.ds(pl.multiple_of(head * HD, HD), HD)
            shut = (keep[m : m + 1, 0:half] - 1.0) * -neg_big
            for part in range(2):
                mine = slice(part * half, (part + 1) * half)
                edge = edge0 + part * half
                sc = dot(k[m, 0 : edge + half, lanes], q[m, mine, lanes], NT) * scale
                pieces = [sc[:edge0] + shut]
                if part:
                    pieces.append(sc[edge0:edge])
                pieces.append(jnp.where(row_ids <= col_ids, sc[edge:], neg_big))
                sc = jnp.concatenate(pieces, axis=0)
                top = jnp.max(sc, axis=0, keepdims=True)
                expo = jnp.exp(sc - top)
                total = jnp.sum(expo, axis=0, keepdims=True)
                weights = (expo * (1.0 / total)).astype(BF)
                res = dot(v[m, 0 : edge + half, lanes], weights, TN)
                att[m, mine, lanes] = res.T.astype(BF)
                lse[m, head, :, mine] = top + jnp.log(total)
            return c

        lax.fori_loop(0, q.shape[2] // HD, one, 0)

    def scatter(kind, m, ref):
        at = 2 * kind + m
        return Scatter(
            ref.at[m], scr["over"].at[at], scr["into"].at[at], scr["ss"].at[at], scr["sr"].at[at]
        )

    mlp_d, h1_d, dm_d, ffn_d, att_d, lse_d = outs
    sums1 = [scatter(0, m, pm) for m in range(2)]
    gathers = [Gather(nm.at[m], scr["mgs"].at[m], scr["mgr"].at[m]) for m in range(2)]

    def project(m):
        def one(j, c):
            cols = pl.ds(pl.multiple_of(j * tile, tile), tile)
            pm[m, :, cols] = dot(att[m], w_out[:, cols]).astype(BF)
            return c

        lax.fori_loop(0, width // tile, one, 0)

    def residual(m):
        h1 = tok[m].astype(F32) + sums1[m].end()
        h1_o[m] = h1
        inv = lax.rsqrt(jnp.mean(h1 * h1, axis=-1, keepdims=True) + eps_norm)
        nm[m, own, :] = (h1 * inv * gain[...]).astype(BF)
        gathers[m].start()

    def feed(m, part):
        here = pl.ds(pl.multiple_of(part * half, half), half)
        flat = pl.ds(pl.multiple_of(m * block + part * half, half), half)

        def panel(j, c):
            cols = pl.ds(pl.multiple_of(j * tile, tile), tile)
            pre = dot(nm[m, here, :], w_up[:, cols])
            sq = pre * pre
            t = jnp.tanh((0.7978845608028654 * pre) * (1.0 + 0.044715 * sq))
            hid[flat, cols] = (0.5 * pre * (1.0 + t)).astype(BF)
            slope = 0.5 * (1.0 + t) + (0.3989422804014327 * pre) * (1.0 - t * t) * (
                1.0 + 0.134145 * sq
            )
            dpre[flat, cols] = (slope * dot(og[m, here, :], w_down[cols, :], NT)).astype(BF)
            return c

        lax.fori_loop(0, panels, panel, 0)

        def back(j, c):
            cols = pl.ds(pl.multiple_of(j * tile, tile), tile)
            dm[m, here, cols] = dot(dpre[flat, :], w_up[cols, :], NT).astype(BF)
            return c

        lax.fori_loop(0, width // tile, back, 0)

    def lower(m, part):
        here = pl.ds(pl.multiple_of(part * half, half), half)
        flat = pl.ds(pl.multiple_of(m * block + part * half, half), half)

        def one(j, c):
            cols = pl.ds(pl.multiple_of(j * tile, tile), tile)
            mlp_o[m, here, cols] = dot(hid[flat, :], w_down[:, cols]).astype(BF)
            return c

        lax.fori_loop(0, width // tile, one, 0)

    attend(0)
    fetch.need("w_out")
    project(0)
    sums1[0].start()
    sums1[0].turn()
    attend(1)
    project(1)
    save(att, att_d)
    save(lse, lse_d)
    sums1[1].start()
    sums1[1].turn()
    fetch.need("mid")
    residual(0)
    fetch.need("w_up", "w_down")
    for g in grad_gathers:
        g.far()
    gathers[0].near()
    feed(0, near)
    residual(1)
    save(h1_o, h1_d)
    gathers[0].pass_on()
    gathers[1].near()
    feed(1, near)
    lower(0, near)
    lower(1, near)
    gathers[0].far()
    feed(0, 1 - near)
    save(dm.at[0], dm_d.at[0])
    gathers[1].pass_on()
    gathers[1].far()
    feed(1, 1 - near)
    save(dm.at[1], dm_d.at[1])

    def down_sum(i, c):
        left = hid[:, pl.ds(pl.multiple_of(i * tile, tile), tile)]
        for j in range(width // tile):
            right = og[:, :, j * tile : (j + 1) * tile].reshape(2 * block, tile)
            at = pl.multiple_of((width // tile + j) * panels * tile + i * tile, tile)
            ffn_o[pl.ds(at, tile), :] = dot(left, right, TN).astype(BF)
        return c

    def up_sum(i, c):
        left = nm[:, :, pl.ds(pl.multiple_of(i * tile, tile), tile)].reshape(2 * block, tile)
        for j in range(panels):
            at = pl.multiple_of(j * width + i * tile, tile)
            ffn_o[pl.ds(at, tile), :] = dot(
                left, dpre[:, j * tile : (j + 1) * tile], TN
            ).astype(BF)
        return c

    high = panels * tile * (width // tile)
    lax.fori_loop(0, panels, down_sum, 0)
    save(ffn_o.at[high : 2 * high], ffn_d.at[high : 2 * high])
    lower(0, 1 - near)
    lower(1, 1 - near)
    save(mlp_o, mlp_d)
    lax.fori_loop(0, width // tile, up_sum, 0)
    save(ffn_o.at[0:high], ffn_d.at[0:high])
    for m in range(2):
        gathers[m].finish()


def forward(*args):
    n = lax.axis_size("seq")
    by = dict(zip(FORWARD_IN, args))
    micro, rows, width = by["tok"].shape
    block = 4 * rows
    chan = by["rate"].shape[1]
    units = by["w_up"].shape[1]
    keys = CTX + 2 * block
    sds = jax.ShapeDtypeStruct
    dma = pltpu.SemaphoreType.DMA
    results = dict(
        nf=sds((micro, block, width), BF),
        q=sds((micro, block, chan), BF),
        k=sds((micro, keys, chan), BF),
        v=sds((micro, keys, chan), BF),
        ctxa=sds((micro, CTX, width), BF),
        start=sds((micro, NS, chan), F32),
        end=sds((micro, NS, chan), F32),
        mlp=sds((micro, block, width), BF),
        h1=sds((micro, rows, width), F32),
        dm=sds((micro, block, width), BF),
        ffn=sds((2 * units * width // 256, 256), BF),
        att=sds((micro, block, chan), BF),
        lse=sds((micro, chan // HD, 1, block), F32),
    )
    in_vmem = ("start", "end")
    scratch = {x: VM(a.shape, a.dtype) for x, a in results.items() if x not in in_vmem}
    scratch.update(
        og=VM((micro, block, width), BF),
        fetch=dma((len(FORWARD_IN),)),
        save=dma((16,)),
        os=dma((2, 3)),
        u=VM((micro, block, chan), F32),
        gath=VM((n, 3 * NS, chan), BF),
        pay=VM((3 * NS, chan), BF),
        y=VM((micro, CTX, chan), F32),
        ctx=VM((micro, CTX, chan), BF),
        ts=dma((9,)),
        tr=dma((9,)),
        kvs=dma((4,)),
        kvr=dma((4,)),
        gs=dma((n,)),
        gr=dma((n,)),
        cs=dma((4,)),
        cr=dma((4,)),
        nm=VM((micro, block, width), BF),
        pm=VM((micro, block, width), BF),
        hid=VM((micro * block, units), BF),
        dpre=VM((micro * block, units), BF),
        over=VM((2, rows, width), BF),
        into=VM((2, 3, rows, width), BF),
        ss=dma((2, 3)),
        sr=dma((2, 3)),
        mgs=dma((2, 3)),
        mgr=dma((2, 3)),
    )
    scratch["or"] = dma((2, 3))
    return launch(
        functools.partial(forward_kernel, n),
        FORWARD_IN,
        args,
        tuple(results.values()),
        [x in in_vmem for x in results],
        scratch,
        0,
        62,
        "forward",
        ("ogm",),
    )


class Ring:
    def __init__(self, n, x, recv, send_sem, recv_sem):
        self.n, self.x, self.recv = n, x, recv
        self.send_sem, self.recv_sem = send_sem, recv_sem
        self.subs, self.rows = recv.shape[2], recv.shape[3]
        s = lax.axis_index("seq")
        half = n // 2
        self.r = jnp.where(lax.rem(s, 2) == 0, s // 2, n - 1 - s // 2)

        def dev(q):
            q = lax.rem(q + n, n)
            return jnp.where(q < half, 2 * q, 2 * (n - 1 - q) + 1)

        self.target = (dev(self.r + 1), dev(self.r - 1))
        self.done = 0
        self.total = 2 * n - 2

    def chunk(self, d, b, off):
        sign = (1, -1)[d]
        c = lax.rem(self.r + sign * off + 2 * self.n, self.n)
        at = ((d * self.n + c) * self.subs + b) * self.rows
        return pl.ds(pl.multiple_of(at, self.rows), self.rows)

    def copy(self, d, b, src, dst, k):
        return pltpu.make_async_remote_copy(
            src_ref=src,
            dst_ref=dst,
            send_sem=self.send_sem.at[d, b, k],
            recv_sem=self.recv_sem.at[d, b, k],
            device_id={"seq": self.target[d]},
            device_id_type=MESH,
        )

    def first(self, d, b):
        return self.copy(d, b, self.x.at[self.chunk(d, b, 0)], self.recv.at[d, 0, b], 0)

    def sums(self, d, b, k):
        prior = jnp.maximum(k - 1, 0)
        return self.copy(d, b, self.recv.at[d, prior, b], self.recv.at[d, k, b], k)

    def alls(self, d, b, k):
        ref = self.x.at[self.chunk(d, b, 1 - k)]
        return self.copy(d, b, ref, ref, self.n - 1 + k)

    def each(self):
        return [(d, b) for b in range(self.subs) for d in range(2)]

    def add(self, d, b, k):
        mine = self.x[self.chunk(d, b, -k - 1)]
        return (self.recv[d, k, b].astype(F32) + mine.astype(F32)).astype(BF)

    def start(self):
        for d, b in self.each():
            self.first(d, b).start()

    def tick(self, t):
        n = self.n

        def leave():
            for d, b in self.each():
                self.first(d, b).wait_send()

        def sum_step():
            for d, b in self.each():
                self.sums(d, b, t).wait_recv()
                self.recv[d, t, b] = self.add(d, b, t)
                self.sums(d, b, t + 1).start()

        def turn():
            for d, b in self.each():
                self.sums(d, b, n - 2).wait_recv()
                self.x[self.chunk(d, b, 1)] = self.add(d, b, n - 2)
                self.alls(d, b, 0).start()

        def all_step():
            k = t - (n - 1)
            for d, b in self.each():
                self.alls(d, b, k).wait_recv()
                self.alls(d, b, k + 1).start()

        def close():
            for d, b in self.each():
                self.alls(d, b, n - 2).wait_recv()

        steps = (
            (t == 0, leave),
            (t < n - 2, sum_step),
            (t == n - 2, turn),
            ((t > n - 2) & (t < 2 * n - 3), all_step),
            (t == 2 * n - 3, close),
        )
        for when, step in steps:
            if isinstance(t, int):
                if when:
                    step()
            else:
                pl.when(when)(step)

    def go(self, fourteenths):
        upto = min(-(-fourteenths * self.total // 14), self.total)
        if upto - self.done == 1:
            self.tick(self.done)
        elif upto > self.done:

            def one(t, c):
                self.tick(t)
                return c

            lax.fori_loop(self.done, upto, one, 0)
        self.done = max(upto, self.done)

    def drain(self):
        def more(k, c):
            for d, b in self.each():
                self.sums(d, b, k + 1).wait_send()
                self.alls(d, b, k).wait_send()
            return c

        lax.fori_loop(0, self.n - 2, more, 0)
        for d, b in self.each():
            self.alls(d, b, self.n - 2).wait_send()


LAST_IN = (
    "q",
    "k",
    "v",
    "lse",
    "att",
    "w_out",
    "nf",
    "ctx",
    "wq",
    "wk",
    "wv",
    "rate",
    "cin",
    "cout",
    "start",
    "keep",
    "endg",
    "mlp",
    "h1",
    "dm",
    "ogm",
    "mid",
    "tok",
    "gain",
    "ffn",
)


def last_kernel(n, refs_in, outs, h, scr):
    x1, x2, x3 = scr["x1"], scr["x2"], scr["x3"]
    ffn_rows = refs_in[LAST_IN.index("ffn")].shape[0]
    h = dict(h, ffn=x1.at[0:ffn_rows])
    fetch = Fetch(LAST_IN, refs_in, h, scr["fetch"])
    need = fetch.need
    mixed_o, tg_o, sum1_o, sum2_o, rate_o, cin_o, cout_o, gain_o = outs
    s = lax.axis_index("seq")
    me, mate, across, diag = tp_peers()
    peers = (mate, across, diag)
    nf, rate, tok = h["nf"], h["rate"], h["tok"]
    block = nf.shape[1]
    rows = block // 4
    width = nf.shape[2]
    chan = rate.shape[1]
    rk, rv, gath, dcr = scr["rk"], scr["rv"], scr["gath"], scr["dcr"]
    gath[...] = jnp.zeros_like(gath)
    if x1.shape[0] > ffn_rows:
        x1[ffn_rows:] = jnp.zeros((x1.shape[0] - ffn_rows, chan), BF)
    used2 = 4 * width
    if x2.shape[0] > used2:
        x2[used2:] = jnp.zeros((x2.shape[0] - used2, chan), BF)
    x3[...] = jnp.zeros_like(x3)

    @pl.when(s == n - 1)
    def _():
        rk[...] = jnp.zeros_like(rk)
        rv[...] = jnp.zeros_like(rv)
        dcr[...] = jnp.zeros_like(dcr)

    greet(n, True)
    before = lax.rem(s + n - 1, n)
    own = pl.ds(pl.multiple_of(me * rows, rows), rows)

    def to_before(sem, slot, src, dst):
        return remote(
            src, dst, scr["send_k"].at[sem, slot], scr["recv_k"].at[sem, slot], seq=before
        )

    ring1 = Ring(n, x1, scr["r1"], scr["s1s"], scr["s1r"])
    ring2 = Ring(n, x2, scr["r2"], scr["s2s"], scr["s2r"])
    ring3 = Ring(n, x3, scr["r3"], scr["s3s"], scr["s3r"])
    rr, da, dh1, mlp, h1 = scr["rr"], scr["da"], scr["dh1"], h["mlp"], h["h1"]

    def scatter(ref, at, m):
        at = 2 * at + m
        return Scatter(
            ref.at[m], scr["over"].at[at], scr["into"].at[at], scr["ss"].at[at], scr["sr"].at[at]
        )

    mid_sums = [scatter(h["dm"], 0, m) for m in range(2)]
    gathers = [Gather(rr.at[m], scr["rs"].at[m], scr["rrv"].at[m]) for m in range(2)]
    need("dm")
    greeted(n, True)
    for c in mid_sums:
        c.start()
    need("ffn")
    ring1.start()
    for c in mid_sums:
        c.turn()
    need("h1", "ogm", "mid")
    mid_grad = jnp.zeros((1, width), F32)
    for m in range(2):
        back, one = rms_back(h1[m], h["mid"][...], mid_sums[m].end())
        mid_grad = mid_grad + one
        dh1[m] = h["ogm"][m].astype(F32) + back
        rr[m, own, :] = dh1[m].astype(BF)
        gathers[m].start()
        ring1.go(m + 1)
    need("w_out", "q", "k", "v", "lse", "keep")

    q, k, v, lse, keep, w_out = (h[name] for name in ("q", "k", "v", "lse", "keep", "w_out"))
    edge0 = k.shape[1] - block
    half = block // 2
    row_ids = lax.broadcasted_iota(jnp.int32, (half, half), 0)
    col_ids = lax.broadcasted_iota(jnp.int32, (half, half), 1)
    scale = HD ** (-0.5)
    dq_s, dko, dvo, dkc, dvc = (scr[x] for x in ("dq", "dko", "dvo", "dkc", "dvc"))
    dkp, dvp, ak, av = (scr[x] for x in ("dkp", "dvp", "ak", "av"))

    def attend_one(m, head):
        i = 2 * m + head
        lanes = pl.ds(pl.multiple_of(head * HD, HD), HD)
        shut = (keep[pl.ds(m, 1), 0:half] - 1.0) * -neg_big
        for part in (1, 0):
            mine = slice(part * half, (part + 1) * half)
            edge = edge0 + part * half
            qq = q[m, mine, lanes]
            kk = k[m, 0 : edge + half, lanes]
            dd = da[m, mine, lanes]
            sc = dot(kk, qq, NT) * scale
            pieces = [sc[:edge0] + shut]
            if part:
                pieces.append(sc[edge0:edge])
            pieces.append(jnp.where(row_ids <= col_ids, sc[edge:], neg_big))
            sc = jnp.concatenate(pieces, axis=0)
            probs = jnp.exp(sc - lse[m, head, :, mine])
            dp = dot(v[m, 0 : edge + half, lanes], dd, NT)
            spread_sum = jnp.sum(probs * dp, axis=0, keepdims=True)
            ds = (probs * (dp - spread_sum)).astype(BF)
            dq_s[m, mine, lanes] = (dot(kk, ds, TN) * scale).T.astype(BF)
            dk = dot(ds, qq) * scale
            dv = dot(probs.astype(BF), dd)
            if part:
                ak[...] = dk
                av[...] = dv
            else:
                ak[0 : edge + half] += dk
                av[0 : edge + half] += dv
        for acc, far, prev, own in ((ak, dkc, dkp, dko), (av, dvc, dvp, dvo)):
            far[m, :, lanes] = acc[0:CTX].astype(BF)
            prev[i] = acc[CTX:edge0].astype(BF)
            own[m, :, lanes] = acc[edge0:]

        @pl.when(s > 0)
        def _():
            to_before(0, i, dkp.at[i], rk.at[i]).start()
            to_before(1, i, dvp.at[i], rv.at[i]).start()

    def stream_back(m, c):
        g = Gather(rr.at[m], scr["rs"].at[m], scr["rrv"].at[m])
        g.near()
        g.pass_on()
        g.far()
        ring1.tick(m + ring1.done)
        da[m] = dot(rr[m], w_out[...], NT).astype(BF)

        def heads(head, c):
            attend_one(m, head)
            return c

        lax.fori_loop(0, chan // HD, heads, 0)
        return c

    lax.fori_loop(0, 2, stream_back, 0)
    ring1.done += 2

    cp, cr, dcs = scr["cp"], scr["cr"], scr["dcs"]
    wq, wk, wv = h["wq"], h["wk"], h["wv"]
    need("wq", "wk", "wv")
    ctx_part = dot(dkc[...].reshape(2 * CTX, chan), wk[...], NT) + dot(
        dvc[...].reshape(2 * CTX, chan), wv[...], NT
    )
    for j in range(4):
        cp[j] = ctx_part[:, j * chan : (j + 1) * chan].astype(BF).reshape(2, CTX, chan)

    def to_peer(i, src, dst, kind):
        return remote(
            src, dst, scr["send_c"].at[kind, i], scr["recv_c"].at[kind, i], tp=peers[i]
        )

    ctx_out = [to_peer(i, cp.at[peers[i]], cr.at[i], 0) for i in range(3)]
    for c in ctx_out:
        c.start()
    need("mlp")
    mlp_sums = [scatter(mlp, 1, m) for m in range(2)]
    for c in mlp_sums:
        c.start()
    ring1.go(5)

    u_s, du_s, hist = scr["u"], scr["du"], scr["hist"]
    cols = pl.ds(pl.multiple_of(me * chan, chan), chan)
    need("nf", "rate", "cin", "cout", "start", "endg")
    for m in range(2):
        u_s[m] = nf[m, :, cols].astype(F32)
    decay = jnp.exp(-rate[...])
    root = jnp.sqrt(1.0 - decay * decay)
    drive = root * h["cin"][...]
    out_c = h["cout"][...]
    start, endg = h["start"], h["endg"]
    for m in range(2):
        hist[0, m] = start[m].astype(BF)

    def run(i, state):
        base = pl.multiple_of(i * 8, 8)
        state = list(state)
        for k in range(8):
            for m in range(2):
                state[m] = decay * state[m] + drive * u_s[m, pl.ds(base + k, 1), :]
                hist[base + k + 1, m] = state[m].astype(BF)
        return tuple(state)

    lax.fori_loop(0, block // 8, run, (start[0], start[1]))
    ctx_back = to_before(0, 4, dcs, dcr)
    total = cp[me].astype(F32)
    for i in range(3):
        ctx_out[i].wait_recv()
        total = total + cr[i].astype(F32)
    dcs[...] = total.astype(BF)

    @pl.when(s > 0)
    def _():
        ctx_back.start()

    for c in mlp_sums:
        c.turn()
    need("att")
    flat_att = h["att"][...].reshape(2 * block, chan)
    tile = 256

    def proj(j, c):
        cols = pl.ds(pl.multiple_of(j * tile, tile), tile)
        right = rr[:, :, cols].reshape(2 * block, tile)
        at = pl.multiple_of(3 * width + j * tile, tile)
        x2[pl.ds(at, tile), :] = dot(flat_att, right, TN).astype(BF)
        here = pl.ds(pl.multiple_of(j * tile, tile), tile)
        left = nf[:, :, here].reshape(2 * block, tile)
        x2[here, :] = dot(left, dq_s[...].reshape(2 * block, chan), TN).astype(BF)
        return c

    ring1.go(6)
    lax.fori_loop(0, width // tile, proj, 0)

    @pl.when(s < n - 1)
    def _():
        ctx_back.wait_recv()

    dy_s = scr["dy"]
    dy_s[...] = dcr[...].astype(F32)
    zero = jnp.zeros((NS, chan), F32)

    def early(i, grad):
        base = pl.multiple_of(CTX - 8 - i * 8, 8)
        grad = list(grad)
        for k in range(7, -1, -1):
            for m in range(2):
                grad[m] = decay * grad[m] + out_c * dy_s[m, pl.ds(base + k, 1), :]
        return tuple(grad)

    got = lax.fori_loop(0, CTX // 8, early, (zero, zero))
    reach = jnp.exp(-rate[...] * (block - CTX + 1.0))
    whole = jnp.exp(-rate[...] * block)
    pay = scr["pay"]
    for m in range(2):
        pay[m * NS : (m + 1) * NS] = (reach * got[m] + whole * endg[m]).astype(BF)
    pay[2 * NS : 3 * NS] = flag_rows(keep)

    def spread(k):
        return remote(
            pay,
            gath.at[k],
            scr["send_g"].at[k],
            scr["recv_g"].at[k],
            seq=lax.rem(s + n - k, n),
        )

    for k in range(1, n):

        @pl.when(s >= k)
        def _():
            spread(k).start()

    ring1.go(7)
    for m in range(2):
        mixed_o[m] = (h1[m] + mlp_sums[m].end()).astype(BF)
    @pl.when(s < n - 1)
    def _():
        for i in range(4):
            to_before(0, i, dkp.at[i], rk.at[i]).wait_recv()
            to_before(1, i, dvp.at[i], rv.at[i]).wait_recv()

    dk_b, dv_b = scr["dkb"], scr["dvb"]
    for m in range(2):
        for head in range(chan // HD):
            lanes = slice(head * HD, (head + 1) * HD)
            i = m * (chan // HD) + head
            dk_b[m, :, lanes] = (dko[m, :, lanes] + rk[i].astype(F32)).astype(BF)
            dv_b[m, :, lanes] = (dvo[m, :, lanes] + rv[i].astype(F32)).astype(BF)

    need("ctx")
    ctx = h["ctx"]

    def kv_grads(i, c):
        at = pl.multiple_of(i * tile, tile)
        here = pl.ds(at, tile)
        left = nf[:, :, here].reshape(2 * block, tile)
        left_ctx = ctx[:, :, here].reshape(2 * CTX, tile)
        for j, (own, far) in enumerate(((dk_b, dkc), (dv_b, dvc))):
            value = dot(left, own[...].reshape(2 * block, chan), TN) + dot(
                left_ctx, far[...].reshape(2 * CTX, chan), TN
            )
            x2[pl.ds((j + 1) * width + at, tile), :] = value.astype(BF)
        return c

    lax.fori_loop(0, width // tile, kv_grads, 0)
    ring2.start()
    ring1.go(8)
    for k in range(1, n):

        @pl.when(s + k < n)
        def _():
            spread(k).wait_recv()

    def chain(i, carry):
        k = n - 1 - i
        got = gath[k].astype(F32)
        valid = s + k < n
        return tuple(
            jnp.where(
                valid,
                got[2 * NS + m : 2 * NS + m + 1]
                * (got[m * NS : (m + 1) * NS] + whole * carry[m]),
                carry[m],
            )
            for m in range(2)
        )

    carry = lax.fori_loop(0, n - 1, chain, (zero, zero))
    grads0 = tuple(endg[m] + carry[m] for m in range(2))

    def back_late(i, val):
        hold, d_drive, d_decay, d_out = list(val[0:2]), val[2], val[3], val[4]
        low_row = pl.multiple_of(CTX - 8 - i * 8, 8)
        base = pl.multiple_of(block - 8 - i * 8, 8)
        for k in range(7, -1, -1):
            for m in range(2):
                dy = dy_s[m, pl.ds(low_row + k, 1), :]
                grad = hold[m] + out_c * dy
                du_s[m, pl.ds(base + k, 1), :] = jnp.sum(drive * grad, axis=0, keepdims=True)
                d_drive = d_drive + grad * u_s[m, pl.ds(base + k, 1), :]
                d_decay = d_decay + grad * hist[base + k, m].astype(F32)
                d_out = d_out + dy * hist[base + k + 1, m].astype(F32)
                hold[m] = decay * grad
        return hold[0], hold[1], d_drive, d_decay, d_out

    val = lax.fori_loop(0, CTX // 8, back_late, (grads0[0], grads0[1], zero, zero, zero))

    def back_early(i, val):
        hold, d_drive, d_decay = list(val[0:2]), val[2], val[3]
        base = pl.multiple_of(block - CTX - 8 - i * 8, 8)
        for k in range(7, -1, -1):
            for m in range(2):
                grad = hold[m]
                du_s[m, pl.ds(base + k, 1), :] = jnp.sum(drive * grad, axis=0, keepdims=True)
                d_drive = d_drive + grad * u_s[m, pl.ds(base + k, 1), :]
                d_decay = d_decay + grad * hist[base + k, m].astype(F32)
                hold[m] = decay * grad
        return hold[0], hold[1], d_drive, d_decay

    _, _, d_drive, d_decay = lax.fori_loop(0, (block - CTX) // 8, back_early, val[0:4])
    x3[0:NS] = (-decay * (d_decay - d_drive * h["cin"][...] * decay / root)).astype(BF)
    x3[NS : 2 * NS] = (d_drive * root).astype(BF)
    x3[2 * NS : 3 * NS] = val[4].astype(BF)
    ring3.start()
    ring1.go(9)
    ring2.go(1)
    part_s = scr["part"]

    def normed_part(i, c):
        m, part = i // 2, lax.rem(i, 2)
        here = pl.ds(pl.multiple_of(part * half, half), half)
        part_s[...] = (
            dot(dq_s[m, here, :], wq[...], NT)
            + dot(dk_b[m, here, :], wk[...], NT)
            + dot(dv_b[m, here, :], wv[...], NT)
        )
        part_s[:, cols] += du_s[m, here, :]
        mlp[m, here, :] = part_s[...].astype(BF)
        return c

    finals = [scatter(mlp, 0, m) for m in range(2)]
    for m in range(2):
        lax.fori_loop(2 * m, 2 * m + 2, normed_part, 0)
        finals[m].start()
    for c in finals:
        c.turn()
    ring1.go(10)
    ring2.go(2)
    ring3.go(1)
    need("tok", "gain")
    gain_grad = jnp.zeros((1, width), F32)
    for m in range(2):
        back, one = rms_back(tok[m].astype(F32), h["gain"][...], finals[m].end())
        tg_o[m] = dh1[m] + back
        gain_grad = gain_grad + one
    gp, gr, gs, gg = scr["gp"], scr["gr"], scr["gs"], scr["gg"]
    for j in range(4):
        gp[j, 0:1] = gain_grad[:, j * chan : (j + 1) * chan]
        gp[j, 1:2] = mid_grad[:, j * chan : (j + 1) * chan]
        gp[j, 2:8] = jnp.zeros((6, chan), F32)
    gains = [to_peer(i, gp.at[peers[i]], gr.at[i], 1) for i in range(3)]
    for c in gains:
        c.start()
    ring1.go(11)
    ring2.go(3)
    ring3.go(2)
    total = gp[me]
    for i in range(3):
        gains[i].wait_recv()
        total = total + gr[i]
    gs[...] = total

    def gain_out(k):
        return remote(
            gs,
            gg.at[k],
            scr["gain_s"].at[k],
            scr["gain_r"].at[k],
            seq=lax.rem(s + k, n),
        )

    for k in range(1, n):
        gain_out(k).start()
    for t in range(12, 15):
        ring1.go(t)
        ring2.go(t - 8)
        ring3.go(t - 9)
    store1 = pltpu.make_async_copy(x1, sum1_o, scr["store"].at[0])
    store1.start()
    for t in range(7, 15):
        ring2.go(t)
        ring3.go(min(t - 1 + (t - 7) // 3, 14))
    store2 = pltpu.make_async_copy(x2, sum2_o, scr["store"].at[1])
    store2.start()
    ring3.go(14)
    for i, small_o in enumerate((rate_o, cin_o, cout_o)):
        small_o[...] = x3[i * NS : (i + 1) * NS].astype(F32)
    for k in range(1, n):
        gain_out(k).wait_recv()
        total = total + gg[k]
    gain_o[...] = total
    for k in range(1, n):
        gain_out(k).wait_send()
    for c in gains + ctx_out:
        c.wait_send()
    for g in gathers:
        g.finish()

    @pl.when(s > 0)
    def _():
        ctx_back.wait_send()
        for i in range(4):
            to_before(0, i, dkp.at[i], rk.at[i]).wait_send()
            to_before(1, i, dvp.at[i], rv.at[i]).wait_send()

    for k in range(1, n):

        @pl.when(s >= k)
        def _():
            spread(k).wait_send()

    ring1.drain()
    ring2.drain()
    ring3.drain()
    store1.wait()
    store2.wait()


def ring_rows(n, used, subs):
    return -(-used // (2 * n * subs * 16)) * 16


def last(*args):
    n = lax.axis_size("seq")
    by = dict(zip(LAST_IN, args))
    micro, block, width = by["nf"].shape
    rows = block // 4
    chan = by["rate"].shape[1]
    keys = by["k"].shape[1]
    sds = jax.ShapeDtypeStruct
    dma = pltpu.SemaphoreType.DMA
    step1 = ring_rows(n, by["ffn"].shape[0], 2)
    step2 = ring_rows(n, 4 * width, 2)
    step3 = ring_rows(n, 3 * NS, 1)
    x1 = VM((4 * n * step1, chan), BF)
    x2 = VM((4 * n * step2, chan), BF)
    scratch = dict(
        x1=x1,
        r1=VM((2, n - 1, 2, step1, chan), BF),
        x2=x2,
        r2=VM((2, n - 1, 2, step2, chan), BF),
        x3=VM((2 * n * step3, chan), BF),
        r3=VM((2, n - 1, 1, step3, chan), BF),
        s1s=dma((2, 2, 2 * n - 2)),
        s1r=dma((2, 2, 2 * n - 2)),
        s2s=dma((2, 2, 2 * n - 2)),
        s2r=dma((2, 2, 2 * n - 2)),
        s3s=dma((2, 1, 2 * n - 2)),
        s3r=dma((2, 1, 2 * n - 2)),
        fetch=dma((len(LAST_IN),)),
        rr=VM((micro, block, width), BF),
        da=VM((micro, block, chan), BF),
        rs=dma((2, 3)),
        rrv=dma((2, 3)),
        rk=VM((4, block, HD), BF),
        rv=VM((4, block, HD), BF),
        dkp=VM((4, block, HD), BF),
        dvp=VM((4, block, HD), BF),
        ak=VM((keys, HD), F32),
        av=VM((keys, HD), F32),
        dq=VM((micro, block, chan), BF),
        dko=VM((micro, block, chan), F32),
        dvo=VM((micro, block, chan), F32),
        dkb=VM((micro, block, chan), BF),
        dvb=VM((micro, block, chan), BF),
        dkc=VM((micro, CTX, chan), BF),
        dvc=VM((micro, CTX, chan), BF),
        cp=VM((4, micro, CTX, chan), BF),
        cr=VM((3, micro, CTX, chan), BF),
        dcs=VM((micro, CTX, chan), BF),
        dcr=VM((micro, CTX, chan), BF),
        dy=VM((micro, CTX, chan), F32),
        u=VM((micro, block, chan), F32),
        du=VM((micro, block, chan), F32),
        hist=VM((block + 1, micro, NS, chan), BF),
        pay=VM((3 * NS, chan), BF),
        gath=VM((n, 3 * NS, chan), BF),
        part=VM((block // 2, width), F32),
        dh1=VM((micro, rows, width), F32),
        over=VM((4, rows, width), BF),
        into=VM((4, 3, rows, width), BF),
        ss=dma((4, 3)),
        sr=dma((4, 3)),
        gp=VM((4, 8, chan), F32),
        gr=VM((3, 8, chan), F32),
        gs=VM((8, chan), F32),
        gg=VM((n, 8, chan), F32),
        gain_s=dma((n,)),
        gain_r=dma((n,)),
        send_k=dma((2, 5)),
        recv_k=dma((2, 5)),
        send_c=dma((2, 3)),
        recv_c=dma((2, 3)),
        send_g=dma((n,)),
        recv_g=dma((n,)),
        store=dma((2,)),
    )
    outs = (
        sds((micro, rows, width), BF),
        sds((micro, rows, width), F32),
        sds(x1.shape, BF),
        sds(x2.shape, BF),
        sds((NS, chan), F32),
        sds((NS, chan), F32),
        sds((NS, chan), F32),
        sds((8, chan), F32),
    )
    return launch(
        functools.partial(last_kernel, n),
        LAST_IN,
        args,
        outs,
        [True, True, False, False, True, True, True, True],
        scratch,
        2,
        62,
        "last",
        ("ffn",),
    )


def finish_kernel(*refs):
    half = len(refs) // 2
    for src, dst in zip(refs[:half], refs[half:]):
        dst[...] = src[...].astype(dst.dtype)


def finish(sum1, sum2, mixed, tokens_grad, end, small, width, units, chan):
    steps = width // chan
    sds = jax.ShapeDtypeStruct
    down_at = units * width // chan
    micro, rows, _ = mixed.shape

    def panel(rows_of, at):
        return (
            pl.BlockSpec((rows_of, chan), lambda j: (at // rows_of + j, 0)),
            pl.BlockSpec((rows_of, chan), lambda j: (0, j)),
        )

    def column(at):
        high = width // steps
        return (
            pl.BlockSpec((high, chan), lambda j: (at // high + j, 0)),
            pl.BlockSpec((high, chan), lambda j: (j, 0)),
        )

    same = pl.BlockSpec((micro, rows // steps, width), lambda j: (0, j, 0))
    whole = pl.BlockSpec(end.shape, lambda j: (0, 0, 0))
    specs = [
        panel(width, 0),
        panel(units, down_at),
        panel(chan, 3 * width),
        column(0),
        column(width),
        column(2 * width),
        (same, same),
        (same, same),
        (whole, whole),
    ] + [
        (pl.BlockSpec(a.shape, lambda j: (0, 0)), pl.BlockSpec(a.shape, lambda j: (0, 0)))
        for a in small
    ]
    return pl.pallas_call(
        finish_kernel,
        grid=(steps,),
        out_shape=(
            sds((width, units), F32),
            sds((units, width), F32),
            sds((chan, width), F32),
            sds((width, chan), F32),
            sds((width, chan), F32),
            sds((width, chan), F32),
            sds(mixed.shape, BF),
            sds(tokens_grad.shape, F32),
            sds(end.shape, F32),
            *(sds(a.shape, F32) for a in small),
        ),
        in_specs=[a for a, _ in specs],
        out_specs=tuple(b for _, b in specs),
        compiler_params=pltpu.CompilerParams(vmem_limit_bytes=62 << 20),
        name="finish",
    )(sum1, sum1, sum2, sum2, sum2, sum2, mixed, tokens_grad, end, *small)


def body(
    tokens,
    out_grad,
    norm_gain,
    w_query,
    w_key,
    w_value,
    w_out,
    mid_gain,
    w_up,
    w_down,
    ssm_rate,
    ssm_in,
    ssm_out,
    resets,
    init_state,
    states_grad,
):
    micro, rows, width = tokens.shape
    chan = ssm_rate.shape[0]
    units = w_up.shape[1]
    rate, cin, cout = ssm_rate.T, ssm_in.T, ssm_out.T
    keep = jnp.broadcast_to(1.0 - resets.astype(F32), (micro, chan))
    init = jnp.swapaxes(init_state, 1, 2)
    endg = jnp.swapaxes(states_grad[:, 0], 1, 2)
    gain_row, mid_row = norm_gain[None], mid_gain[None]
    nf, q, k, v, ctx, start, end, mlp, h1, dm, ffn, att, lse = forward(
        *(tokens, gain_row, w_key, w_value, w_query, rate, cin, cout, keep, init, out_grad),
        *(w_out, mid_row, w_up, w_down),
    )
    mixed, tokens_grad, sum1, sum2, rate_g, in_g, out_g, gains = last(
        *(q, k, v, lse, att, w_out, nf, ctx, w_query, w_key, w_value, rate, cin, cout),
        *(start, keep, endg, mlp, h1, dm, out_grad, mid_row, tokens, gain_row, ffn),
    )
    done = finish(
        sum1, sum2, mixed, tokens_grad, end, (rate_g, in_g, out_g), width, units, chan
    )
    up_g, down_g, proj_g, query_g, key_g, value_g, mixed, tokens_grad, end = done[:9]
    rate_g, in_g, out_g = done[9:]
    return (
        mixed,
        jnp.swapaxes(end, 1, 2)[:, None],
        tokens_grad,
        gains[0],
        query_g,
        key_g,
        value_g,
        proj_g,
        gains[1],
        up_g,
        down_g,
        rate_g.T,
        in_g.T,
        out_g.T,
    )


def solution(mesh):
    return jax.shard_map(
        body,
        mesh=mesh,
        in_specs=(
            P(None, ("seq", "tp"), None),
            P(None, ("seq", "tp"), None),
            P(),
            P(None, "tp"),
            P(None, "tp"),
            P(None, "tp"),
            P("tp", None),
            P(),
            P(None, "tp"),
            P("tp", None),
            P("tp", None),
            P("tp", None),
            P("tp", None),
            P(None, "seq"),
            P(None, "tp", None),
            P(None, "seq", "tp", None),
        ),
        out_specs=(
            P(None, ("seq", "tp"), None),
            P(None, "seq", "tp", None),
            P(None, ("seq", "tp"), None),
            P("tp"),
            P(None, "tp"),
            P(None, "tp"),
            P(None, "tp"),
            P("tp", None),
            P("tp"),
            P(None, "tp"),
            P("tp", None),
            P("tp", None),
            P("tp", None),
            P("tp", None),
        ),
        check_vma=False,
    )
```

```python
import functools

import jax
import jax.numpy as jnp
from jax import lax
from jax.experimental import pallas as pl
from jax.experimental.pallas import tpu as pltpu
from jax.sharding import PartitionSpec as P

HD = 128
NS = 16
CTX = 128


eps_norm = 1e-06
neg_big = -1e30
LOG2E = 1.4426950408889634
MESH = pl.DeviceIdType.MESH
VM = pltpu.VMEM
BF = jnp.bfloat16
F32 = jnp.float32
NT = (((1,), (1,)), ((), ()))
TN = (((0,), (0,)), ((), ()))
NN = (((1,), (0,)), ((), ()))


def dot(left, right, dims=NN):
    return lax.dot_general(left, right, dims, preferred_element_type=F32)


def vmem_specs(count):
    return [pl.BlockSpec(memory_space=VM)] * count


def tp_peers():
    me = lax.axis_index("tp")
    mate = me + 1 - 2 * lax.rem(me, 2)
    return me, mate, lax.rem(me + 2, 4), lax.rem(mate + 2, 4)


def flag_rows(keep):
    rest = jnp.zeros((NS - keep.shape[0], keep.shape[1]), F32)
    return jnp.concatenate([keep[...], rest], axis=0).astype(BF)


def remote(src, dst, send, recv, **where):
    return pltpu.make_async_remote_copy(
        src_ref=src,
        dst_ref=dst,
        send_sem=send,
        recv_sem=recv,
        device_id=where,
        device_id_type=MESH,
    )


def greet(n, with_seq):
    s = lax.axis_index("seq")
    barrier = pltpu.get_barrier_semaphore()
    for peer in tp_peers()[1:]:
        pl.semaphore_signal(barrier, inc=1, device_id={"tp": peer}, device_id_type=MESH)
    if with_seq:
        for k in range(1, n):
            pl.semaphore_signal(
                barrier, inc=1, device_id={"seq": lax.rem(s + k, n)}, device_id_type=MESH
            )


def greeted(n, with_seq):
    pl.semaphore_wait(pltpu.get_barrier_semaphore(), 3 + (n - 1 if with_seq else 0))


class Fetch:
    def __init__(self, names, refs, held, sems):
        self.copies = {
            name: pltpu.make_async_copy(ref, held[name], sems.at[i])
            for i, (name, ref) in enumerate(zip(names, refs))
        }
        self.ready = set()
        for c in self.copies.values():
            c.start()

    def need(self, *wanted):
        for name in wanted:
            if name not in self.ready:
                self.copies[name].wait()
                self.ready.add(name)


class Gather:
    def __init__(self, ref, send, recv):
        rows = ref.shape[0] // 4
        me, mate, across, _ = tp_peers()

        def give(slot, quarter, peer):
            part = ref.at[pl.ds(pl.multiple_of(quarter * rows, rows), rows), :]
            return remote(part, part, send.at[slot], recv.at[slot], tp=peer)

        self.cross = give(1, me, across)
        self.side = give(0, me, mate)
        self.relay = give(2, across, mate)

    def start(self):
        self.cross.start()
        self.side.start()

    def near(self):
        self.side.wait_recv()

    def pass_on(self):
        self.cross.wait_recv()
        self.relay.start()

    def far(self):
        self.relay.wait_recv()

    def finish(self):
        for c in (self.side, self.cross, self.relay):
            c.wait_send()


class Scatter:
    def __init__(self, ref, over, into, send, recv):
        self.ref, self.over, self.into = ref, over, into
        self.rows = ref.shape[0] // 4
        self.me, self.mate, self.across, self.diag = tp_peers()
        self.hop = [
            remote(self.quarter(self.diag), into.at[0], send.at[0], recv.at[0], tp=self.mate),
            remote(self.quarter(self.mate), into.at[1], send.at[1], recv.at[1], tp=self.mate),
            remote(over, into.at[2], send.at[2], recv.at[2], tp=self.across),
        ]

    def span(self, quarter):
        return pl.ds(pl.multiple_of(quarter * self.rows, self.rows), self.rows)

    def quarter(self, quarter):
        return self.ref.at[self.span(quarter), :]

    def start(self):
        self.hop[0].start()
        self.hop[1].start()

    def turn(self):
        self.hop[0].wait_recv()
        mine = self.ref[self.span(self.across), :].astype(F32)
        self.over[...] = (mine + self.into[0].astype(F32)).astype(BF)
        self.hop[2].start()

    def end(self):
        self.hop[1].wait_recv()
        value = self.ref[self.span(self.me), :].astype(F32) + self.into[1].astype(F32)
        self.hop[2].wait_recv()
        value = value + self.into[2].astype(F32)
        for c in self.hop:
            c.wait_send()
        return value


FORWARD_IN = (
    "tok",
    "gain",
    "wk",
    "wv",
    "wq",
    "rate",
    "cin",
    "cout",
    "flag",
    "init",
    "ogm",
    "w_out",
    "mid",
    "w_up",
    "w_down",
)


class Save:
    def __init__(self, sems):
        self.sems, self.copies = sems, []

    def __call__(self, src, dst):
        self.copies.append(pltpu.make_async_copy(src, dst, self.sems.at[len(self.copies)]))
        self.copies[-1].start()

    def finish(self):
        for c in self.copies:
            c.wait()


def forward_kernel(n, refs_in, outs, held, scr):
    s = lax.axis_index("seq")
    me, mate, across, diag = tp_peers()
    og = scr["og"]
    own_rows = og.shape[1] // 4
    own = pl.ds(pl.multiple_of(me * own_rows, own_rows), own_rows)
    held = dict(held, ogm=og.at[:, own, :])
    fetch = Fetch(FORWARD_IN, refs_in, held, scr["fetch"])
    nf_d, q_d, k_d, v_d, ctx_d, keep_d, start_o, end_o = outs[:8]
    nf, q_o, k_o, v_o, ctx_o = (scr[x] for x in ("nf", "q", "k", "v", "ctxa"))
    save = Save(scr["save"])
    grad_gathers = [Gather(og.at[m], scr["os"].at[m], scr["or"].at[m]) for m in range(2)]
    tok, rate, flag, init = (held[x] for x in ("tok", "rate", "flag", "init"))
    keep = scr["keep"]
    wq, wk, wv = held["wq"], held["wk"], held["wv"]
    u_s, gath, pay, y_s, ctx_s = (scr[x] for x in ("u", "gath", "pay", "y", "ctx"))
    block = nf.shape[1]
    rows = block // 4
    chan = rate.shape[1]
    gath[...] = jnp.zeros_like(gath)

    @pl.when(s == 0)
    def _():
        k_o[:, 0 : CTX + block, :] = jnp.zeros((2, CTX + block, chan), BF)
        v_o[:, 0 : CTX + block, :] = jnp.zeros((2, CTX + block, chan), BF)
        ctx_o[...] = jnp.zeros_like(ctx_o)

    greet(n, True)

    def span(quarter):
        return pl.ds(pl.multiple_of(quarter * rows, rows), rows)

    def lanes(part):
        return pl.ds(pl.multiple_of(part * chan, chan), chan)

    fetch.need("tok", "gain")
    x = tok[...].astype(F32).reshape(2 * rows, -1)
    normed = x * lax.rsqrt(jnp.mean(x * x, axis=-1, keepdims=True) + eps_norm) * held["gain"][...]
    nf[:, span(me), :] = normed.astype(BF).reshape(2, rows, -1)
    greeted(n, True)

    def give(slot, quarter, peer, part=None):
        cols = slice(None) if part is None else lanes(part)
        ref = nf.at[:, span(quarter), cols]
        return remote(ref, ref, scr["ts"].at[slot], scr["tr"].at[slot], tp=peer)

    cross = [give(1 + i, me, across, part) for i, part in enumerate((across, diag, me, mate))]
    relay = [give(5 + i, across, mate, part) for i, part in enumerate((me, mate, across, diag))]
    side = give(0, me, mate)
    for c in cross:
        c.start()
    side.start()

    def pass_kv(slot, src, half):
        high = 2 * rows
        part = pl.ds(pl.multiple_of(CTX + half * high, rows), high)
        own = pl.ds(pl.multiple_of(CTX + block + half * high, rows), high)
        return remote(
            src.at[:, own, :],
            src.at[:, part, :],
            scr["kvs"].at[slot],
            scr["kvr"].at[slot],
            seq=lax.rem(s + 1, n),
        )

    def qkv(order, half):
        high = 2 * rows
        here = pl.ds(pl.multiple_of(half * high, high), high)
        part = nf[:, here, :].reshape(2 * high, -1)
        own = pl.ds(pl.multiple_of(CTX + block + half * high, rows), high)
        k_o[:, own, :] = dot(part, wk[...]).astype(BF).reshape(2, high, chan)
        v_o[:, own, :] = dot(part, wv[...]).astype(BF).reshape(2, high, chan)

        @pl.when(s < n - 1)
        def _():
            pass_kv(2 * order, k_o, half).start()
            if order == 0:
                pass_kv(1, v_o, half).start()

        q_o[:, here, :] = dot(part, wq[...]).astype(BF).reshape(2, high, chan)

    near = me // 2
    side.wait_recv()
    fetch.need("wk", "wv", "wq")
    qkv(0, near)
    cross[0].wait_recv()
    cross[1].wait_recv()
    relay[1].start()
    relay[0].start()
    relay[1].wait_recv()
    fetch.need("rate", "cin", "cout", "flag", "init")
    for m in range(2):
        keep[m : m + 1, :] = jnp.broadcast_to(1.0 - flag[m : m + 1, :].astype(F32), (1, chan))
    save(keep, keep_d)
    cols = lanes(me)
    for m in range(2):
        u_s[m] = nf[m, :, cols].astype(F32)
    decay = jnp.exp(-rate[...])
    drive = jnp.sqrt(1.0 - decay * decay) * held["cin"][...]

    def run(i, state):
        base = pl.multiple_of(i * 8, 8)
        state = list(state)
        for k in range(8):
            for m in range(2):
                state[m] = decay * state[m] + drive * u_s[m, pl.ds(base + k, 1), :]
        return tuple(state)

    zero = jnp.zeros((NS, chan), F32)
    late = lax.fori_loop(0, (block - CTX) // 8, run, (zero, zero))
    last_state = lax.fori_loop((block - CTX) // 8, block // 8, run, late)
    for m in range(2):
        pay[m * NS : (m + 1) * NS] = last_state[m].astype(BF)
    pay[2 * NS : 3 * NS] = flag_rows(keep)

    def spread(k):
        return remote(
            pay, gath.at[k], scr["gs"].at[k], scr["gr"].at[k], seq=lax.rem(s + k, n)
        )

    for k in range(1, n):

        @pl.when(s + k < n)
        def _():
            spread(k).start()

    for i in (2, 3):
        cross[i].wait_recv()
        relay[i].start()
    for i in (0, 2, 3):
        relay[i].wait_recv()
    fetch.need("ogm")
    for g in grad_gathers:
        g.start()
    qkv(1, 1 - near)
    save(nf, nf_d)
    save(q_o, q_d)

    whole = jnp.exp(-rate[...] * block)
    for k in range(1, n):

        @pl.when(s >= k)
        def _():
            spread(k).wait_recv()

    def entry(begin_keep, end, b):
        return tuple(jnp.where(b == 0, init[m], begin_keep[m] * end[m]) for m in range(2))

    def chain(b, end):
        k = jnp.maximum(s - b, 0)
        got = gath[k].astype(F32)
        begin = entry((got[2 * NS : 2 * NS + 1], got[2 * NS + 1 : 2 * NS + 2]), end, b)
        new = tuple(got[m * NS : (m + 1) * NS] + whole * begin[m] for m in range(2))
        return tuple(jnp.where(b < s, new[m], end[m]) for m in range(2))

    end = lax.fori_loop(0, n - 1, chain, (zero, zero))
    begin = entry((keep[0:1, :], keep[1:2, :]), end, s)
    toward = jnp.exp(-rate[...] * (block - CTX))
    state = tuple(late[m] + toward * begin[m] for m in range(2))
    out_c = held["cout"][...]

    def run_out(i, state):
        base = pl.multiple_of(block - CTX + i * 8, 8)
        row = pl.multiple_of(i * 8, 8)
        state = list(state)
        for k in range(8):
            for m in range(2):
                state[m] = decay * state[m] + drive * u_s[m, pl.ds(base + k, 1), :]
                y_s[m, pl.ds(row + k, 1), :] = jnp.sum(out_c * state[m], axis=0, keepdims=True)
        return tuple(state)

    state = lax.fori_loop(0, CTX // 8, run_out, state)
    ctx_s[...] = y_s[...].astype(BF)
    down = remote(
        ctx_s, ctx_o.at[:, :, cols], scr["cs"].at[0], scr["cr"].at[0], seq=lax.rem(s + 1, n)
    )

    @pl.when(s < n - 1)
    def _():
        down.start()
        pass_kv(3, v_o, 1 - near).start()

    for m in range(2):
        start_o[m] = begin[m]
        end_o[m] = last_state[m] + whole * begin[m]
    for g in grad_gathers:
        g.near()
        g.pass_on()

    @pl.when(s > 0)
    def _():
        down.wait_recv()
        theirs = lanes(across)
        shares = [
            remote(
                ctx_o.at[:, :, part],
                ctx_o.at[:, :, part],
                scr["cs"].at[1 + i],
                scr["cr"].at[1 + i],
                tp=peer,
            )
            for i, (part, peer) in enumerate(((cols, across), (cols, mate), (theirs, mate)))
        ]
        shares[0].start()
        shares[1].start()
        shares[0].wait_recv()
        shares[2].start()
        shares[1].wait_recv()
        shares[2].wait_recv()
        flat = ctx_o[...].reshape(2 * CTX, -1)
        k_o[:, 0:CTX, :] = dot(flat, wk[...]).astype(BF).reshape(2, CTX, chan)
        v_o[:, 0:CTX, :] = dot(flat, wv[...]).astype(BF).reshape(2, CTX, chan)
        for order, half in enumerate((near, 1 - near)):
            pass_kv(2 * order, k_o, half).wait_recv()
            pass_kv(2 * order + 1, v_o, half).wait_recv()
        for c in shares:
            c.wait_send()

    save(k_o, k_d)
    save(v_o, v_d)
    save(ctx_o, ctx_d)
    forward_middle(fetch, held, scr, outs[8:], save, q_o, k_o, v_o, og, grad_gathers)

    @pl.when(s < n - 1)
    def _():
        down.wait_send()
        for order, half in enumerate((near, 1 - near)):
            pass_kv(2 * order, k_o, half).wait_send()
            pass_kv(2 * order + 1, v_o, half).wait_send()

    for k in range(1, n):

        @pl.when(s + k < n)
        def _():
            spread(k).wait_send()

    for c in [side] + cross + relay:
        c.wait_send()
    for g in grad_gathers:
        g.finish()
    save.finish()


def launch(
    body, names, args, outs, out_vmem, scratch, collective_id, limit, name, placed=()
):
    keys = list(scratch)
    count = len(names)
    plain = [name for name in names if name not in placed]

    def kernel(*refs):
        refs_in, refs = refs[:count], refs[count:]
        outs_r, refs = refs[: len(outs)], refs[len(outs) :]
        held, refs = dict(zip(plain, refs)), refs[len(plain) :]
        body(refs_in, outs_r, held, dict(zip(keys, refs)))

    scratch = dict(scratch)
    return pl.pallas_call(
        kernel,
        out_shape=tuple(outs),
        in_specs=[pl.BlockSpec(memory_space=pl.ANY)] * count,
        out_specs=tuple(
            pl.BlockSpec(memory_space=VM if in_vmem else pl.ANY) for in_vmem in out_vmem
        ),
        scratch_shapes=[VM(a.shape, a.dtype) for x, a in zip(names, args) if x in plain]
        + list(scratch.values()),
        compiler_params=pltpu.CompilerParams(
            collective_id=collective_id, has_side_effects=True, vmem_limit_bytes=limit << 20
        ),
        name=name,
    )(*args)


def rms_back(x, gain, grad):
    inv = lax.rsqrt(jnp.mean(x * x, axis=-1, keepdims=True) + eps_norm)
    unit = x * inv
    scaled = grad * gain
    gain_grad = jnp.sum(grad * unit, axis=0, keepdims=True)
    return inv * (scaled - unit * jnp.mean(scaled * unit, axis=-1, keepdims=True)), gain_grad


def forward_middle(fetch, held, scr, outs, save, q, k, v, og, grad_gathers):
    nm, pm, dm, hid, dpre = (scr[x] for x in ("nm", "pm", "dm", "hid", "dpre"))
    mlp_o, h1_o, ffn_o, att, lse = (scr[x] for x in ("mlp", "h1", "ffn", "att", "lse"))
    w_out, tok, gain, w_up, w_down = (
        held[x] for x in ("w_out", "tok", "mid", "w_up", "w_down")
    )
    keep = scr["keep"]
    me = tp_peers()[0]
    near = me // 2
    block = q.shape[1]
    rows = block // 4
    width = w_out.shape[1]
    tile = 256
    panels = w_up.shape[1] // tile
    own = pl.ds(pl.multiple_of(me * rows, rows), rows)
    edge0 = k.shape[1] - block
    half = block // 2
    row_ids = lax.broadcasted_iota(jnp.int32, (half, half), 0)
    col_ids = lax.broadcasted_iota(jnp.int32, (half, half), 1)
    scale = HD ** (-0.5) * LOG2E

    def attend(m):
        def one(head, c):
            lanes = pl.ds(pl.multiple_of(head * HD, HD), HD)
            shut = (keep[m : m + 1, 0:half] - 1.0) * -neg_big
            for part in range(2):
                mine = slice(part * half, (part + 1) * half)
                edge = edge0 + part * half
                sc = dot(k[m, 0 : edge + half, lanes], q[m, mine, lanes], NT) * scale
                pieces = [sc[:edge0] + shut]
                if part:
                    pieces.append(sc[edge0:edge])
                pieces.append(jnp.where(row_ids <= col_ids, sc[edge:], neg_big))
                sc = jnp.concatenate(pieces, axis=0)
                top = jnp.max(sc, axis=0, keepdims=True)
                expo = jnp.exp2(sc - top)
                total = jnp.sum(expo, axis=0, keepdims=True)
                res = dot(v[m, 0 : edge + half, lanes], expo.astype(BF), TN) * (1.0 / total)
                att[m, mine, lanes] = res.T.astype(BF)
                lse[m, head, :, mine] = top + LOG2E * jnp.log(total)
            return c

        lax.fori_loop(0, q.shape[2] // HD, one, 0)

    def scatter(kind, m, ref):
        at = 2 * kind + m
        return Scatter(
            ref.at[m], scr["over"].at[at], scr["into"].at[at], scr["ss"].at[at], scr["sr"].at[at]
        )

    mlp_d, h1_d, dm_d, ffn_d, att_d, lse_d = outs
    sums1 = [scatter(0, m, pm) for m in range(2)]
    gathers = [Gather(nm.at[m], scr["mgs"].at[m], scr["mgr"].at[m]) for m in range(2)]

    def project(m):
        def one(j, c):
            cols = pl.ds(pl.multiple_of(j * tile, tile), tile)
            pm[m, :, cols] = dot(att[m], w_out[:, cols]).astype(BF)
            return c

        lax.fori_loop(0, width // tile, one, 0)

    def residual(m):
        h1 = tok[m].astype(F32) + sums1[m].end()
        h1_o[m] = h1
        inv = lax.rsqrt(jnp.mean(h1 * h1, axis=-1, keepdims=True) + eps_norm)
        nm[m, own, :] = (h1 * inv * gain[...]).astype(BF)
        gathers[m].start()

    def feed(m, part):
        here = pl.ds(pl.multiple_of(part * half, half), half)
        flat = pl.ds(pl.multiple_of(m * block + part * half, half), half)

        def panel(j, c):
            cols = pl.ds(pl.multiple_of(j * tile, tile), tile)
            pre = dot(nm[m, here, :], w_up[:, cols])
            sq = pre * pre
            t = jnp.tanh((0.7978845608028654 * pre) * (1.0 + 0.044715 * sq))
            hid[flat, cols] = (0.5 * pre * (1.0 + t)).astype(BF)
            slope = 0.5 * (1.0 + t) + (0.3989422804014327 * pre) * (1.0 - t * t) * (
                1.0 + 0.134145 * sq
            )
            dpre[flat, cols] = (slope * dot(og[m, here, :], w_down[cols, :], NT)).astype(BF)
            return c

        lax.fori_loop(0, panels, panel, 0)

        def back(j, c):
            cols = pl.ds(pl.multiple_of(j * tile, tile), tile)
            dm[m, here, cols] = dot(dpre[flat, :], w_up[cols, :], NT).astype(BF)
            return c

        lax.fori_loop(0, width // tile, back, 0)

    def lower(m, part):
        here = pl.ds(pl.multiple_of(part * half, half), half)
        flat = pl.ds(pl.multiple_of(m * block + part * half, half), half)

        def one(j, c):
            cols = pl.ds(pl.multiple_of(j * tile, tile), tile)
            mlp_o[m, here, cols] = dot(hid[flat, :], w_down[:, cols]).astype(BF)
            return c

        lax.fori_loop(0, width // tile, one, 0)

    attend(0)
    fetch.need("w_out")
    project(0)
    sums1[0].start()
    sums1[0].turn()
    attend(1)
    project(1)
    save(att, att_d)
    save(lse, lse_d)
    sums1[1].start()
    sums1[1].turn()
    fetch.need("mid")
    residual(0)
    fetch.need("w_up", "w_down")
    for g in grad_gathers:
        g.far()
    gathers[0].near()
    feed(0, near)
    residual(1)
    save(h1_o, h1_d)
    gathers[0].pass_on()
    gathers[1].near()
    feed(1, near)
    lower(0, near)
    lower(1, near)
    gathers[0].far()
    feed(0, 1 - near)
    save(dm.at[0], dm_d.at[0])
    gathers[1].pass_on()
    gathers[1].far()
    feed(1, 1 - near)
    save(dm.at[1], dm_d.at[1])

    def down_sum(i, c):
        left = hid[:, pl.ds(pl.multiple_of(i * tile, tile), tile)].T
        for j in range(width // tile):
            right = og[:, :, j * tile : (j + 1) * tile].reshape(2 * block, tile)
            at = pl.multiple_of((width // tile + j) * panels * tile + i * tile, tile)
            ffn_o[pl.ds(at, tile), :] = dot(left, right).astype(BF)
        return c

    def up_sum(i, c):
        left = nm[:, :, pl.ds(pl.multiple_of(i * tile, tile), tile)].reshape(2 * block, tile).T
        for j in range(panels):
            at = pl.multiple_of(j * width + i * tile, tile)
            ffn_o[pl.ds(at, tile), :] = dot(left, dpre[:, j * tile : (j + 1) * tile]).astype(BF)
        return c

    high = panels * tile * (width // tile)
    lax.fori_loop(0, panels, down_sum, 0)
    save(ffn_o.at[high : 2 * high], ffn_d.at[high : 2 * high])
    lower(0, 1 - near)
    lower(1, 1 - near)
    save(mlp_o, mlp_d)
    lax.fori_loop(0, width // tile, up_sum, 0)
    save(ffn_o.at[0:high], ffn_d.at[0:high])
    for m in range(2):
        gathers[m].finish()


def forward(*args):
    n = lax.axis_size("seq")
    by = dict(zip(FORWARD_IN, args))
    micro, rows, width = by["tok"].shape
    block = 4 * rows
    chan = by["rate"].shape[1]
    units = by["w_up"].shape[1]
    keys = CTX + 2 * block
    sds = jax.ShapeDtypeStruct
    dma = pltpu.SemaphoreType.DMA
    results = dict(
        nf=sds((micro, block, width), BF),
        q=sds((micro, block, chan), BF),
        k=sds((micro, keys, chan), BF),
        v=sds((micro, keys, chan), BF),
        ctxa=sds((micro, CTX, width), BF),
        keep=sds((micro, chan), F32),
        start=sds((micro, NS, chan), F32),
        end=sds((micro, NS, chan), F32),
        mlp=sds((micro, block, width), BF),
        h1=sds((micro, rows, width), F32),
        dm=sds((micro, block, width), BF),
        ffn=sds((2 * units * width // 256, 256), BF),
        att=sds((micro, block, chan), BF),
        lse=sds((micro, chan // HD, 1, block), F32),
    )
    in_vmem = ("start", "end")
    scratch = {x: VM(a.shape, a.dtype) for x, a in results.items() if x not in in_vmem}
    scratch.update(
        og=VM((micro, block, width), BF),
        fetch=dma((len(FORWARD_IN),)),
        save=dma((16,)),
        os=dma((2, 3)),
        u=VM((micro, block, chan), F32),
        gath=VM((n, 3 * NS, chan), BF),
        pay=VM((3 * NS, chan), BF),
        y=VM((micro, CTX, chan), F32),
        ctx=VM((micro, CTX, chan), BF),
        ts=dma((9,)),
        tr=dma((9,)),
        kvs=dma((4,)),
        kvr=dma((4,)),
        gs=dma((n,)),
        gr=dma((n,)),
        cs=dma((4,)),
        cr=dma((4,)),
        nm=VM((micro, block, width), BF),
        pm=VM((micro, block, width), BF),
        hid=VM((micro * block, units), BF),
        dpre=VM((micro * block, units), BF),
        over=VM((2, rows, width), BF),
        into=VM((2, 3, rows, width), BF),
        ss=dma((2, 3)),
        sr=dma((2, 3)),
        mgs=dma((2, 3)),
        mgr=dma((2, 3)),
    )
    scratch["or"] = dma((2, 3))
    return launch(
        functools.partial(forward_kernel, n),
        FORWARD_IN,
        args,
        tuple(results.values()),
        [x in in_vmem for x in results],
        scratch,
        0,
        62,
        "forward",
        ("ogm",),
    )


class Ring:
    def __init__(self, n, x, recv, send_sem, recv_sem):
        self.n, self.x, self.recv = n, x, recv
        self.send_sem, self.recv_sem = send_sem, recv_sem
        self.subs, self.rows = recv.shape[2], recv.shape[3]
        s = lax.axis_index("seq")
        half = n // 2
        self.r = jnp.where(lax.rem(s, 2) == 0, s // 2, n - 1 - s // 2)

        def dev(q):
            q = lax.rem(q + n, n)
            return jnp.where(q < half, 2 * q, 2 * (n - 1 - q) + 1)

        self.target = (dev(self.r + 1), dev(self.r - 1))
        self.done = 0
        self.total = 2 * n - 2

    def chunk(self, d, b, off):
        sign = (1, -1)[d]
        c = lax.rem(self.r + sign * off + 2 * self.n, self.n)
        at = ((d * self.n + c) * self.subs + b) * self.rows
        return pl.ds(pl.multiple_of(at, self.rows), self.rows)

    def copy(self, d, b, src, dst, k):
        return pltpu.make_async_remote_copy(
            src_ref=src,
            dst_ref=dst,
            send_sem=self.send_sem.at[d, b, k],
            recv_sem=self.recv_sem.at[d, b, k],
            device_id={"seq": self.target[d]},
            device_id_type=MESH,
        )

    def first(self, d, b):
        return self.copy(d, b, self.x.at[self.chunk(d, b, 0)], self.recv.at[d, 0, b], 0)

    def sums(self, d, b, k):
        prior = jnp.maximum(k - 1, 0)
        return self.copy(d, b, self.recv.at[d, prior, b], self.recv.at[d, k, b], k)

    def alls(self, d, b, k):
        ref = self.x.at[self.chunk(d, b, 1 - k)]
        return self.copy(d, b, ref, ref, self.n - 1 + k)

    def each(self):
        return [(d, b) for b in range(self.subs) for d in range(2)]

    def add(self, d, b, k):
        mine = self.x[self.chunk(d, b, -k - 1)]
        return (self.recv[d, k, b].astype(F32) + mine.astype(F32)).astype(BF)

    def start(self):
        for d, b in self.each():
            self.first(d, b).start()

    def tick(self, t):
        n = self.n

        def leave():
            for d, b in self.each():
                self.first(d, b).wait_send()

        def sum_step():
            for d, b in self.each():
                self.sums(d, b, t).wait_recv()
                self.recv[d, t, b] = self.add(d, b, t)
                self.sums(d, b, t + 1).start()

        def turn():
            for d, b in self.each():
                self.sums(d, b, n - 2).wait_recv()
                self.x[self.chunk(d, b, 1)] = self.add(d, b, n - 2)
                self.alls(d, b, 0).start()

        def all_step():
            k = t - (n - 1)
            for d, b in self.each():
                self.alls(d, b, k).wait_recv()
                self.alls(d, b, k + 1).start()

        def close():
            for d, b in self.each():
                self.alls(d, b, n - 2).wait_recv()

        steps = (
            (t == 0, leave),
            (t < n - 2, sum_step),
            (t == n - 2, turn),
            ((t > n - 2) & (t < 2 * n - 3), all_step),
            (t == 2 * n - 3, close),
        )
        for when, step in steps:
            if isinstance(t, int):
                if when:
                    step()
            else:
                pl.when(when)(step)

    def go(self, fourteenths):
        upto = min(-(-fourteenths * self.total // 14), self.total)
        if upto - self.done == 1:
            self.tick(self.done)
        elif upto > self.done:

            def one(t, c):
                self.tick(t)
                return c

            lax.fori_loop(self.done, upto, one, 0)
        self.done = max(upto, self.done)

    def drain(self):
        def more(k, c):
            for d, b in self.each():
                self.sums(d, b, k + 1).wait_send()
                self.alls(d, b, k).wait_send()
            return c

        lax.fori_loop(0, self.n - 2, more, 0)
        for d, b in self.each():
            self.alls(d, b, self.n - 2).wait_send()


LAST_IN = (
    "q",
    "k",
    "v",
    "lse",
    "att",
    "w_out",
    "nf",
    "ctx",
    "wq",
    "wk",
    "wv",
    "rate",
    "cin",
    "cout",
    "start",
    "keep",
    "endg",
    "mlp",
    "h1",
    "dm",
    "ogm",
    "mid",
    "tok",
    "gain",
    "ffn",
)


def last_kernel(n, refs_in, outs, h, scr):
    x1, x2, x3 = scr["x1"], scr["x2"], scr["x3"]
    ffn_rows = refs_in[LAST_IN.index("ffn")].shape[0]
    h = dict(h, ffn=x1.at[0:ffn_rows])
    fetch = Fetch(LAST_IN, refs_in, h, scr["fetch"])
    need = fetch.need
    mixed_o, tg_o, sum1_o, sum2_o, rate_o, cin_o, cout_o, norm_o, mid_o = outs
    s = lax.axis_index("seq")
    me, mate, across, diag = tp_peers()
    peers = (mate, across, diag)
    nf, rate, tok = h["nf"], h["rate"], h["tok"]
    block = nf.shape[1]
    rows = block // 4
    width = nf.shape[2]
    chan = rate.shape[1]
    rk, rv, gath, dcr = scr["rk"], scr["rv"], scr["gath"], scr["dcr"]
    gath[...] = jnp.zeros_like(gath)
    if x1.shape[0] > ffn_rows:
        x1[ffn_rows:] = jnp.zeros((x1.shape[0] - ffn_rows, chan), BF)
    used2 = 4 * width
    if x2.shape[0] > used2:
        x2[used2:] = jnp.zeros((x2.shape[0] - used2, chan), BF)
    x3[...] = jnp.zeros_like(x3)

    @pl.when(s == n - 1)
    def _():
        rk[...] = jnp.zeros_like(rk)
        rv[...] = jnp.zeros_like(rv)
        dcr[...] = jnp.zeros_like(dcr)

    greet(n, True)
    before = lax.rem(s + n - 1, n)
    own = pl.ds(pl.multiple_of(me * rows, rows), rows)

    def to_before(sem, slot, src, dst):
        return remote(
            src, dst, scr["send_k"].at[sem, slot], scr["recv_k"].at[sem, slot], seq=before
        )

    ring1 = Ring(n, x1, scr["r1"], scr["s1s"], scr["s1r"])
    ring2 = Ring(n, x2, scr["r2"], scr["s2s"], scr["s2r"])
    ring3 = Ring(n, x3, scr["r3"], scr["s3s"], scr["s3r"])
    rr, da, dh1, mlp, h1 = scr["rr"], scr["da"], scr["dh1"], h["mlp"], h["h1"]

    def scatter(ref, at, m):
        at = 2 * at + m
        return Scatter(
            ref.at[m], scr["over"].at[at], scr["into"].at[at], scr["ss"].at[at], scr["sr"].at[at]
        )

    mid_sums = [scatter(h["dm"], 0, m) for m in range(2)]
    gathers = [Gather(rr.at[m], scr["rs"].at[m], scr["rrv"].at[m]) for m in range(2)]
    need("dm")
    greeted(n, True)
    for c in mid_sums:
        c.start()
    need("ffn")
    ring1.start()
    for c in mid_sums:
        c.turn()
    need("h1", "ogm", "mid")
    mid_grad = jnp.zeros((1, width), F32)
    for m in range(2):
        back, one = rms_back(h1[m], h["mid"][...], mid_sums[m].end())
        mid_grad = mid_grad + one
        dh1[m] = h["ogm"][m].astype(F32) + back
        rr[m, own, :] = dh1[m].astype(BF)
        gathers[m].start()
        ring1.go(m + 1)
    need("w_out", "q", "k", "v", "lse", "keep")

    q, k, v, lse, keep, w_out = (h[name] for name in ("q", "k", "v", "lse", "keep", "w_out"))
    edge0 = k.shape[1] - block
    half = block // 2
    row_ids = lax.broadcasted_iota(jnp.int32, (half, half), 0)
    col_ids = lax.broadcasted_iota(jnp.int32, (half, half), 1)
    scale = HD ** (-0.5)
    dq_s, dko, dvo, dkc, dvc = (scr[x] for x in ("dq", "dko", "dvo", "dkc", "dvc"))
    dkp, dvp, ak, av = (scr[x] for x in ("dkp", "dvp", "ak", "av"))

    def attend_one(m, head):
        i = 2 * m + head
        lanes = pl.ds(pl.multiple_of(head * HD, HD), HD)
        shut = (keep[pl.ds(m, 1), 0:half] - 1.0) * -neg_big
        for part in (1, 0):
            mine = slice(part * half, (part + 1) * half)
            edge = edge0 + part * half
            qq = q[m, mine, lanes]
            kk = k[m, 0 : edge + half, lanes]
            dd = da[m, mine, lanes]
            sc = dot(kk, qq, NT) * (scale * LOG2E)
            pieces = [sc[:edge0] + shut]
            if part:
                pieces.append(sc[edge0:edge])
            pieces.append(jnp.where(row_ids <= col_ids, sc[edge:], neg_big))
            sc = jnp.concatenate(pieces, axis=0)
            probs = jnp.exp2(sc - lse[m, head, :, mine])
            dp = dot(v[m, 0 : edge + half, lanes], dd, NT)
            spread_sum = jnp.sum(probs * dp, axis=0, keepdims=True)
            ds = (probs * (dp - spread_sum)).astype(BF)
            dq_s[m, mine, lanes] = (dot(kk, ds, TN) * scale).T.astype(BF)
            dk = dot(ds, qq) * scale
            dv = dot(probs.astype(BF), dd)
            if part:
                ak[...] = dk
                av[...] = dv
            else:
                ak[0 : edge + half] += dk
                av[0 : edge + half] += dv
        for acc, far, prev, own in ((ak, dkc, dkp, dko), (av, dvc, dvp, dvo)):
            far[m, :, lanes] = acc[0:CTX].astype(BF)
            prev[i] = acc[CTX:edge0].astype(BF)
            own[m, :, lanes] = acc[edge0:]

        @pl.when(s > 0)
        def _():
            to_before(0, i, dkp.at[i], rk.at[i]).start()
            to_before(1, i, dvp.at[i], rv.at[i]).start()

    def stream_back(m, c):
        g = Gather(rr.at[m], scr["rs"].at[m], scr["rrv"].at[m])
        g.near()
        g.pass_on()
        g.far()
        ring1.tick(m + ring1.done)
        da[m] = dot(rr[m], w_out[...], NT).astype(BF)

        def heads(head, c):
            attend_one(m, head)
            return c

        lax.fori_loop(0, chan // HD, heads, 0)
        return c

    lax.fori_loop(0, 2, stream_back, 0)
    ring1.done += 2

    cp, cr, dcs = scr["cp"], scr["cr"], scr["dcs"]
    wq, wk, wv = h["wq"], h["wk"], h["wv"]
    need("wq", "wk", "wv")
    ctx_part = dot(dkc[...].reshape(2 * CTX, chan), wk[...], NT) + dot(
        dvc[...].reshape(2 * CTX, chan), wv[...], NT
    )
    for j in range(4):
        cp[j] = ctx_part[:, j * chan : (j + 1) * chan].astype(BF).reshape(2, CTX, chan)

    def to_peer(i, src, dst, kind):
        return remote(
            src, dst, scr["send_c"].at[kind, i], scr["recv_c"].at[kind, i], tp=peers[i]
        )

    ctx_out = [to_peer(i, cp.at[peers[i]], cr.at[i], 0) for i in range(3)]
    for c in ctx_out:
        c.start()
    need("mlp")
    mlp_sums = [scatter(mlp, 1, m) for m in range(2)]
    for c in mlp_sums:
        c.start()
    ring1.go(5)

    u_s, du_s, hist = scr["u"], scr["du"], scr["hist"]
    cols = pl.ds(pl.multiple_of(me * chan, chan), chan)
    need("nf", "rate", "cin", "cout", "start", "endg")
    for m in range(2):
        u_s[m] = nf[m, :, cols].astype(F32)
    decay = jnp.exp(-rate[...])
    root = jnp.sqrt(1.0 - decay * decay)
    drive = root * h["cin"][...]
    out_c = h["cout"][...]
    start, endg = h["start"], h["endg"]
    for m in range(2):
        hist[0, m] = start[m].astype(BF)

    def run(i, state):
        base = pl.multiple_of(i * 8, 8)
        state = list(state)
        for k in range(8):
            for m in range(2):
                state[m] = decay * state[m] + drive * u_s[m, pl.ds(base + k, 1), :]
                hist[base + k + 1, m] = state[m].astype(BF)
        return tuple(state)

    lax.fori_loop(0, block // 8, run, (start[0], start[1]))
    ctx_back = to_before(0, 4, dcs, dcr)
    total = cp[me].astype(F32)
    for i in range(3):
        ctx_out[i].wait_recv()
        total = total + cr[i].astype(F32)
    dcs[...] = total.astype(BF)

    @pl.when(s > 0)
    def _():
        ctx_back.start()

    for c in mlp_sums:
        c.turn()
    need("att")
    flat_att = h["att"][...].reshape(2 * block, chan).T
    tile = 256

    def proj(j, c):
        cols = pl.ds(pl.multiple_of(j * tile, tile), tile)
        right = rr[:, :, cols].reshape(2 * block, tile)
        at = pl.multiple_of(3 * width + j * tile, tile)
        x2[pl.ds(at, tile), :] = dot(flat_att, right).astype(BF)
        here = pl.ds(pl.multiple_of(j * tile, tile), tile)
        left = nf[:, :, here].reshape(2 * block, tile)
        x2[here, :] = dot(left, dq_s[...].reshape(2 * block, chan), TN).astype(BF)
        return c

    ring1.go(6)
    lax.fori_loop(0, width // tile, proj, 0)

    @pl.when(s < n - 1)
    def _():
        ctx_back.wait_recv()

    dy_s = scr["dy"]
    dy_s[...] = dcr[...].astype(F32)
    zero = jnp.zeros((NS, chan), F32)

    def early(i, grad):
        base = pl.multiple_of(CTX - 8 - i * 8, 8)
        grad = list(grad)
        for k in range(7, -1, -1):
            for m in range(2):
                grad[m] = decay * grad[m] + out_c * dy_s[m, pl.ds(base + k, 1), :]
        return tuple(grad)

    got = lax.fori_loop(0, CTX // 8, early, (zero, zero))
    reach = jnp.exp(-rate[...] * (block - CTX + 1.0))
    whole = jnp.exp(-rate[...] * block)
    pay = scr["pay"]
    for m in range(2):
        pay[m * NS : (m + 1) * NS] = (reach * got[m] + whole * endg[m]).astype(BF)
    pay[2 * NS : 3 * NS] = flag_rows(keep)

    def spread(k):
        return remote(
            pay,
            gath.at[k],
            scr["send_g"].at[k],
            scr["recv_g"].at[k],
            seq=lax.rem(s + n - k, n),
        )

    for k in range(1, n):

        @pl.when(s >= k)
        def _():
            spread(k).start()

    ring1.go(7)
    for m in range(2):
        mixed_o[m] = (h1[m] + mlp_sums[m].end()).astype(BF)
    @pl.when(s < n - 1)
    def _():
        for i in range(4):
            to_before(0, i, dkp.at[i], rk.at[i]).wait_recv()
            to_before(1, i, dvp.at[i], rv.at[i]).wait_recv()

    dk_b, dv_b = scr["dkb"], scr["dvb"]
    for m in range(2):
        for head in range(chan // HD):
            lanes = slice(head * HD, (head + 1) * HD)
            i = m * (chan // HD) + head
            dk_b[m, :, lanes] = (dko[m, :, lanes] + rk[i].astype(F32)).astype(BF)
            dv_b[m, :, lanes] = (dvo[m, :, lanes] + rv[i].astype(F32)).astype(BF)

    need("ctx")
    ctx = h["ctx"]

    def kv_grads(i, c):
        at = pl.multiple_of(i * tile, tile)
        here = pl.ds(at, tile)
        left = nf[:, :, here].reshape(2 * block, tile).T
        left_ctx = ctx[:, :, here].reshape(2 * CTX, tile).T
        for j, (own, far) in enumerate(((dk_b, dkc), (dv_b, dvc))):
            value = dot(left, own[...].reshape(2 * block, chan)) + dot(
                left_ctx, far[...].reshape(2 * CTX, chan)
            )
            x2[pl.ds((j + 1) * width + at, tile), :] = value.astype(BF)
        return c

    lax.fori_loop(0, width // tile, kv_grads, 0)
    ring2.start()
    ring1.go(8)
    for k in range(1, n):

        @pl.when(s + k < n)
        def _():
            spread(k).wait_recv()

    def chain(i, carry):
        k = n - 1 - i
        got = gath[k].astype(F32)
        valid = s + k < n
        return tuple(
            jnp.where(
                valid,
                got[2 * NS + m : 2 * NS + m + 1]
                * (got[m * NS : (m + 1) * NS] + whole * carry[m]),
                carry[m],
            )
            for m in range(2)
        )

    carry = lax.fori_loop(0, n - 1, chain, (zero, zero))
    grads0 = tuple(endg[m] + carry[m] for m in range(2))

    def back_late(i, val):
        hold, d_drive, d_decay, d_out = list(val[0:2]), val[2], val[3], val[4]
        low_row = pl.multiple_of(CTX - 8 - i * 8, 8)
        base = pl.multiple_of(block - 8 - i * 8, 8)
        for k in range(7, -1, -1):
            for m in range(2):
                dy = dy_s[m, pl.ds(low_row + k, 1), :]
                grad = hold[m] + out_c * dy
                du_s[m, pl.ds(base + k, 1), :] = jnp.sum(drive * grad, axis=0, keepdims=True)
                d_drive = d_drive + grad * u_s[m, pl.ds(base + k, 1), :]
                d_decay = d_decay + grad * hist[base + k, m].astype(F32)
                d_out = d_out + dy * hist[base + k + 1, m].astype(F32)
                hold[m] = decay * grad
        return hold[0], hold[1], d_drive, d_decay, d_out

    val = lax.fori_loop(0, CTX // 8, back_late, (grads0[0], grads0[1], zero, zero, zero))

    def back_early(i, val):
        hold, d_drive, d_decay = list(val[0:2]), val[2], val[3]
        base = pl.multiple_of(block - CTX - 8 - i * 8, 8)
        for k in range(7, -1, -1):
            for m in range(2):
                grad = hold[m]
                du_s[m, pl.ds(base + k, 1), :] = jnp.sum(drive * grad, axis=0, keepdims=True)
                d_drive = d_drive + grad * u_s[m, pl.ds(base + k, 1), :]
                d_decay = d_decay + grad * hist[base + k, m].astype(F32)
                hold[m] = decay * grad
        return hold[0], hold[1], d_drive, d_decay

    _, _, d_drive, d_decay = lax.fori_loop(0, (block - CTX) // 8, back_early, val[0:4])
    x3[0:NS] = (-decay * (d_decay - d_drive * h["cin"][...] * decay / root)).astype(BF)
    x3[NS : 2 * NS] = (d_drive * root).astype(BF)
    x3[2 * NS : 3 * NS] = val[4].astype(BF)
    ring3.start()
    ring1.go(9)
    ring2.go(1)
    part_s = scr["part"]

    def normed_part(i, c):
        m, part = i // 2, lax.rem(i, 2)
        here = pl.ds(pl.multiple_of(part * half, half), half)
        part_s[...] = (
            dot(dq_s[m, here, :], wq[...], NT)
            + dot(dk_b[m, here, :], wk[...], NT)
            + dot(dv_b[m, here, :], wv[...], NT)
        )
        part_s[:, cols] += du_s[m, here, :]
        mlp[m, here, :] = part_s[...].astype(BF)
        return c

    finals = [scatter(mlp, 0, m) for m in range(2)]
    for m in range(2):
        lax.fori_loop(2 * m, 2 * m + 2, normed_part, 0)
        finals[m].start()
    for c in finals:
        c.turn()
    ring1.go(10)
    ring2.go(2)
    ring3.go(1)
    need("tok", "gain")
    gain_grad = jnp.zeros((1, width), F32)
    for m in range(2):
        back, one = rms_back(tok[m].astype(F32), h["gain"][...], finals[m].end())
        tg_o[m] = dh1[m] + back
        gain_grad = gain_grad + one
    gp, gr, gs, gg = scr["gp"], scr["gr"], scr["gs"], scr["gg"]
    for j in range(4):
        gp[j, 0:1] = gain_grad[:, j * chan : (j + 1) * chan]
        gp[j, 1:2] = mid_grad[:, j * chan : (j + 1) * chan]
        gp[j, 2:8] = jnp.zeros((6, chan), F32)
    gains = [to_peer(i, gp.at[peers[i]], gr.at[i], 1) for i in range(3)]
    for c in gains:
        c.start()
    ring1.go(11)
    ring2.go(3)
    ring3.go(2)
    total = gp[me]
    for i in range(3):
        gains[i].wait_recv()
        total = total + gr[i]
    gs[...] = total

    def gain_out(k):
        return remote(
            gs,
            gg.at[k],
            scr["gain_s"].at[k],
            scr["gain_r"].at[k],
            seq=lax.rem(s + k, n),
        )

    for k in range(1, n):
        gain_out(k).start()
    for t in range(12, 15):
        ring1.go(t)
        ring2.go(t - 8)
        ring3.go(t - 9)
    store1 = pltpu.make_async_copy(x1, sum1_o, scr["store"].at[0])
    store1.start()
    for t in range(7, 15):
        ring2.go(t)
        ring3.go(min(t - 1 + (t - 7) // 3, 14))
    store2 = pltpu.make_async_copy(x2, sum2_o, scr["store"].at[1])
    store2.start()
    ring3.go(14)
    for i, small_o in enumerate((rate_o, cin_o, cout_o)):
        small_o[...] = x3[i * NS : (i + 1) * NS].astype(F32)
    for k in range(1, n):
        gain_out(k).wait_recv()
        total = total + gg[k]
    norm_o[...] = total[0:1]
    mid_o[...] = total[1:2]
    for k in range(1, n):
        gain_out(k).wait_send()
    for c in gains + ctx_out:
        c.wait_send()
    for g in gathers:
        g.finish()

    @pl.when(s > 0)
    def _():
        ctx_back.wait_send()
        for i in range(4):
            to_before(0, i, dkp.at[i], rk.at[i]).wait_send()
            to_before(1, i, dvp.at[i], rv.at[i]).wait_send()

    for k in range(1, n):

        @pl.when(s >= k)
        def _():
            spread(k).wait_send()

    ring1.drain()
    ring2.drain()
    ring3.drain()
    store1.wait()
    store2.wait()


def ring_rows(n, used, subs):
    return -(-used // (2 * n * subs * 16)) * 16


def last(*args):
    n = lax.axis_size("seq")
    by = dict(zip(LAST_IN, args))
    micro, block, width = by["nf"].shape
    rows = block // 4
    chan = by["rate"].shape[1]
    keys = by["k"].shape[1]
    sds = jax.ShapeDtypeStruct
    dma = pltpu.SemaphoreType.DMA
    step1 = ring_rows(n, by["ffn"].shape[0], 2)
    step2 = ring_rows(n, 4 * width, 2)
    step3 = ring_rows(n, 3 * NS, 1)
    x1 = VM((4 * n * step1, chan), BF)
    x2 = VM((4 * n * step2, chan), BF)
    scratch = dict(
        x1=x1,
        r1=VM((2, n - 1, 2, step1, chan), BF),
        x2=x2,
        r2=VM((2, n - 1, 2, step2, chan), BF),
        x3=VM((2 * n * step3, chan), BF),
        r3=VM((2, n - 1, 1, step3, chan), BF),
        s1s=dma((2, 2, 2 * n - 2)),
        s1r=dma((2, 2, 2 * n - 2)),
        s2s=dma((2, 2, 2 * n - 2)),
        s2r=dma((2, 2, 2 * n - 2)),
        s3s=dma((2, 1, 2 * n - 2)),
        s3r=dma((2, 1, 2 * n - 2)),
        fetch=dma((len(LAST_IN),)),
        rr=VM((micro, block, width), BF),
        da=VM((micro, block, chan), BF),
        rs=dma((2, 3)),
        rrv=dma((2, 3)),
        rk=VM((4, block, HD), BF),
        rv=VM((4, block, HD), BF),
        dkp=VM((4, block, HD), BF),
        dvp=VM((4, block, HD), BF),
        ak=VM((keys, HD), F32),
        av=VM((keys, HD), F32),
        dq=VM((micro, block, chan), BF),
        dko=VM((micro, block, chan), F32),
        dvo=VM((micro, block, chan), F32),
        dkb=VM((micro, block, chan), BF),
        dvb=VM((micro, block, chan), BF),
        dkc=VM((micro, CTX, chan), BF),
        dvc=VM((micro, CTX, chan), BF),
        cp=VM((4, micro, CTX, chan), BF),
        cr=VM((3, micro, CTX, chan), BF),
        dcs=VM((micro, CTX, chan), BF),
        dcr=VM((micro, CTX, chan), BF),
        dy=VM((micro, CTX, chan), F32),
        u=VM((micro, block, chan), F32),
        du=VM((micro, block, chan), F32),
        hist=VM((block + 1, micro, NS, chan), BF),
        pay=VM((3 * NS, chan), BF),
        gath=VM((n, 3 * NS, chan), BF),
        part=VM((block // 2, width), F32),
        dh1=VM((micro, rows, width), F32),
        over=VM((4, rows, width), BF),
        into=VM((4, 3, rows, width), BF),
        ss=dma((4, 3)),
        sr=dma((4, 3)),
        gp=VM((4, 8, chan), F32),
        gr=VM((3, 8, chan), F32),
        gs=VM((8, chan), F32),
        gg=VM((n, 8, chan), F32),
        gain_s=dma((n,)),
        gain_r=dma((n,)),
        send_k=dma((2, 5)),
        recv_k=dma((2, 5)),
        send_c=dma((2, 3)),
        recv_c=dma((2, 3)),
        send_g=dma((n,)),
        recv_g=dma((n,)),
        store=dma((2,)),
    )
    outs = (
        sds((micro, rows, width), BF),
        sds((micro, rows, width), F32),
        sds(x1.shape, BF),
        sds(x2.shape, BF),
        sds((NS, chan), F32),
        sds((NS, chan), F32),
        sds((NS, chan), F32),
        sds((1, chan), F32),
        sds((1, chan), F32),
    )
    return launch(
        functools.partial(last_kernel, n),
        LAST_IN,
        args,
        outs,
        [True, True, False, False, True, True, True, True, True],
        scratch,
        2,
        62,
        "last",
        ("ffn",),
    )


def finish_kernel(*refs):
    half = len(refs) // 2
    for src, dst in zip(refs[:half], refs[half:]):
        dst[...] = src[...].astype(dst.dtype)


def finish(sum1, sum2, mixed, tokens_grad, end, small, width, units, chan):
    steps = width // chan
    sds = jax.ShapeDtypeStruct
    down_at = units * width // chan
    micro, rows, _ = mixed.shape

    def panel(rows_of, at):
        return (
            pl.BlockSpec((rows_of, chan), lambda j: (at // rows_of + j, 0)),
            pl.BlockSpec((rows_of, chan), lambda j: (0, j)),
        )

    def column(at):
        high = width // steps
        return (
            pl.BlockSpec((high, chan), lambda j: (at // high + j, 0)),
            pl.BlockSpec((high, chan), lambda j: (j, 0)),
        )

    same = pl.BlockSpec((micro, rows // steps, width), lambda j: (0, j, 0))
    whole = pl.BlockSpec(end.shape, lambda j: (0, 0, 0))
    specs = [
        panel(width, 0),
        panel(units, down_at),
        panel(chan, 3 * width),
        column(0),
        column(width),
        column(2 * width),
        (same, same),
        (same, same),
        (whole, whole),
    ] + [
        (pl.BlockSpec(a.shape, lambda j: (0, 0)), pl.BlockSpec(a.shape, lambda j: (0, 0)))
        for a in small
    ]
    return pl.pallas_call(
        finish_kernel,
        grid=(steps,),
        out_shape=(
            sds((width, units), F32),
            sds((units, width), F32),
            sds((chan, width), F32),
            sds((width, chan), F32),
            sds((width, chan), F32),
            sds((width, chan), F32),
            sds(mixed.shape, BF),
            sds(tokens_grad.shape, F32),
            sds(end.shape, F32),
            *(sds(a.shape, F32) for a in small),
        ),
        in_specs=[a for a, _ in specs],
        out_specs=tuple(b for _, b in specs),
        compiler_params=pltpu.CompilerParams(vmem_limit_bytes=62 << 20),
        name="finish",
    )(sum1, sum1, sum2, sum2, sum2, sum2, mixed, tokens_grad, end, *small)


def body(
    tokens,
    out_grad,
    norm_gain,
    w_query,
    w_key,
    w_value,
    w_out,
    mid_gain,
    w_up,
    w_down,
    ssm_rate,
    ssm_in,
    ssm_out,
    resets,
    init_state,
    states_grad,
):
    micro, rows, width = tokens.shape
    chan = ssm_rate.shape[0]
    units = w_up.shape[1]
    rate, cin, cout = ssm_rate.T, ssm_in.T, ssm_out.T
    flag = jnp.broadcast_to(resets, (micro, chan))
    init = jnp.swapaxes(init_state, 1, 2)
    endg = jnp.swapaxes(states_grad[:, 0], 1, 2)
    gain_row, mid_row = norm_gain[None], mid_gain[None]
    nf, q, k, v, ctx, keep, start, end, mlp, h1, dm, ffn, att, lse = forward(
        *(tokens, gain_row, w_key, w_value, w_query, rate, cin, cout, flag, init, out_grad),
        *(w_out, mid_row, w_up, w_down),
    )
    mixed, tokens_grad, sum1, sum2, *small = last(
        *(q, k, v, lse, att, w_out, nf, ctx, w_query, w_key, w_value, rate, cin, cout),
        *(start, keep, endg, mlp, h1, dm, out_grad, mid_row, tokens, gain_row, ffn),
    )
    done = finish(sum1, sum2, mixed, tokens_grad, end, small, width, units, chan)
    up_g, down_g, proj_g, query_g, key_g, value_g, mixed, tokens_grad, end = done[:9]
    rate_g, in_g, out_g, norm_g, mid_g = done[9:]
    return (
        mixed,
        jnp.swapaxes(end, 1, 2)[:, None],
        tokens_grad,
        norm_g[0],
        query_g,
        key_g,
        value_g,
        proj_g,
        mid_g[0],
        up_g,
        down_g,
        rate_g.T,
        in_g.T,
        out_g.T,
    )


def solution(mesh):
    return jax.shard_map(
        body,
        mesh=mesh,
        in_specs=(
            P(None, ("seq", "tp"), None),
            P(None, ("seq", "tp"), None),
            P(),
            P(None, "tp"),
            P(None, "tp"),
            P(None, "tp"),
            P("tp", None),
            P(),
            P(None, "tp"),
            P("tp", None),
            P("tp", None),
            P("tp", None),
            P("tp", None),
            P(None, "seq"),
            P(None, "tp", None),
            P(None, "seq", "tp", None),
        ),
        out_specs=(
            P(None, ("seq", "tp"), None),
            P(None, "seq", "tp", None),
            P(None, ("seq", "tp"), None),
            P("tp"),
            P(None, "tp"),
            P(None, "tp"),
            P(None, "tp"),
            P("tp", None),
            P("tp"),
            P(None, "tp"),
            P("tp", None),
            P("tp", None),
            P("tp", None),
            P("tp", None),
        ),
        check_vma=False,
    )
```

```python
import functools

import jax
import jax.numpy as jnp
from jax import lax
from jax.experimental import pallas as pl
from jax.experimental.pallas import tpu as pltpu
from jax.sharding import PartitionSpec as P

HD = 128
NS = 16
CTX = 128


eps_norm = 1e-06
neg_big = -1e30
LOG2E = 1.4426950408889634
MESH = pl.DeviceIdType.MESH
VM = pltpu.VMEM
BF = jnp.bfloat16
F32 = jnp.float32
NT = (((1,), (1,)), ((), ()))
TN = (((0,), (0,)), ((), ()))
NN = (((1,), (0,)), ((), ()))


def dot(left, right, dims=NN):
    return lax.dot_general(left, right, dims, preferred_element_type=F32)


def vmem_specs(count):
    return [pl.BlockSpec(memory_space=VM)] * count


def tp_peers():
    me = lax.axis_index("tp")
    mate = me + 1 - 2 * lax.rem(me, 2)
    return me, mate, lax.rem(me + 2, 4), lax.rem(mate + 2, 4)


def flag_rows(keep):
    rest = jnp.zeros((NS - keep.shape[0], keep.shape[1]), F32)
    return jnp.concatenate([keep[...], rest], axis=0).astype(BF)


def remote(src, dst, send, recv, **where):
    return pltpu.make_async_remote_copy(
        src_ref=src,
        dst_ref=dst,
        send_sem=send,
        recv_sem=recv,
        device_id=where,
        device_id_type=MESH,
    )


def greet(n, with_seq):
    s = lax.axis_index("seq")
    barrier = pltpu.get_barrier_semaphore()
    for peer in tp_peers()[1:]:
        pl.semaphore_signal(barrier, inc=1, device_id={"tp": peer}, device_id_type=MESH)
    if with_seq:
        for k in range(1, n):
            pl.semaphore_signal(
                barrier, inc=1, device_id={"seq": lax.rem(s + k, n)}, device_id_type=MESH
            )


def greeted(n, with_seq):
    pl.semaphore_wait(pltpu.get_barrier_semaphore(), 3 + (n - 1 if with_seq else 0))


class Fetch:
    def __init__(self, names, refs, held, sems):
        self.copies = {
            name: pltpu.make_async_copy(ref, held[name], sems.at[i])
            for i, (name, ref) in enumerate(zip(names, refs))
        }
        self.ready = set()
        for c in self.copies.values():
            c.start()

    def need(self, *wanted):
        for name in wanted:
            if name not in self.ready:
                self.copies[name].wait()
                self.ready.add(name)


class Gather:
    def __init__(self, ref, send, recv):
        rows = ref.shape[0] // 4
        me, mate, across, _ = tp_peers()

        def give(slot, quarter, peer):
            part = ref.at[pl.ds(pl.multiple_of(quarter * rows, rows), rows), :]
            return remote(part, part, send.at[slot], recv.at[slot], tp=peer)

        self.cross = give(1, me, across)
        self.side = give(0, me, mate)
        self.relay = give(2, across, mate)

    def start(self):
        self.cross.start()
        self.side.start()

    def near(self):
        self.side.wait_recv()

    def pass_on(self):
        self.cross.wait_recv()
        self.relay.start()

    def far(self):
        self.relay.wait_recv()

    def finish(self):
        for c in (self.side, self.cross, self.relay):
            c.wait_send()


class Scatter:
    def __init__(self, ref, over, into, send, recv):
        self.ref, self.over, self.into = ref, over, into
        self.rows = ref.shape[0] // 4
        self.me, self.mate, self.across, self.diag = tp_peers()
        self.hop = [
            remote(self.quarter(self.diag), into.at[0], send.at[0], recv.at[0], tp=self.mate),
            remote(self.quarter(self.mate), into.at[1], send.at[1], recv.at[1], tp=self.mate),
            remote(over, into.at[2], send.at[2], recv.at[2], tp=self.across),
        ]

    def span(self, quarter):
        return pl.ds(pl.multiple_of(quarter * self.rows, self.rows), self.rows)

    def quarter(self, quarter):
        return self.ref.at[self.span(quarter), :]

    def start(self):
        self.hop[0].start()
        self.hop[1].start()

    def turn(self):
        self.hop[0].wait_recv()
        mine = self.ref[self.span(self.across), :].astype(F32)
        self.over[...] = (mine + self.into[0].astype(F32)).astype(BF)
        self.hop[2].start()

    def end(self):
        self.hop[1].wait_recv()
        value = self.ref[self.span(self.me), :].astype(F32) + self.into[1].astype(F32)
        self.hop[2].wait_recv()
        value = value + self.into[2].astype(F32)
        for c in self.hop:
            c.wait_send()
        return value


FORWARD_IN = (
    "tok",
    "gain",
    "wk",
    "wv",
    "wq",
    "rate",
    "cin",
    "cout",
    "flag",
    "init",
    "ogm",
    "w_out",
    "mid",
    "w_up",
    "w_down",
)


class Save:
    def __init__(self, sems):
        self.sems, self.copies = sems, []

    def __call__(self, src, dst):
        self.copies.append(pltpu.make_async_copy(src, dst, self.sems.at[len(self.copies)]))
        self.copies[-1].start()

    def finish(self):
        for c in self.copies:
            c.wait()


def forward_kernel(n, refs_in, outs, held, scr):
    s = lax.axis_index("seq")
    me, mate, across, diag = tp_peers()
    og = scr["og"]
    own_rows = og.shape[1] // 4
    own = pl.ds(pl.multiple_of(me * own_rows, own_rows), own_rows)
    held = dict(held, ogm=og.at[:, own, :])
    fetch = Fetch(FORWARD_IN, refs_in, held, scr["fetch"])
    nf_d, q_d, k_d, v_d, ctx_d, keep_d, start_o, end_o = outs[:8]
    nf, q_o, k_o, v_o, ctx_o = (scr[x] for x in ("nf", "q", "k", "v", "ctxa"))
    save = Save(scr["save"])
    grad_gathers = [Gather(og.at[m], scr["os"].at[m], scr["or"].at[m]) for m in range(2)]
    tok, rate, flag, init = (held[x] for x in ("tok", "rate", "flag", "init"))
    keep = scr["keep"]
    wq, wk, wv = held["wq"], held["wk"], held["wv"]
    u_s, gath, pay, y_s, ctx_s = (scr[x] for x in ("u", "gath", "pay", "y", "ctx"))
    block = nf.shape[1]
    rows = block // 4
    chan = rate.shape[1]
    gath[...] = jnp.zeros_like(gath)

    @pl.when(s == 0)
    def _():
        k_o[:, 0 : CTX + block, :] = jnp.zeros((2, CTX + block, chan), BF)
        v_o[:, 0 : CTX + block, :] = jnp.zeros((2, CTX + block, chan), BF)
        ctx_o[...] = jnp.zeros_like(ctx_o)

    greet(n, True)

    def span(quarter):
        return pl.ds(pl.multiple_of(quarter * rows, rows), rows)

    def lanes(part):
        return pl.ds(pl.multiple_of(part * chan, chan), chan)

    fetch.need("tok", "gain")
    x = tok[...].astype(F32).reshape(2 * rows, -1)
    normed = x * lax.rsqrt(jnp.mean(x * x, axis=-1, keepdims=True) + eps_norm) * held["gain"][...]
    nf[:, span(me), :] = normed.astype(BF).reshape(2, rows, -1)
    greeted(n, True)

    def give(slot, quarter, peer, part=None):
        cols = slice(None) if part is None else lanes(part)
        ref = nf.at[:, span(quarter), cols]
        return remote(ref, ref, scr["ts"].at[slot], scr["tr"].at[slot], tp=peer)

    cross = [give(1 + i, me, across, part) for i, part in enumerate((across, diag, me, mate))]
    relay = [give(5 + i, across, mate, part) for i, part in enumerate((me, mate, across, diag))]
    side = give(0, me, mate)
    for c in cross:
        c.start()
    side.start()

    def pass_kv(slot, src, half):
        high = 2 * rows
        part = pl.ds(pl.multiple_of(CTX + half * high, rows), high)
        own = pl.ds(pl.multiple_of(CTX + block + half * high, rows), high)
        return remote(
            src.at[:, own, :],
            src.at[:, part, :],
            scr["kvs"].at[slot],
            scr["kvr"].at[slot],
            seq=lax.rem(s + 1, n),
        )

    def qkv(order, half):
        high = 2 * rows
        here = pl.ds(pl.multiple_of(half * high, high), high)
        part = nf[:, here, :].reshape(2 * high, -1)
        own = pl.ds(pl.multiple_of(CTX + block + half * high, rows), high)
        k_o[:, own, :] = dot(part, wk[...]).astype(BF).reshape(2, high, chan)
        v_o[:, own, :] = dot(part, wv[...]).astype(BF).reshape(2, high, chan)

        @pl.when(s < n - 1)
        def _():
            pass_kv(2 * order, k_o, half).start()
            if order == 0:
                pass_kv(1, v_o, half).start()

        q_o[:, here, :] = dot(part, wq[...]).astype(BF).reshape(2, high, chan)

    near = me // 2
    side.wait_recv()
    fetch.need("wk", "wv", "wq")
    qkv(0, near)
    cross[0].wait_recv()
    cross[1].wait_recv()
    relay[1].start()
    relay[0].start()
    relay[1].wait_recv()
    fetch.need("rate", "cin", "cout", "flag", "init")
    for m in range(2):
        keep[m : m + 1, :] = jnp.broadcast_to(1.0 - flag[m : m + 1, :].astype(F32), (1, chan))
    save(keep, keep_d)
    cols = lanes(me)
    for m in range(2):
        u_s[m] = nf[m, :, cols].astype(F32)
    decay = jnp.exp(-rate[...])
    drive = jnp.sqrt(1.0 - decay * decay) * held["cin"][...]

    def run(i, state):
        base = pl.multiple_of(i * 8, 8)
        state = list(state)
        for k in range(8):
            for m in range(2):
                state[m] = decay * state[m] + drive * u_s[m, pl.ds(base + k, 1), :]
        return tuple(state)

    zero = jnp.zeros((NS, chan), F32)
    late = lax.fori_loop(0, (block - CTX) // 8, run, (zero, zero))
    last_state = lax.fori_loop((block - CTX) // 8, block // 8, run, late)
    for m in range(2):
        pay[m * NS : (m + 1) * NS] = last_state[m].astype(BF)
    pay[2 * NS : 3 * NS] = flag_rows(keep)

    def spread(k):
        return remote(
            pay, gath.at[k], scr["gs"].at[k], scr["gr"].at[k], seq=lax.rem(s + k, n)
        )

    for k in range(1, n):

        @pl.when(s + k < n)
        def _():
            spread(k).start()

    for i in (2, 3):
        cross[i].wait_recv()
        relay[i].start()
    for i in (0, 2, 3):
        relay[i].wait_recv()
    fetch.need("ogm")
    for g in grad_gathers:
        g.start()
    qkv(1, 1 - near)
    save(nf, nf_d)
    save(q_o, q_d)

    whole = jnp.exp(-rate[...] * block)
    for k in range(1, n):

        @pl.when(s >= k)
        def _():
            spread(k).wait_recv()

    def entry(begin_keep, end, b):
        return tuple(jnp.where(b == 0, init[m], begin_keep[m] * end[m]) for m in range(2))

    def chain(b, end):
        k = jnp.maximum(s - b, 0)
        got = gath[k].astype(F32)
        begin = entry((got[2 * NS : 2 * NS + 1], got[2 * NS + 1 : 2 * NS + 2]), end, b)
        new = tuple(got[m * NS : (m + 1) * NS] + whole * begin[m] for m in range(2))
        return tuple(jnp.where(b < s, new[m], end[m]) for m in range(2))

    end = lax.fori_loop(0, n - 1, chain, (zero, zero))
    begin = entry((keep[0:1, :], keep[1:2, :]), end, s)
    toward = jnp.exp(-rate[...] * (block - CTX))
    state = tuple(late[m] + toward * begin[m] for m in range(2))
    out_c = held["cout"][...]

    def run_out(i, state):
        base = pl.multiple_of(block - CTX + i * 8, 8)
        row = pl.multiple_of(i * 8, 8)
        state = list(state)
        for k in range(8):
            for m in range(2):
                state[m] = decay * state[m] + drive * u_s[m, pl.ds(base + k, 1), :]
                y_s[m, pl.ds(row + k, 1), :] = jnp.sum(out_c * state[m], axis=0, keepdims=True)
        return tuple(state)

    state = lax.fori_loop(0, CTX // 8, run_out, state)
    ctx_s[...] = y_s[...].astype(BF)
    down = remote(
        ctx_s, ctx_o.at[:, :, cols], scr["cs"].at[0], scr["cr"].at[0], seq=lax.rem(s + 1, n)
    )

    @pl.when(s < n - 1)
    def _():
        down.start()
        pass_kv(3, v_o, 1 - near).start()

    for m in range(2):
        start_o[m] = begin[m]
        end_o[m] = last_state[m] + whole * begin[m]
    for g in grad_gathers:
        g.near()
        g.pass_on()

    @pl.when(s > 0)
    def _():
        down.wait_recv()
        theirs = lanes(across)
        shares = [
            remote(
                ctx_o.at[:, :, part],
                ctx_o.at[:, :, part],
                scr["cs"].at[1 + i],
                scr["cr"].at[1 + i],
                tp=peer,
            )
            for i, (part, peer) in enumerate(((cols, across), (cols, mate), (theirs, mate)))
        ]
        shares[0].start()
        shares[1].start()
        shares[0].wait_recv()
        shares[2].start()
        shares[1].wait_recv()
        shares[2].wait_recv()
        flat = ctx_o[...].reshape(2 * CTX, -1)
        k_o[:, 0:CTX, :] = dot(flat, wk[...]).astype(BF).reshape(2, CTX, chan)
        v_o[:, 0:CTX, :] = dot(flat, wv[...]).astype(BF).reshape(2, CTX, chan)
        for order, half in enumerate((near, 1 - near)):
            pass_kv(2 * order, k_o, half).wait_recv()
            pass_kv(2 * order + 1, v_o, half).wait_recv()
        for c in shares:
            c.wait_send()

    save(k_o, k_d)
    save(v_o, v_d)
    save(ctx_o, ctx_d)
    forward_middle(fetch, held, scr, outs[8:], save, q_o, k_o, v_o, og, grad_gathers)

    @pl.when(s < n - 1)
    def _():
        down.wait_send()
        for order, half in enumerate((near, 1 - near)):
            pass_kv(2 * order, k_o, half).wait_send()
            pass_kv(2 * order + 1, v_o, half).wait_send()

    for k in range(1, n):

        @pl.when(s + k < n)
        def _():
            spread(k).wait_send()

    for c in [side] + cross + relay:
        c.wait_send()
    for g in grad_gathers:
        g.finish()
    save.finish()


def launch(
    body, names, args, outs, out_vmem, scratch, collective_id, limit, name, placed=()
):
    keys = list(scratch)
    count = len(names)
    plain = [name for name in names if name not in placed]

    def kernel(*refs):
        refs_in, refs = refs[:count], refs[count:]
        outs_r, refs = refs[: len(outs)], refs[len(outs) :]
        held, refs = dict(zip(plain, refs)), refs[len(plain) :]
        body(refs_in, outs_r, held, dict(zip(keys, refs)))

    scratch = dict(scratch)
    return pl.pallas_call(
        kernel,
        out_shape=tuple(outs),
        in_specs=[pl.BlockSpec(memory_space=pl.ANY)] * count,
        out_specs=tuple(
            pl.BlockSpec(memory_space=VM if in_vmem else pl.ANY) for in_vmem in out_vmem
        ),
        scratch_shapes=[VM(a.shape, a.dtype) for x, a in zip(names, args) if x in plain]
        + list(scratch.values()),
        compiler_params=pltpu.CompilerParams(
            collective_id=collective_id, has_side_effects=True, vmem_limit_bytes=limit << 20
        ),
        name=name,
    )(*args)


def rms_back(x, gain, grad):
    inv = lax.rsqrt(jnp.mean(x * x, axis=-1, keepdims=True) + eps_norm)
    unit = x * inv
    scaled = grad * gain
    gain_grad = jnp.sum(grad * unit, axis=0, keepdims=True)
    return inv * (scaled - unit * jnp.mean(scaled * unit, axis=-1, keepdims=True)), gain_grad


def forward_middle(fetch, held, scr, outs, save, q, k, v, og, grad_gathers):
    nm, pm, dm, hid, dpre = (scr[x] for x in ("nm", "pm", "dm", "hid", "dpre"))
    mlp_o, h1_o, ffn_o, att, lse = (scr[x] for x in ("mlp", "h1", "ffn", "att", "lse"))
    w_out, tok, gain, w_up, w_down = (
        held[x] for x in ("w_out", "tok", "mid", "w_up", "w_down")
    )
    keep = scr["keep"]
    me = tp_peers()[0]
    near = me // 2
    block = q.shape[1]
    rows = block // 4
    width = w_out.shape[1]
    tile = 256
    panels = w_up.shape[1] // tile
    own = pl.ds(pl.multiple_of(me * rows, rows), rows)
    edge0 = k.shape[1] - block
    half = block // 2
    row_ids = lax.broadcasted_iota(jnp.int32, (half, half), 0)
    col_ids = lax.broadcasted_iota(jnp.int32, (half, half), 1)
    scale = HD ** (-0.5) * LOG2E

    def attend(m):
        def one(head, c):
            lanes = pl.ds(pl.multiple_of(head * HD, HD), HD)
            shut = (keep[m : m + 1, 0:half] - 1.0) * -neg_big
            for part in range(2):
                mine = slice(part * half, (part + 1) * half)
                edge = edge0 + part * half
                sc = dot(k[m, 0 : edge + half, lanes], q[m, mine, lanes], NT) * scale
                pieces = [sc[:edge0] + shut]
                if part:
                    pieces.append(sc[edge0:edge])
                pieces.append(jnp.where(row_ids <= col_ids, sc[edge:], neg_big))
                sc = jnp.concatenate(pieces, axis=0)
                top = jnp.max(sc, axis=0, keepdims=True)
                expo = jnp.exp2(sc - top)
                total = jnp.sum(expo, axis=0, keepdims=True)
                res = dot(v[m, 0 : edge + half, lanes], expo.astype(BF), TN) * (1.0 / total)
                att[m, mine, lanes] = res.T.astype(BF)
                lse[m, head, :, mine] = top + LOG2E * jnp.log(total)
            return c

        lax.fori_loop(0, q.shape[2] // HD, one, 0)

    def scatter(kind, m, ref):
        at = 2 * kind + m
        return Scatter(
            ref.at[m], scr["over"].at[at], scr["into"].at[at], scr["ss"].at[at], scr["sr"].at[at]
        )

    mlp_d, h1_d, dm_d, ffn_d, att_d, lse_d = outs
    sums1 = [scatter(0, m, pm) for m in range(2)]
    gathers = [Gather(nm.at[m], scr["mgs"].at[m], scr["mgr"].at[m]) for m in range(2)]

    def project(m):
        def one(j, c):
            cols = pl.ds(pl.multiple_of(j * tile, tile), tile)
            pm[m, :, cols] = dot(att[m], w_out[:, cols]).astype(BF)
            return c

        lax.fori_loop(0, width // tile, one, 0)

    def residual(m):
        h1 = tok[m].astype(F32) + sums1[m].end()
        h1_o[m] = h1
        inv = lax.rsqrt(jnp.mean(h1 * h1, axis=-1, keepdims=True) + eps_norm)
        nm[m, own, :] = (h1 * inv * gain[...]).astype(BF)
        gathers[m].start()

    def feed(m, part):
        here = pl.ds(pl.multiple_of(part * half, half), half)
        flat = pl.ds(pl.multiple_of(m * block + part * half, half), half)

        def panel(j, c):
            cols = pl.ds(pl.multiple_of(j * tile, tile), tile)
            pre = dot(nm[m, here, :], w_up[:, cols])
            sq = pre * pre
            t = jnp.tanh((0.7978845608028654 * pre) * (1.0 + 0.044715 * sq))
            hid[flat, cols] = (0.5 * pre * (1.0 + t)).astype(BF)
            slope = 0.5 * (1.0 + t) + (0.3989422804014327 * pre) * (1.0 - t * t) * (
                1.0 + 0.134145 * sq
            )
            dpre[flat, cols] = (slope * dot(og[m, here, :], w_down[cols, :], NT)).astype(BF)
            return c

        lax.fori_loop(0, panels, panel, 0)

        def back(j, c):
            cols = pl.ds(pl.multiple_of(j * tile, tile), tile)
            dm[m, here, cols] = dot(dpre[flat, :], w_up[cols, :], NT).astype(BF)
            return c

        lax.fori_loop(0, width // tile, back, 0)

    def lower(m, part):
        here = pl.ds(pl.multiple_of(part * half, half), half)
        flat = pl.ds(pl.multiple_of(m * block + part * half, half), half)

        def one(j, c):
            cols = pl.ds(pl.multiple_of(j * tile, tile), tile)
            mlp_o[m, here, cols] = dot(hid[flat, :], w_down[:, cols]).astype(BF)
            return c

        lax.fori_loop(0, width // tile, one, 0)

    attend(0)
    fetch.need("w_out")
    project(0)
    sums1[0].start()
    sums1[0].turn()
    attend(1)
    project(1)
    save(att, att_d)
    save(lse, lse_d)
    sums1[1].start()
    sums1[1].turn()
    fetch.need("mid")
    residual(0)
    fetch.need("w_up", "w_down")
    for g in grad_gathers:
        g.far()
    gathers[0].near()
    feed(0, near)
    residual(1)
    save(h1_o, h1_d)
    gathers[0].pass_on()
    gathers[1].near()
    feed(1, near)
    lower(0, near)
    lower(1, near)
    gathers[0].far()
    feed(0, 1 - near)
    save(dm.at[0], dm_d.at[0])
    gathers[1].pass_on()
    gathers[1].far()
    feed(1, 1 - near)
    save(dm.at[1], dm_d.at[1])

    def down_sum(i, c):
        left = hid[:, pl.ds(pl.multiple_of(i * tile, tile), tile)].T
        for j in range(width // tile):
            right = og[:, :, j * tile : (j + 1) * tile].reshape(2 * block, tile)
            at = pl.multiple_of((width // tile + j) * panels * tile + i * tile, tile)
            ffn_o[pl.ds(at, tile), :] = dot(left, right).astype(BF)
        return c

    def up_sum(i, c):
        left = nm[:, :, pl.ds(pl.multiple_of(i * tile, tile), tile)].reshape(2 * block, tile).T
        for j in range(panels):
            at = pl.multiple_of(j * width + i * tile, tile)
            ffn_o[pl.ds(at, tile), :] = dot(left, dpre[:, j * tile : (j + 1) * tile]).astype(BF)
        return c

    high = panels * tile * (width // tile)
    lax.fori_loop(0, panels, down_sum, 0)
    save(ffn_o.at[high : 2 * high], ffn_d.at[high : 2 * high])
    lower(0, 1 - near)
    lower(1, 1 - near)
    save(mlp_o, mlp_d)
    lax.fori_loop(0, width // tile, up_sum, 0)
    save(ffn_o.at[0:high], ffn_d.at[0:high])
    for m in range(2):
        gathers[m].finish()


def forward(*args):
    n = lax.axis_size("seq")
    by = dict(zip(FORWARD_IN, args))
    micro, rows, width = by["tok"].shape
    block = 4 * rows
    chan = by["rate"].shape[1]
    units = by["w_up"].shape[1]
    keys = CTX + 2 * block
    sds = jax.ShapeDtypeStruct
    dma = pltpu.SemaphoreType.DMA
    results = dict(
        nf=sds((micro, block, width), BF),
        q=sds((micro, block, chan), BF),
        k=sds((micro, keys, chan), BF),
        v=sds((micro, keys, chan), BF),
        ctxa=sds((micro, CTX, width), BF),
        keep=sds((micro, chan), F32),
        start=sds((micro, NS, chan), F32),
        end=sds((micro, NS, chan), F32),
        mlp=sds((micro, block, width), BF),
        h1=sds((micro, rows, width), F32),
        dm=sds((micro, block, width), BF),
        ffn=sds((2 * units * width // 256, 256), BF),
        att=sds((micro, block, chan), BF),
        lse=sds((micro, chan // HD, 1, block), F32),
    )
    in_vmem = ("start", "end")
    scratch = {x: VM(a.shape, a.dtype) for x, a in results.items() if x not in in_vmem}
    scratch.update(
        og=VM((micro, block, width), BF),
        fetch=dma((len(FORWARD_IN),)),
        save=dma((16,)),
        os=dma((2, 3)),
        u=VM((micro, block, chan), F32),
        gath=VM((n, 3 * NS, chan), BF),
        pay=VM((3 * NS, chan), BF),
        y=VM((micro, CTX, chan), F32),
        ctx=VM((micro, CTX, chan), BF),
        ts=dma((9,)),
        tr=dma((9,)),
        kvs=dma((4,)),
        kvr=dma((4,)),
        gs=dma((n,)),
        gr=dma((n,)),
        cs=dma((4,)),
        cr=dma((4,)),
        nm=VM((micro, block, width), BF),
        pm=VM((micro, block, width), BF),
        hid=VM((micro * block, units), BF),
        dpre=VM((micro * block, units), BF),
        over=VM((2, rows, width), BF),
        into=VM((2, 3, rows, width), BF),
        ss=dma((2, 3)),
        sr=dma((2, 3)),
        mgs=dma((2, 3)),
        mgr=dma((2, 3)),
    )
    scratch["or"] = dma((2, 3))
    return launch(
        functools.partial(forward_kernel, n),
        FORWARD_IN,
        args,
        tuple(results.values()),
        [x in in_vmem for x in results],
        scratch,
        0,
        62,
        "forward",
        ("ogm",),
    )


class Ring:
    def __init__(self, n, x, recv, send_sem, recv_sem):
        self.n, self.x, self.recv = n, x, recv
        self.send_sem, self.recv_sem = send_sem, recv_sem
        self.subs, self.rows = recv.shape[2], recv.shape[3]
        s = lax.axis_index("seq")
        half = n // 2
        self.r = jnp.where(lax.rem(s, 2) == 0, s // 2, n - 1 - s // 2)

        def dev(q):
            q = lax.rem(q + n, n)
            return jnp.where(q < half, 2 * q, 2 * (n - 1 - q) + 1)

        self.target = (dev(self.r + 1), dev(self.r - 1))
        self.done = 0
        self.total = 2 * n - 2

    def chunk(self, d, b, off):
        sign = (1, -1)[d]
        c = lax.rem(self.r + sign * off + 2 * self.n, self.n)
        at = ((d * self.n + c) * self.subs + b) * self.rows
        return pl.ds(pl.multiple_of(at, self.rows), self.rows)

    def copy(self, d, b, src, dst, k):
        return pltpu.make_async_remote_copy(
            src_ref=src,
            dst_ref=dst,
            send_sem=self.send_sem.at[d, b, k],
            recv_sem=self.recv_sem.at[d, b, k],
            device_id={"seq": self.target[d]},
            device_id_type=MESH,
        )

    def first(self, d, b):
        return self.copy(d, b, self.x.at[self.chunk(d, b, 0)], self.recv.at[d, 0, b], 0)

    def sums(self, d, b, k):
        prior = jnp.maximum(k - 1, 0)
        return self.copy(d, b, self.recv.at[d, prior, b], self.recv.at[d, k, b], k)

    def alls(self, d, b, k):
        ref = self.x.at[self.chunk(d, b, 1 - k)]
        return self.copy(d, b, ref, ref, self.n - 1 + k)

    def each(self):
        return [(d, b) for b in range(self.subs) for d in range(2)]

    def add(self, d, b, k):
        mine = self.x[self.chunk(d, b, -k - 1)]
        return (self.recv[d, k, b].astype(F32) + mine.astype(F32)).astype(BF)

    def start(self):
        for d, b in self.each():
            self.first(d, b).start()

    def tick(self, t):
        n = self.n

        def leave():
            for d, b in self.each():
                self.first(d, b).wait_send()

        def sum_step():
            for d, b in self.each():
                self.sums(d, b, t).wait_recv()
                self.recv[d, t, b] = self.add(d, b, t)
                self.sums(d, b, t + 1).start()

        def turn():
            for d, b in self.each():
                self.sums(d, b, n - 2).wait_recv()
                self.x[self.chunk(d, b, 1)] = self.add(d, b, n - 2)
                self.alls(d, b, 0).start()

        def all_step():
            k = t - (n - 1)
            for d, b in self.each():
                self.alls(d, b, k).wait_recv()
                self.alls(d, b, k + 1).start()

        def close():
            for d, b in self.each():
                self.alls(d, b, n - 2).wait_recv()

        steps = (
            (t == 0, leave),
            (t < n - 2, sum_step),
            (t == n - 2, turn),
            ((t > n - 2) & (t < 2 * n - 3), all_step),
            (t == 2 * n - 3, close),
        )
        for when, step in steps:
            if isinstance(t, int):
                if when:
                    step()
            else:
                pl.when(when)(step)

    def go(self, fourteenths):
        upto = min(-(-fourteenths * self.total // 14), self.total)
        if upto - self.done == 1:
            self.tick(self.done)
        elif upto > self.done:

            def one(t, c):
                self.tick(t)
                return c

            lax.fori_loop(self.done, upto, one, 0)
        self.done = max(upto, self.done)

    def drain(self):
        def more(k, c):
            for d, b in self.each():
                self.sums(d, b, k + 1).wait_send()
                self.alls(d, b, k).wait_send()
            return c

        lax.fori_loop(0, self.n - 2, more, 0)
        for d, b in self.each():
            self.alls(d, b, self.n - 2).wait_send()


LAST_IN = (
    "dm",
    "ffn",
    "nf",
    "rate",
    "cin",
    "cout",
    "start",
    "endg",
    "h1",
    "ogm",
    "mid",
    "w_out",
    "keep",
    "q",
    "k",
    "v",
    "lse",
    "att",
    "ctx",
    "wq",
    "wk",
    "wv",
    "mlp",
    "tok",
    "gain",
)


def last_kernel(n, refs_in, outs, h, scr):
    x1, x2, x3 = scr["x1"], scr["x2"], scr["x3"]
    ffn_rows = refs_in[LAST_IN.index("ffn")].shape[0]
    h = dict(h, ffn=x1.at[0:ffn_rows])
    fetch = Fetch(LAST_IN, refs_in, h, scr["fetch"])
    need = fetch.need
    mixed_o, tg_o, sum1_o, sum2_o, rate_o, cin_o, cout_o, norm_o, mid_o = outs
    s = lax.axis_index("seq")
    me, mate, across, diag = tp_peers()
    peers = (mate, across, diag)
    nf, rate, tok = h["nf"], h["rate"], h["tok"]
    block = nf.shape[1]
    rows = block // 4
    width = nf.shape[2]
    chan = rate.shape[1]
    rk, rv, gath, dcr = scr["rk"], scr["rv"], scr["gath"], scr["dcr"]
    gath[...] = jnp.zeros_like(gath)
    if x1.shape[0] > ffn_rows:
        x1[ffn_rows:] = jnp.zeros((x1.shape[0] - ffn_rows, chan), BF)
    used2 = 4 * width
    if x2.shape[0] > used2:
        x2[used2:] = jnp.zeros((x2.shape[0] - used2, chan), BF)
    x3[...] = jnp.zeros_like(x3)

    @pl.when(s == n - 1)
    def _():
        rk[...] = jnp.zeros_like(rk)
        rv[...] = jnp.zeros_like(rv)
        dcr[...] = jnp.zeros_like(dcr)

    greet(n, True)
    before = lax.rem(s + n - 1, n)
    own = pl.ds(pl.multiple_of(me * rows, rows), rows)

    def to_before(sem, slot, src, dst):
        return remote(
            src, dst, scr["send_k"].at[sem, slot], scr["recv_k"].at[sem, slot], seq=before
        )

    ring1 = Ring(n, x1, scr["r1"], scr["s1s"], scr["s1r"])
    ring2 = Ring(n, x2, scr["r2"], scr["s2s"], scr["s2r"])
    ring3 = Ring(n, x3, scr["r3"], scr["s3s"], scr["s3r"])
    rr, da, dh1, mlp, h1 = scr["rr"], scr["da"], scr["dh1"], h["mlp"], h["h1"]

    def scatter(ref, at, m):
        at = 2 * at + m
        return Scatter(
            ref.at[m], scr["over"].at[at], scr["into"].at[at], scr["ss"].at[at], scr["sr"].at[at]
        )

    mid_sums = [scatter(h["dm"], 0, m) for m in range(2)]
    gathers = [Gather(rr.at[m], scr["rs"].at[m], scr["rrv"].at[m]) for m in range(2)]
    need("dm")
    greeted(n, True)
    for c in mid_sums:
        c.start()
    need("ffn")
    ring1.start()
    for c in mid_sums:
        c.turn()
    u_s, du_s, hist = scr["u"], scr["du"], scr["hist"]
    cols = pl.ds(pl.multiple_of(me * chan, chan), chan)
    need("nf", "rate", "cin", "cout", "start", "endg")
    for m in range(2):
        u_s[m] = nf[m, :, cols].astype(F32)
    decay = jnp.exp(-rate[...])
    root = jnp.sqrt(1.0 - decay * decay)
    drive = root * h["cin"][...]
    out_c = h["cout"][...]
    start, endg = h["start"], h["endg"]
    for m in range(2):
        hist[0, m] = start[m].astype(BF)

    def run(i, state):
        base = pl.multiple_of(i * 8, 8)
        state = list(state)
        for k in range(8):
            for m in range(2):
                state[m] = decay * state[m] + drive * u_s[m, pl.ds(base + k, 1), :]
                hist[base + k + 1, m] = state[m].astype(BF)
        return tuple(state)

    lax.fori_loop(0, block // 8, run, (start[0], start[1]))
    need("h1", "ogm", "mid")
    mid_grad = jnp.zeros((1, width), F32)
    for m in range(2):
        back, one = rms_back(h1[m], h["mid"][...], mid_sums[m].end())
        mid_grad = mid_grad + one
        dh1[m] = h["ogm"][m].astype(F32) + back
        rr[m, own, :] = dh1[m].astype(BF)
        gathers[m].start()
        ring1.go(m + 1)
    need("w_out", "q", "k", "v", "lse", "keep")

    q, k, v, lse, keep, w_out = (h[name] for name in ("q", "k", "v", "lse", "keep", "w_out"))
    edge0 = k.shape[1] - block
    half = block // 2
    row_ids = lax.broadcasted_iota(jnp.int32, (half, half), 0)
    col_ids = lax.broadcasted_iota(jnp.int32, (half, half), 1)
    scale = HD ** (-0.5)
    dq_s, dko, dvo, dkc, dvc = (scr[x] for x in ("dq", "dko", "dvo", "dkc", "dvc"))
    dkp, dvp, ak, av = (scr[x] for x in ("dkp", "dvp", "ak", "av"))

    def attend_one(m, head):
        i = 2 * m + head
        lanes = pl.ds(pl.multiple_of(head * HD, HD), HD)
        shut = (keep[pl.ds(m, 1), 0:half] - 1.0) * -neg_big
        for part in (1, 0):
            mine = slice(part * half, (part + 1) * half)
            edge = edge0 + part * half
            qq = q[m, mine, lanes]
            kk = k[m, 0 : edge + half, lanes]
            dd = da[m, mine, lanes]
            sc = dot(kk, qq, NT) * (scale * LOG2E)
            pieces = [sc[:edge0] + shut]
            if part:
                pieces.append(sc[edge0:edge])
            pieces.append(jnp.where(row_ids <= col_ids, sc[edge:], neg_big))
            sc = jnp.concatenate(pieces, axis=0)
            probs = jnp.exp2(sc - lse[m, head, :, mine])
            dp = dot(v[m, 0 : edge + half, lanes], dd, NT)
            spread_sum = jnp.sum(probs * dp, axis=0, keepdims=True)
            ds = (probs * (dp - spread_sum)).astype(BF)
            dq_s[m, mine, lanes] = (dot(kk, ds, TN) * scale).T.astype(BF)
            dk = dot(ds, qq) * scale
            dv = dot(probs.astype(BF), dd)
            if part:
                ak[...] = dk
                av[...] = dv
            else:
                ak[0 : edge + half] += dk
                av[0 : edge + half] += dv
        for acc, far, prev, own in ((ak, dkc, dkp, dko), (av, dvc, dvp, dvo)):
            far[m, :, lanes] = acc[0:CTX].astype(BF)
            prev[i] = acc[CTX:edge0].astype(BF)
            own[m, :, lanes] = acc[edge0:]

        @pl.when(s > 0)
        def _():
            to_before(0, i, dkp.at[i], rk.at[i]).start()
            to_before(1, i, dvp.at[i], rv.at[i]).start()

    def stream_back(m, c):
        g = Gather(rr.at[m], scr["rs"].at[m], scr["rrv"].at[m])
        g.far()
        ring1.tick(m + ring1.done)
        da[m] = dot(rr[m], w_out[...], NT).astype(BF)

        def heads(head, c):
            attend_one(m, head)

            @pl.when((m == 0) & (head == 0))
            def _():
                gathers[1].near()
                gathers[1].pass_on()

            return c

        lax.fori_loop(0, chan // HD, heads, 0)
        return c

    gathers[0].near()
    gathers[0].pass_on()
    lax.fori_loop(0, 2, stream_back, 0)
    ring1.done += 2

    cp, cr, dcs = scr["cp"], scr["cr"], scr["dcs"]
    wq, wk, wv = h["wq"], h["wk"], h["wv"]
    need("wq", "wk", "wv")
    ctx_part = dot(dkc[...].reshape(2 * CTX, chan), wk[...], NT) + dot(
        dvc[...].reshape(2 * CTX, chan), wv[...], NT
    )
    for j in range(4):
        cp[j] = ctx_part[:, j * chan : (j + 1) * chan].astype(BF).reshape(2, CTX, chan)

    def to_peer(i, src, dst, kind):
        return remote(
            src, dst, scr["send_c"].at[kind, i], scr["recv_c"].at[kind, i], tp=peers[i]
        )

    ctx_out = [
        remote(cp.at[q], cr.at[i], scr["send_c"].at[0, i], scr["recv_c"].at[0, i], tp=peer)
        for i, (q, peer) in enumerate(((diag, mate), (mate, mate), (across, across)))
    ]
    ctx_out[0].start()
    ctx_out[1].start()
    need("mlp")
    mlp_sums = [scatter(mlp, 1, m) for m in range(2)]
    for c in mlp_sums:
        c.start()
    ctx_out[0].wait_recv()
    cp[across] = (cp[across].astype(F32) + cr[0].astype(F32)).astype(BF)
    ctx_out[2].start()
    ring1.go(5)

    need("att")
    flat_att = h["att"][...].reshape(2 * block, chan).T
    tile = 256

    def proj(j, c):
        cols = pl.ds(pl.multiple_of(j * tile, tile), tile)
        right = rr[:, :, cols].reshape(2 * block, tile)
        at = pl.multiple_of(3 * width + j * tile, tile)
        x2[pl.ds(at, tile), :] = dot(flat_att, right).astype(BF)
        here = pl.ds(pl.multiple_of(j * tile, tile), tile)
        left = nf[:, :, here].reshape(2 * block, tile)
        x2[here, :] = dot(left, dq_s[...].reshape(2 * block, chan), TN).astype(BF)
        return c

    lax.fori_loop(0, width // tile, proj, 0)
    ctx_back = to_before(0, 4, dcs, dcr)
    total = cp[me].astype(F32)
    for i in (1, 2):
        ctx_out[i].wait_recv()
        total = total + cr[i].astype(F32)
    dcs[...] = total.astype(BF)

    @pl.when(s > 0)
    def _():
        ctx_back.start()

    for c in mlp_sums:
        c.turn()
    ring1.go(6)

    @pl.when(s < n - 1)
    def _():
        ctx_back.wait_recv()

    dy_s = scr["dy"]
    dy_s[...] = dcr[...].astype(F32)
    zero = jnp.zeros((NS, chan), F32)

    def early(i, grad):
        base = pl.multiple_of(CTX - 8 - i * 8, 8)
        grad = list(grad)
        for k in range(7, -1, -1):
            for m in range(2):
                grad[m] = decay * grad[m] + out_c * dy_s[m, pl.ds(base + k, 1), :]
        return tuple(grad)

    got = lax.fori_loop(0, CTX // 8, early, (zero, zero))
    reach = jnp.exp(-rate[...] * (block - CTX + 1.0))
    whole = jnp.exp(-rate[...] * block)
    pay = scr["pay"]
    for m in range(2):
        pay[m * NS : (m + 1) * NS] = (reach * got[m] + whole * endg[m]).astype(BF)
    pay[2 * NS : 3 * NS] = flag_rows(keep)

    def spread(k):
        return remote(
            pay,
            gath.at[k],
            scr["send_g"].at[k],
            scr["recv_g"].at[k],
            seq=lax.rem(s + n - k, n),
        )

    for k in range(1, n):

        @pl.when(s >= k)
        def _():
            spread(k).start()

    ring1.go(7)
    for m in range(2):
        mixed_o[m] = (h1[m] + mlp_sums[m].end()).astype(BF)
    @pl.when(s < n - 1)
    def _():
        for i in range(4):
            to_before(0, i, dkp.at[i], rk.at[i]).wait_recv()
            to_before(1, i, dvp.at[i], rv.at[i]).wait_recv()

    dk_b, dv_b = scr["dkb"], scr["dvb"]
    for m in range(2):
        for head in range(chan // HD):
            lanes = slice(head * HD, (head + 1) * HD)
            i = m * (chan // HD) + head
            dk_b[m, :, lanes] = (dko[m, :, lanes] + rk[i].astype(F32)).astype(BF)
            dv_b[m, :, lanes] = (dvo[m, :, lanes] + rv[i].astype(F32)).astype(BF)

    need("ctx")
    ctx = h["ctx"]

    def kv_grads(i, c):
        at = pl.multiple_of(i * tile, tile)
        here = pl.ds(at, tile)
        left = nf[:, :, here].reshape(2 * block, tile).T
        left_ctx = ctx[:, :, here].reshape(2 * CTX, tile).T
        for j, (own, far) in enumerate(((dk_b, dkc), (dv_b, dvc))):
            value = dot(left, own[...].reshape(2 * block, chan)) + dot(
                left_ctx, far[...].reshape(2 * CTX, chan)
            )
            x2[pl.ds((j + 1) * width + at, tile), :] = value.astype(BF)
        return c

    lax.fori_loop(0, width // tile, kv_grads, 0)
    ring2.start()
    ring1.go(8)
    for k in range(1, n):

        @pl.when(s + k < n)
        def _():
            spread(k).wait_recv()

    def chain(i, carry):
        k = n - 1 - i
        got = gath[k].astype(F32)
        valid = s + k < n
        return tuple(
            jnp.where(
                valid,
                got[2 * NS + m : 2 * NS + m + 1]
                * (got[m * NS : (m + 1) * NS] + whole * carry[m]),
                carry[m],
            )
            for m in range(2)
        )

    carry = lax.fori_loop(0, n - 1, chain, (zero, zero))
    grads0 = tuple(endg[m] + carry[m] for m in range(2))

    def back_late(i, val):
        hold, d_drive, d_decay, d_out = list(val[0:2]), val[2], val[3], val[4]
        low_row = pl.multiple_of(CTX - 8 - i * 8, 8)
        base = pl.multiple_of(block - 8 - i * 8, 8)
        for k in range(7, -1, -1):
            for m in range(2):
                dy = dy_s[m, pl.ds(low_row + k, 1), :]
                grad = hold[m] + out_c * dy
                du_s[m, pl.ds(base + k, 1), :] = jnp.sum(drive * grad, axis=0, keepdims=True)
                d_drive = d_drive + grad * u_s[m, pl.ds(base + k, 1), :]
                d_decay = d_decay + grad * hist[base + k, m].astype(F32)
                d_out = d_out + dy * hist[base + k + 1, m].astype(F32)
                hold[m] = decay * grad
        return hold[0], hold[1], d_drive, d_decay, d_out

    val = lax.fori_loop(0, CTX // 8, back_late, (grads0[0], grads0[1], zero, zero, zero))

    def back_early(i, val):
        hold, d_drive, d_decay = list(val[0:2]), val[2], val[3]
        base = pl.multiple_of(block - CTX - 8 - i * 8, 8)
        for k in range(7, -1, -1):
            for m in range(2):
                grad = hold[m]
                du_s[m, pl.ds(base + k, 1), :] = jnp.sum(drive * grad, axis=0, keepdims=True)
                d_drive = d_drive + grad * u_s[m, pl.ds(base + k, 1), :]
                d_decay = d_decay + grad * hist[base + k, m].astype(F32)
                hold[m] = decay * grad
        return hold[0], hold[1], d_drive, d_decay

    _, _, d_drive, d_decay = lax.fori_loop(0, (block - CTX) // 8, back_early, val[0:4])
    x3[0:NS] = (-decay * (d_decay - d_drive * h["cin"][...] * decay / root)).astype(BF)
    x3[NS : 2 * NS] = (d_drive * root).astype(BF)
    x3[2 * NS : 3 * NS] = val[4].astype(BF)
    ring3.start()
    ring1.go(9)
    ring2.go(1)
    part_s = scr["part"]

    def normed_part(i, c):
        m, part = i // 2, lax.rem(i, 2)
        here = pl.ds(pl.multiple_of(part * half, half), half)
        part_s[...] = (
            dot(dq_s[m, here, :], wq[...], NT)
            + dot(dk_b[m, here, :], wk[...], NT)
            + dot(dv_b[m, here, :], wv[...], NT)
        )
        part_s[:, cols] += du_s[m, here, :]
        mlp[m, here, :] = part_s[...].astype(BF)
        return c

    finals = [scatter(mlp, 0, m) for m in range(2)]
    for m in range(2):
        lax.fori_loop(2 * m, 2 * m + 2, normed_part, 0)
        finals[m].start()
    for c in finals:
        c.turn()
    ring1.go(10)
    ring2.go(2)
    ring3.go(1)
    need("tok", "gain")
    gain_grad = jnp.zeros((1, width), F32)
    for m in range(2):
        back, one = rms_back(tok[m].astype(F32), h["gain"][...], finals[m].end())
        tg_o[m] = dh1[m] + back
        gain_grad = gain_grad + one
    gp, gr, gs, gg = scr["gp"], scr["gr"], scr["gs"], scr["gg"]
    for j in range(4):
        gp[j, 0:1] = gain_grad[:, j * chan : (j + 1) * chan]
        gp[j, 1:2] = mid_grad[:, j * chan : (j + 1) * chan]
        gp[j, 2:8] = jnp.zeros((6, chan), F32)
    gains = [to_peer(i, gp.at[peers[i]], gr.at[i], 1) for i in range(3)]
    for c in gains:
        c.start()
    ring1.go(11)
    ring2.go(3)
    ring3.go(2)
    total = gp[me]
    for i in range(3):
        gains[i].wait_recv()
        total = total + gr[i]
    gs[...] = total

    def gain_out(k):
        return remote(
            gs,
            gg.at[k],
            scr["gain_s"].at[k],
            scr["gain_r"].at[k],
            seq=lax.rem(s + k, n),
        )

    for k in range(1, n):
        gain_out(k).start()
    for t in range(12, 15):
        ring1.go(t)
        ring2.go(t - 8)
        ring3.go(t - 9)
    store1 = pltpu.make_async_copy(x1, sum1_o, scr["store"].at[0])
    store1.start()
    for t in range(7, 15):
        ring2.go(t)
        ring3.go(min(t - 1 + (t - 7) // 3, 14))
    store2 = pltpu.make_async_copy(x2, sum2_o, scr["store"].at[1])
    store2.start()
    ring3.go(14)
    for i, small_o in enumerate((rate_o, cin_o, cout_o)):
        small_o[...] = x3[i * NS : (i + 1) * NS].astype(F32)
    for k in range(1, n):
        gain_out(k).wait_recv()
        total = total + gg[k]
    norm_o[...] = total[0:1]
    mid_o[...] = total[1:2]
    for k in range(1, n):
        gain_out(k).wait_send()
    for c in gains + ctx_out:
        c.wait_send()
    for g in gathers:
        g.finish()

    @pl.when(s > 0)
    def _():
        ctx_back.wait_send()
        for i in range(4):
            to_before(0, i, dkp.at[i], rk.at[i]).wait_send()
            to_before(1, i, dvp.at[i], rv.at[i]).wait_send()

    for k in range(1, n):

        @pl.when(s >= k)
        def _():
            spread(k).wait_send()

    ring1.drain()
    ring2.drain()
    ring3.drain()
    store1.wait()
    store2.wait()


def ring_rows(n, used, subs):
    return -(-used // (2 * n * subs * 16)) * 16


def last(*args):
    n = lax.axis_size("seq")
    by = dict(zip(LAST_IN, args))
    micro, block, width = by["nf"].shape
    rows = block // 4
    chan = by["rate"].shape[1]
    keys = by["k"].shape[1]
    sds = jax.ShapeDtypeStruct
    dma = pltpu.SemaphoreType.DMA
    step1 = ring_rows(n, by["ffn"].shape[0], 2)
    step2 = ring_rows(n, 4 * width, 2)
    step3 = ring_rows(n, 3 * NS, 1)
    x1 = VM((4 * n * step1, chan), BF)
    x2 = VM((4 * n * step2, chan), BF)
    scratch = dict(
        x1=x1,
        r1=VM((2, n - 1, 2, step1, chan), BF),
        x2=x2,
        r2=VM((2, n - 1, 2, step2, chan), BF),
        x3=VM((2 * n * step3, chan), BF),
        r3=VM((2, n - 1, 1, step3, chan), BF),
        s1s=dma((2, 2, 2 * n - 2)),
        s1r=dma((2, 2, 2 * n - 2)),
        s2s=dma((2, 2, 2 * n - 2)),
        s2r=dma((2, 2, 2 * n - 2)),
        s3s=dma((2, 1, 2 * n - 2)),
        s3r=dma((2, 1, 2 * n - 2)),
        fetch=dma((len(LAST_IN),)),
        rr=VM((micro, block, width), BF),
        da=VM((micro, block, chan), BF),
        rs=dma((2, 3)),
        rrv=dma((2, 3)),
        rk=VM((4, block, HD), BF),
        rv=VM((4, block, HD), BF),
        dkp=VM((4, block, HD), BF),
        dvp=VM((4, block, HD), BF),
        ak=VM((keys, HD), F32),
        av=VM((keys, HD), F32),
        dq=VM((micro, block, chan), BF),
        dko=VM((micro, block, chan), F32),
        dvo=VM((micro, block, chan), F32),
        dkb=VM((micro, block, chan), BF),
        dvb=VM((micro, block, chan), BF),
        dkc=VM((micro, CTX, chan), BF),
        dvc=VM((micro, CTX, chan), BF),
        cp=VM((4, micro, CTX, chan), BF),
        cr=VM((3, micro, CTX, chan), BF),
        dcs=VM((micro, CTX, chan), BF),
        dcr=VM((micro, CTX, chan), BF),
        dy=VM((micro, CTX, chan), F32),
        u=VM((micro, block, chan), F32),
        du=VM((micro, block, chan), F32),
        hist=VM((block + 1, micro, NS, chan), BF),
        pay=VM((3 * NS, chan), BF),
        gath=VM((n, 3 * NS, chan), BF),
        part=VM((block // 2, width), F32),
        dh1=VM((micro, rows, width), F32),
        over=VM((4, rows, width), BF),
        into=VM((4, 3, rows, width), BF),
        ss=dma((4, 3)),
        sr=dma((4, 3)),
        gp=VM((4, 8, chan), F32),
        gr=VM((3, 8, chan), F32),
        gs=VM((8, chan), F32),
        gg=VM((n, 8, chan), F32),
        gain_s=dma((n,)),
        gain_r=dma((n,)),
        send_k=dma((2, 5)),
        recv_k=dma((2, 5)),
        send_c=dma((2, 3)),
        recv_c=dma((2, 3)),
        send_g=dma((n,)),
        recv_g=dma((n,)),
        store=dma((2,)),
    )
    outs = (
        sds((micro, rows, width), BF),
        sds((micro, rows, width), F32),
        sds(x1.shape, BF),
        sds(x2.shape, BF),
        sds((NS, chan), F32),
        sds((NS, chan), F32),
        sds((NS, chan), F32),
        sds((1, chan), F32),
        sds((1, chan), F32),
    )
    return launch(
        functools.partial(last_kernel, n),
        LAST_IN,
        args,
        outs,
        [True, True, False, False, True, True, True, True, True],
        scratch,
        2,
        62,
        "last",
        ("ffn",),
    )


def finish_kernel(*refs):
    half = len(refs) // 2
    for src, dst in zip(refs[:half], refs[half:]):
        dst[...] = src[...].astype(dst.dtype)


def finish(sum1, sum2, mixed, tokens_grad, end, small, width, units, chan):
    steps = width // chan
    sds = jax.ShapeDtypeStruct
    down_at = units * width // chan
    micro, rows, _ = mixed.shape

    def panel(rows_of, at):
        return (
            pl.BlockSpec((rows_of, chan), lambda j: (at // rows_of + j, 0)),
            pl.BlockSpec((rows_of, chan), lambda j: (0, j)),
        )

    def column(at):
        high = width // steps
        return (
            pl.BlockSpec((high, chan), lambda j: (at // high + j, 0)),
            pl.BlockSpec((high, chan), lambda j: (j, 0)),
        )

    same = pl.BlockSpec((micro, rows // steps, width), lambda j: (0, j, 0))
    whole = pl.BlockSpec(end.shape, lambda j: (0, 0, 0))
    specs = [
        panel(width, 0),
        panel(units, down_at),
        panel(chan, 3 * width),
        column(0),
        column(width),
        column(2 * width),
        (same, same),
        (same, same),
        (whole, whole),
    ] + [
        (pl.BlockSpec(a.shape, lambda j: (0, 0)), pl.BlockSpec(a.shape, lambda j: (0, 0)))
        for a in small
    ]
    return pl.pallas_call(
        finish_kernel,
        grid=(steps,),
        out_shape=(
            sds((width, units), F32),
            sds((units, width), F32),
            sds((chan, width), F32),
            sds((width, chan), F32),
            sds((width, chan), F32),
            sds((width, chan), F32),
            sds(mixed.shape, BF),
            sds(tokens_grad.shape, F32),
            sds(end.shape, F32),
            *(sds(a.shape, F32) for a in small),
        ),
        in_specs=[a for a, _ in specs],
        out_specs=tuple(b for _, b in specs),
        compiler_params=pltpu.CompilerParams(vmem_limit_bytes=62 << 20),
        name="finish",
    )(sum1, sum1, sum2, sum2, sum2, sum2, mixed, tokens_grad, end, *small)


def body(
    tokens,
    out_grad,
    norm_gain,
    w_query,
    w_key,
    w_value,
    w_out,
    mid_gain,
    w_up,
    w_down,
    ssm_rate,
    ssm_in,
    ssm_out,
    resets,
    init_state,
    states_grad,
):
    micro, rows, width = tokens.shape
    chan = ssm_rate.shape[0]
    units = w_up.shape[1]
    rate, cin, cout = ssm_rate.T, ssm_in.T, ssm_out.T
    flag = jnp.broadcast_to(resets, (micro, chan))
    init = jnp.swapaxes(init_state, 1, 2)
    endg = jnp.swapaxes(states_grad[:, 0], 1, 2)
    gain_row, mid_row = norm_gain[None], mid_gain[None]
    nf, q, k, v, ctx, keep, start, end, mlp, h1, dm, ffn, att, lse = forward(
        *(tokens, gain_row, w_key, w_value, w_query, rate, cin, cout, flag, init, out_grad),
        *(w_out, mid_row, w_up, w_down),
    )
    mixed, tokens_grad, sum1, sum2, *small = last(
        *(dm, ffn, nf, rate, cin, cout, start, endg, h1, out_grad, mid_row, w_out),
        *(keep, q, k, v, lse, att, ctx, w_query, w_key, w_value, mlp, tokens, gain_row),
    )
    done = finish(sum1, sum2, mixed, tokens_grad, end, small, width, units, chan)
    up_g, down_g, proj_g, query_g, key_g, value_g, mixed, tokens_grad, end = done[:9]
    rate_g, in_g, out_g, norm_g, mid_g = done[9:]
    return (
        mixed,
        jnp.swapaxes(end, 1, 2)[:, None],
        tokens_grad,
        norm_g[0],
        query_g,
        key_g,
        value_g,
        proj_g,
        mid_g[0],
        up_g,
        down_g,
        rate_g.T,
        in_g.T,
        out_g.T,
    )


def solution(mesh):
    return jax.shard_map(
        body,
        mesh=mesh,
        in_specs=(
            P(None, ("seq", "tp"), None),
            P(None, ("seq", "tp"), None),
            P(),
            P(None, "tp"),
            P(None, "tp"),
            P(None, "tp"),
            P("tp", None),
            P(),
            P(None, "tp"),
            P("tp", None),
            P("tp", None),
            P("tp", None),
            P("tp", None),
            P(None, "seq"),
            P(None, "tp", None),
            P(None, "seq", "tp", None),
        ),
        out_specs=(
            P(None, ("seq", "tp"), None),
            P(None, "seq", "tp", None),
            P(None, ("seq", "tp"), None),
            P("tp"),
            P(None, "tp"),
            P(None, "tp"),
            P(None, "tp"),
            P("tp", None),
            P("tp"),
            P(None, "tp"),
            P("tp", None),
            P("tp", None),
            P("tp", None),
            P("tp", None),
        ),
        check_vma=False,
    )
```
